32 devices in a mesh: beam: 16 (over z, x, core), head: 2 (over y).
Axes of the slice: x: 2, y: 2, z: 4, core: 2. Of those that a mesh axis runs over, the one named last changes fastest.
Arguments:
- queries: bfloat16 [64, 8192], P('beam', 'head')
- new_keys: bfloat16 [64, 1024], P('beam', 'head')
- new_values: bfloat16 [64, 1024], P('beam', 'head'), may hold values from -6 to 6
- prompt_keys: bfloat16 [4, 4096, 1024], P(None, 'beam', 'head')
- prompt_values: bfloat16 [4, 4096, 1024], P(None, 'beam', 'head'), may hold values from -6 to 6
- private_keys: bfloat16 [64, 512, 1024], P('beam', None, 'head'), may hold values from -16 to 16
- private_values: bfloat16 [64, 512, 1024], P('beam', None, 'head'), may hold values from -6 to 6
- parents: int32 [64], P('beam'), may hold values from 0 to 63, as said below
- block_counts: int32 [64], P('beam'), may hold values from 1 to 4
- out_weight: bfloat16 [8192, 8192], P('head', 'beam'), may hold values from -0.0625 to 0.0625
Outputs:
- mixed: bfloat16 [64, 8192], P('head', 'beam')
The draws below stay inside these ranges and needn't reach their ends.
Inputs may be any that keep to these rules, and one draw needn't show every extreme that they name: Every beam's parent belongs to the same request: parents[b] // 16 == b // 16.
All inputs are finite; a program needn't handle non-finite values.
Results may differ from the reference program's by a relative error of at most 0.0049.
Values may be sent and summed in bfloat16 or wider, within the bound.
No kernel may reach another device: no remote copies, remote signals or barrier semaphores. Data moves between devices by JAX's collectives and lax.ppermute only.
A program may use at most 128 MiB of HBM per device.

```python
import math
import jax
import jax.numpy as jnp
from jax import lax

D = 8192
HQ = 64
KVH = 8
HD = 128
QPK = 8
BEAM_WIDTH = 16
BEAMS = 64
REQUESTS = 4
PROMPT = 4096
BLOCK_LEN = 128
BLOCKS = 4
PRIV = 512


def base_queries(key):
    return jax.random.normal(key, (BEAMS, HQ * HD), jnp.float32)


def base_prompt(key):
    return 2.5 * jax.random.normal(jax.random.fold_in(key, 101), (REQUESTS, PROMPT, KVH * HD), jnp.float32)


def draw_queries(key, part):
    base = base_queries(key)
    return base.astype(jnp.bfloat16)


def draw_new_keys(key, part):
    base = base_queries(key)
    key = jax.random.fold_in(key, 3)
    grouped = jnp.mean(base.reshape(BEAMS, KVH, QPK, HD), axis=2).reshape(BEAMS, KVH * HD)
    noise = jax.random.normal(key, (BEAMS, KVH * HD), jnp.float32)
    factor = QPK / math.sqrt(HD) * (2.0 + math.log(PROMPT))
    return (factor * grouped + noise).astype(jnp.bfloat16)


def draw_prompt_keys(key, part):
    prompt = base_prompt(key)
    return prompt.astype(jnp.bfloat16)


def draw_private_keys(key, part):
    key = jax.random.fold_in(key, 6)
    spread = math.sqrt(2.0 * (2.8 + math.log(PROMPT / PRIV)))
    values = spread * jax.random.normal(key, (BEAMS, PRIV, KVH * HD), jnp.float32)
    return jnp.clip(values, -16.0, 16.0).astype(jnp.bfloat16)


def draw_parents(key, part):
    key = jax.random.fold_in(key, 4)
    offsets = jax.random.randint(key, (BEAMS,), 0, BEAM_WIDTH)
    chosen = jnp.arange(BEAMS) // BEAM_WIDTH * BEAM_WIDTH + offsets
    chosen = chosen.at[0].set(0).at[BEAMS - 1].set(BEAMS - 1)
    return chosen.astype(jnp.int32)


def draw_block_counts(key, part):
    key = jax.random.fold_in(key, 5)
    counts = jax.random.randint(key, (BEAMS,), 1, BLOCKS + 1)
    counts = counts.at[0].set(BLOCKS).at[1].set(1)
    return counts.astype(jnp.int32)


def shard_levels(own_key, extent, pieces, low, largest):
    loudness, own = 1.0, jax.random.fold_in(own_key, 6)
    for axis_at, shards_of in pieces:
        draws = jnp.exp(jax.random.uniform(jax.random.fold_in(own, axis_at), (shards_of,), jnp.float32, low / len(pieces), largest / len(pieces)))
        loudness = loudness * jnp.repeat(draws, extent[axis_at] // shards_of).reshape([-1 if axis == axis_at else 1 for axis in range(len(extent))])
    return loudness


def centred(rng, extent, scale, bound, pieces=(), kind=jnp.bfloat16):
    values = scale * jax.random.normal(rng, extent, jnp.float32)
    if pieces:
        values = values * shard_levels(rng, extent, pieces, -0.22, 0.18)
    return jnp.clip(values, -bound, bound).astype(kind)


def setup_inputs(seed: int = 0) -> dict:
    arg_keys = jax.random.split(jax.random.key(seed), 11)
    queries = draw_queries(jax.random.fold_in(arg_keys[10], 71), 0)
    new_keys = draw_new_keys(jax.random.fold_in(arg_keys[10], 71), 0)
    new_values = centred(arg_keys[2], (BEAMS, KVH * HD), 1.0, 6.0, ((0, 16), (1, 2)))
    prompt_keys = draw_prompt_keys(jax.random.fold_in(arg_keys[10], 71), 0)
    prompt_values = centred(arg_keys[4], (REQUESTS, PROMPT, KVH * HD), 1.0, 6.0, ((1, 16), (2, 2)))
    private_keys = draw_private_keys(jax.random.fold_in(arg_keys[10], 71), 0)
    private_values = centred(arg_keys[6], (BEAMS, PRIV, KVH * HD), 1.0, 6.0, ((0, 16), (2, 2)))
    parents = draw_parents(jax.random.fold_in(arg_keys[10], 71), 0)
    block_counts = draw_block_counts(jax.random.fold_in(arg_keys[10], 71), 0)
    out_weight = centred(arg_keys[9], (HQ * HD, D), (HQ * HD) ** -0.5, 0.0625, ((0, 2), (1, 16)))
    return dict(queries=queries, new_keys=new_keys, new_values=new_values, prompt_keys=prompt_keys, prompt_values=prompt_values, private_keys=private_keys, private_values=private_values, parents=parents, block_counts=block_counts, out_weight=out_weight)


masked_score = -1e+30

def reference(queries, new_keys, new_values, prompt_keys, prompt_values, private_keys, private_values, parents, block_counts, out_weight):
    logit_scale = 1.0 / math.sqrt(HD)

    def one_request(request):
        first_beam = (request * BEAM_WIDTH).astype(jnp.int32)
        query_head_count = lax.dynamic_slice_in_dim(queries, first_beam, BEAM_WIDTH, 0).astype(jnp.float32).reshape(BEAM_WIDTH, KVH, QPK, HD)
        beam_self_keys = lax.dynamic_slice_in_dim(new_keys, first_beam, BEAM_WIDTH, 0).astype(jnp.float32).reshape(BEAM_WIDTH, KVH, HD)
        own_values = lax.dynamic_slice_in_dim(new_values, first_beam, BEAM_WIDTH, 0).astype(jnp.float32).reshape(BEAM_WIDTH, KVH, 1, HD)
        prompt_heads = lax.dynamic_index_in_dim(prompt_keys, request, 0, keepdims=False).astype(jnp.float32).reshape(PROMPT, KVH, HD)
        prompt_vals = lax.dynamic_index_in_dim(prompt_values, request, 0, keepdims=False).astype(jnp.float32).reshape(PROMPT, KVH, HD)
        parent_rows = lax.dynamic_slice_in_dim(parents, first_beam, BEAM_WIDTH, 0).astype(jnp.int32)
        cache_keys = jnp.take(private_keys, parent_rows, axis=0).astype(jnp.float32).reshape(BEAM_WIDTH, PRIV, KVH, HD)
        cache_vals = jnp.take(private_values, parent_rows, axis=0).astype(jnp.float32).reshape(BEAM_WIDTH, PRIV, KVH, HD)
        counts = jnp.take(block_counts, parent_rows).astype(jnp.int32)
        prompt_scores = jnp.einsum('bkqd,tkd->bkqt', query_head_count, prompt_heads) * logit_scale
        prompt_max = lax.optimization_barrier(jnp.max(prompt_scores, axis=-1))
        prompt_weights = jnp.exp(prompt_scores - prompt_max[..., None])
        prompt_denominator = lax.optimization_barrier(jnp.sum(prompt_weights, axis=-1))
        rounded = lax.optimization_barrier(prompt_weights.astype(jnp.bfloat16))
        prompt_num = jnp.einsum('bkqt,tkd->bkqd', rounded.astype(jnp.float32), prompt_vals)
        cache_scores = jnp.einsum('bkqd,bpkd->bkqp', query_head_count, cache_keys) * logit_scale
        allowed = jnp.arange(PRIV, dtype=jnp.int32)[None, :] < (counts * BLOCK_LEN)[:, None]
        cache_scores = jnp.where(allowed[:, None, None, :], cache_scores, masked_score)
        private_max = lax.optimization_barrier(jnp.max(cache_scores, axis=-1))
        private_weights = jnp.exp(cache_scores - private_max[..., None])
        private_den = lax.optimization_barrier(jnp.sum(private_weights, axis=-1))
        rounded_private = lax.optimization_barrier(private_weights.astype(jnp.bfloat16))
        private_num = jnp.einsum('bkqp,bpkd->bkqd', rounded_private.astype(jnp.float32), cache_vals)
        beam_self_logit = jnp.einsum('sxjr,sxr->sxj', query_head_count, beam_self_keys) * logit_scale
        overall = jnp.maximum(jnp.maximum(prompt_max, private_max), beam_self_logit)
        first = jnp.exp(prompt_max - overall)
        second = jnp.exp(private_max - overall)
        third = jnp.exp(beam_self_logit - overall)
        numer = first[..., None] * prompt_num + second[..., None] * private_num + third[..., None] * own_values
        denom = first * prompt_denominator + second * private_den + third
        return (numer / denom[..., None]).astype(jnp.bfloat16).reshape(BEAM_WIDTH, KVH * QPK * HD)
    attended = lax.map(one_request, jnp.arange(REQUESTS, dtype=jnp.int32)).reshape(BEAMS, HQ * HD)
    return jnp.dot(attended, out_weight, preferred_element_type=jnp.float32).astype(jnp.bfloat16)
```

```python
import functools
import math

import jax
import jax.numpy as jnp
from jax import lax
from jax.experimental import pallas as pl
from jax.experimental.pallas import tpu as pltpu
from jax.sharding import PartitionSpec as P

HD = 128
QPK = 8
BEAM_WIDTH = 16
BLOCK_LEN = 128
STATS = 128
SCALE = 1.0 / math.sqrt(HD)
LOG2E = math.log2(math.e)

masked_score = -1e30
f32, bf16 = jnp.float32, jnp.bfloat16


def dot(a, b, ca, cb):
    return lax.dot_general(a, b, (((ca,), (cb,)), ((), ())), preferred_element_type=f32)


def soft(scores):
    top = jnp.max(scores, axis=1, keepdims=True)
    weights = jnp.exp2((scores - top) * (SCALE * LOG2E))
    return weights, top * SCALE, jnp.sum(weights, axis=1, keepdims=True)


def prep_kernel(q_hbm, nk_hbm, par_hbm, q_ref, own_ref, tail_ref, nk_ref, par_ref, sems):
    copies = [
        pltpu.make_async_copy(src, dst, sems.at[n])
        for n, (src, dst) in enumerate(((q_hbm, q_ref), (nk_hbm, nk_ref), (par_hbm, par_ref)))
    ]
    for x in copies:
        x.start()
    for x in copies:
        x.wait()
    beams = q_ref.shape[0]
    row = lax.broadcasted_iota(jnp.int32, (beams, STATS), 0)
    parent = jnp.zeros(row.shape, jnp.int32)
    for b in range(beams):
        parent = jnp.where(row == b, par_ref[b], parent)
    tail_ref[...] = parent.astype(f32).astype(bf16)
    lane = lax.broadcasted_iota(jnp.int32, (beams, STATS), 1)
    own = jnp.zeros((beams, STATS), f32)
    for h in range(q_ref.shape[1] // HD):
        k = h // QPK
        key = nk_ref[:, k * HD : (k + 1) * HD].astype(f32)
        s = jnp.sum(q_ref[:, h * HD : (h + 1) * HD].astype(f32) * key, axis=1, keepdims=True)
        own = jnp.where(lane == h, s * SCALE, own)
    own_ref[...] = own


def line_kernel(tail_ref, *refs):
    *pieces, out_ref = refs
    width = pieces[0].shape[1]
    out_ref[:, :width] = jnp.concatenate([x[...] for x in pieces], axis=0)
    out_ref[:, width:] = jnp.concatenate([tail_ref[...]] * len(pieces), axis=0)


def load_kernel(
    cnt_hbm, pk_hbm, pv_hbm, ck_hbm, cv_hbm,
    pk_ref, pv_ref, ck_ref, cv_ref, lim_ref, cnt_ref, cnt_sem, prompt_sems, old_sems,
):
    heads, pairs, _, _ = pk_ref.shape
    olds = ck_hbm.shape[0]
    requests = 2 * pairs
    mine = lax.axis_index("beam") // (BEAM_WIDTH // olds)
    copies = [pltpu.make_async_copy(cnt_hbm, cnt_ref, cnt_sem.at[0])]
    for k in range(heads):
        cols = pl.ds(k * HD, HD)
        for n, (src, dst) in enumerate(((pk_hbm, pk_ref), (pv_hbm, pv_ref))):
            for t in range(requests):
                copies.append(
                    pltpu.make_async_copy(
                        src.at[lax.rem(mine - t + requests, requests), :, cols],
                        dst.at[k, t // 2, :, pl.ds(t % 2 * HD, HD)],
                        prompt_sems.at[n, k, t],
                    )
                )
        for n, (src, dst) in enumerate(((ck_hbm, ck_ref), (cv_hbm, cv_ref))):
            for o in range(olds):
                copies.append(
                    pltpu.make_async_copy(
                        src.at[o, :, cols], dst.at[k, :, pl.ds(o * HD, HD)], old_sems.at[n, k, o]
                    )
                )
    for x in copies:
        x.start()
    for x in copies:
        x.wait()
    lane = lax.broadcasted_iota(jnp.int32, lim_ref.shape, 1)
    limit = jnp.zeros(lim_ref.shape, jnp.int32)
    for o in range(olds):
        limit = jnp.where(lane == o, cnt_ref[o] * BLOCK_LEN, limit)
    lim_ref[...] = limit


def attend_kernel(
    q_ref, pk_ref, pv_ref, ck_ref, cv_ref, lim_ref, out_ref, s_ref, p_ref, cs_ref, cp_ref
):
    count = q_ref.shape[0]
    pieces = [q_ref.at[r] for r in range(count)]
    outs = [out_ref.at[r] for r in range(count)]
    heads, pairs, length, _ = pk_ref.shape
    requests = 2 * pairs
    _, span, olds = ck_ref.shape
    olds = olds // HD
    total = q_ref.shape[2]
    beams = q_ref.shape[1] // requests
    block = count * beams
    stride = heads * QPK
    rows = QPK * block
    me = lax.axis_index("beam")

    parent = jnp.concatenate([x[:, total - STATS :].astype(f32)[:beams] for x in pieces], axis=0)
    parent = jnp.concatenate([parent] * QPK, axis=0).astype(jnp.int32) - me * olds
    column = parent[:, :1]
    local = (column >= 0) & (column < olds)
    limit = jnp.zeros((rows, 1), jnp.int32)
    for o in range(olds):
        limit = jnp.where(column == o, lim_ref[0:1, o : o + 1], limit)
    stats = [jnp.zeros((block, STATS), f32) for _ in range(requests)]
    lane = lax.broadcasted_iota(jnp.int32, (block, STATS), 1) % stride
    blank = jnp.zeros((rows, HD), bf16)
    kept = {}

    def scores(k):
        slot = k % 2
        tiles = [
            x[:, (k * QPK + i) * HD : (k * QPK + i + 1) * HD] for i in range(QPK) for x in pieces
        ]
        q = [
            jnp.concatenate([x[t * beams : (t + 1) * beams] for x in tiles], axis=0)
            for t in range(requests)
        ]
        for u in range(pairs):
            both = jnp.concatenate(
                [
                    jnp.concatenate([q[2 * u], blank], axis=1),
                    jnp.concatenate([blank, q[2 * u + 1]], axis=1),
                ],
                axis=0,
            )
            s_ref[slot, 2 * u * rows : 2 * (u + 1) * rows] = dot(both, pk_ref[k, u], 1, 1)
        chosen = jnp.concatenate([jnp.where(parent == o, q[0], blank) for o in range(olds)], axis=1)
        cs_ref[slot] = dot(chosen, ck_ref[k], 1, 1)

    def weigh(k):
        slot = k % 2
        p, top, den = soft(s_ref[slot])
        p_ref[slot] = p.astype(bf16)
        place = lax.broadcasted_iota(jnp.int32, (rows, span), 1)
        c, ctop, cden = soft(jnp.where(place < limit, cs_ref[slot], masked_score))
        cp_ref[slot] = c.astype(bf16)
        kept[k] = (top, den, ctop, cden)

    def values(k):
        slot = k % 2
        tops, dens, ctop, cden = kept.pop(k)
        nums = []
        for u in range(pairs):
            both = dot(p_ref[slot, 2 * u * rows : 2 * (u + 1) * rows], pv_ref[k, u], 1, 0)
            nums += [both[:rows, :HD], both[rows:, HD:]]
        every = dot(cp_ref[slot], cv_ref[k], 1, 0)
        cnum = every[:, :HD]
        for o in range(1, olds):
            cnum = jnp.where(parent == o, every[:, o * HD : (o + 1) * HD], cnum)
        done = []
        for t in range(requests):
            part = slice(t * rows, (t + 1) * rows)
            num, top, den = nums[t], tops[part], dens[part]
            if t == 0:
                both = jnp.where(local, jnp.maximum(top, ctop), top)
                a = jnp.exp(top - both)
                e = jnp.where(local, jnp.exp(jnp.where(local, ctop, both) - both), 0.0)
                num = a * num + e * cnum
                den = a * den + e * cden
                top = both
            done.append(num * (1.0 / den))
            lse = top + jnp.log(den)
            for i in range(QPK):
                stats[t] = jnp.where(
                    lane == k * QPK + i,
                    jnp.broadcast_to(
                        lse[i * block : (i + 1) * block], (block, STATS)
                    ),
                    stats[t],
                )
        for i in range(QPK):
            cols = slice((k * QPK + i) * HD, (k * QPK + i + 1) * HD)
            for r, out in enumerate(outs):
                first = i * block + r * beams
                out[:, cols] = jnp.concatenate(
                    [x[first : first + beams] for x in done], axis=0
                ).astype(bf16)

    for step in range(heads + 2):
        if step < heads:
            scores(step)
        if 0 <= step - 1 < heads:
            weigh(step - 1)
        if 0 <= step - 2:
            values(step - 2)
    for r, out in enumerate(outs):
        out[:, total - STATS :] = pack_stats(
            jnp.concatenate([x[r * beams : (r + 1) * beams] for x in stats], axis=0), stride
        )


def pack_stats(x, stride):
    hi = x.astype(bf16).astype(f32)
    mid = (x - hi).astype(bf16).astype(f32)
    which = lax.broadcasted_iota(jnp.int32, x.shape, 1) // stride
    return jnp.where(which == 0, hi, jnp.where(which == 1, mid, x - hi - mid)).astype(bf16)


def read_stats(x, stride):
    x = x.astype(f32)
    return x + pltpu.roll(x, STATS - stride, 1) + pltpu.roll(x, STATS - 2 * stride, 1)


def merge(a, b, out):
    total = a.shape[-1]
    count = (total - STATS) // HD
    la, lb = read_stats(a[:, total - STATS :], count), read_stats(b[:, total - STATS :], count)
    top = jnp.maximum(la, lb)
    wa, wb = jnp.exp(la - top), jnp.exp(lb - top)
    den = wa + wb
    wa = wa * (1.0 / den)
    wb = wb * (1.0 / den)
    for h in range(count):
        cols = slice(h * HD, (h + 1) * HD)
        out[:, cols] = (
            wa[:, h : h + 1] * a[:, cols].astype(f32) + wb[:, h : h + 1] * b[:, cols].astype(f32)
        ).astype(bf16)
    lse = top + jnp.log(den)
    lane = lax.broadcasted_iota(jnp.int32, lse.shape, 1)
    again = jnp.where(
        lane < count,
        lse,
        jnp.where(lane < 2 * count, pltpu.roll(lse, count, 1), pltpu.roll(lse, 2 * count, 1)),
    )
    out[:, total - STATS :] = pack_stats(again, count)


def core_kernel(kept0, kept2, came_ref, keep_ref, send_ref):
    merge(kept0.at[0], came_ref.at[0], keep_ref)
    merge(kept2.at[0], came_ref.at[1], send_ref)


def plane_kernel(kept_ref, came_ref, *refs):
    *outs, whole_ref = refs
    merge(kept_ref, came_ref, whole_ref)
    beams = outs[0].shape[0]
    for t, out in enumerate(outs):
        out[...] = whole_ref[t * beams : (t + 1) * beams]


def finish_kernel(own_ref, nv_ref, *refs):
    *parts, out_ref = refs
    beams, total = parts[0].shape
    heads = nv_ref.shape[1] // HD
    stride = heads * QPK
    own = own_ref[...]
    lses = [read_stats(x[:, total - STATS :], stride) for x in parts]
    top = functools.reduce(jnp.maximum, lses, own)
    ws = [jnp.exp(x - top) for x in lses]
    w_own = jnp.exp(own - top)
    inv = 1.0 / functools.reduce(jnp.add, ws, w_own)
    ws = [w * inv for w in ws]
    w_own = w_own * inv
    for k in range(heads):
        value = nv_ref[:, k * HD : (k + 1) * HD].astype(f32)
        for i in range(QPK):
            h = k * QPK + i
            acc = w_own[:, h : h + 1] * value
            for w, x in zip(ws, parts):
                acc = acc + w[:, h : h + 1] * x[:, h * HD : (h + 1) * HD].astype(f32)
            out_ref[:, h * HD : (h + 1) * HD] = acc.astype(bf16)


def project_kernel(near_ref, far_ref, w_ref, keep_ref, send_ref, rows_ref):
    pieces = (near_ref.at[0], far_ref.at[0], near_ref.at[1], far_ref.at[1])
    group = len(pieces)
    _, requests, beams, width = near_ref.shape
    me, side = lax.axis_index("beam"), lax.axis_index("head")
    mine, spot = me // group, me % group
    for r, x in enumerate(pieces):
        for t in range(requests):
            rows_ref[lax.rem(mine - t + requests, requests), spot ^ r] = x[t]
    a = jnp.concatenate(
        [rows_ref[z, j] for z in range(requests) for j in range(group)], axis=0
    )
    out = jnp.dot(a, w_ref[...], preferred_element_type=f32)
    half = requests * BEAM_WIDTH // 2

    @pl.when(side == 0)
    def _():
        keep_ref[...] = out[:half]
        send_ref[...] = out[half:]

    @pl.when(side != 0)
    def _():
        keep_ref[...] = out[half:]
        send_ref[...] = out[:half]


def whole_blocks(n, smem=(), far=()):
    places = [pltpu.SMEM if i in smem else pltpu.HBM if i in far else pltpu.VMEM for i in range(n)]
    return [pl.BlockSpec(memory_space=place) for place in places]


def call(kernel, name, out_shape, *args, smem=(), far=(), scratch=(), vmem=8, cost=None):
    many = isinstance(out_shape, tuple)
    return pl.pallas_call(
        kernel,
        out_shape=out_shape,
        in_specs=whole_blocks(len(args), smem, far),
        out_specs=tuple(whole_blocks(len(out_shape))) if many else whole_blocks(1)[0],
        scratch_shapes=list(scratch),
        compiler_params=pltpu.CompilerParams(vmem_limit_bytes=vmem * 1024 * 1024),
        cost_estimate=cost and pl.CostEstimate(flops=cost, bytes_accessed=cost, transcendentals=0),
        name=name,
    )(*(pltpu.with_memory_space_constraint(x, pltpu.HBM) if i in far else x for i, x in enumerate(args)))


def per_device(
    queries,
    new_keys,
    new_values,
    prompt_keys,
    prompt_values,
    private_keys,
    private_values,
    parents,
    block_counts,
    out_weight,
):
    beams, width = queries.shape
    group = BEAM_WIDTH // beams
    assert group == 4
    devices = lax.axis_size("beam")
    requests = prompt_keys.shape[0]
    sides = lax.axis_size("head")
    total = width + STATS

    def swap(x, with_bit):
        return lax.ppermute(x, "beam", [(i, i ^ with_bit) for i in range(devices)])

    def shift(x, by):
        return lax.ppermute(
            x, "beam", [(i, (i + by * group) % devices) for i in range(devices)]
        )

    rows = requests * beams
    heads = width // (QPK * HD)
    length, span = prompt_keys.shape[1], private_keys.shape[1]
    line = jax.ShapeDtypeStruct((rows, total), bf16)
    asked, own, parent_tail = call(
        prep_kernel,
        "prep",
        (
            jax.ShapeDtypeStruct((beams, width), bf16),
            jax.ShapeDtypeStruct((beams, STATS), f32),
            jax.ShapeDtypeStruct((beams, STATS), bf16),
        ),
        queries,
        new_keys,
        parents,
        far=(0, 1, 2),
        scratch=[
            pltpu.VMEM(new_keys.shape, bf16),
            pltpu.SMEM((beams,), jnp.int32),
            pltpu.SemaphoreType.DMA((3,)),
        ],
    )
    came = [shift(queries, t) for t in range(1, requests)]
    prompt = jax.ShapeDtypeStruct((heads, requests // 2, length, 2 * HD), bf16)
    private = jax.ShapeDtypeStruct((heads, span, beams * HD), bf16)
    caches = call(
        load_kernel,
        "load",
        (prompt, prompt, private, private, jax.ShapeDtypeStruct((8, STATS), jnp.int32)),
        block_counts,
        prompt_keys,
        prompt_values,
        private_keys,
        private_values,
        far=(0, 1, 2, 3, 4),
        scratch=[
            pltpu.SMEM((beams,), jnp.int32),
            pltpu.SemaphoreType.DMA((1,)),
            pltpu.SemaphoreType.DMA((2, heads, requests)),
            pltpu.SemaphoreType.DMA((2, heads, beams)),
        ],
        vmem=10,
        cost=12 * 2**20,
    )
    *came, _ = lax.optimization_barrier((*came, caches[-1]))
    asked = call(line_kernel, "line", line, parent_tail, asked, *came)

    def attend(asked, name):
        many = asked.shape[0] * beams * QPK
        return call(
            attend_kernel,
            name,
            jax.ShapeDtypeStruct(asked.shape, bf16),
            asked,
            *caches,
            scratch=[
                pltpu.VMEM((2, requests * many, length), f32),
                pltpu.VMEM((2, requests * many, length), bf16),
                pltpu.VMEM((2, many, span), f32),
                pltpu.VMEM((2, many, span), bf16),
            ],
            vmem=24,
        )

    other = swap(asked, 2)
    keep0 = attend(asked[None], "attend_own")
    other, keep0 = lax.optimization_barrier((other, keep0))
    far = swap(jnp.stack([asked, other]), 1)
    keep2 = attend(other[None], "attend_side")
    far, keep2 = lax.optimization_barrier((far, keep2))
    send = attend(far, "attend_far")
    keep, send = call(
        core_kernel, "core_merge", (line, line), keep0, keep2, swap(send, 1)
    )
    piece = jax.ShapeDtypeStruct((beams, total), bf16)
    parts = call(
        plane_kernel,
        "plane_merge",
        (piece,) * requests,
        keep,
        swap(send, 2),
        scratch=[pltpu.VMEM((rows, total), bf16)],
    )
    parts = [shift(x, -t) if t else x for t, x in enumerate(parts)]
    attended = call(
        finish_kernel,
        "finish",
        jax.ShapeDtypeStruct((beams, width), bf16),
        own,
        new_values,
        *parts,
    )
    if sides == 2:
        near = jnp.stack([shift(attended, t) if t else attended for t in range(requests)])
        near = jnp.stack([near, swap(near, 2)])
        shape = jax.ShapeDtypeStruct(
            (requests * BEAM_WIDTH // 2, out_weight.shape[1]), f32
        )
        keep, send = call(
            project_kernel,
            "project",
            (shape, shape),
            near,
            swap(near, 1),
            out_weight,
            scratch=[pltpu.VMEM((requests, group, beams, width), bf16)],
            vmem=16,
        )
        return (keep + lax.ppermute(send, "head", [(0, 1), (1, 0)])).astype(bf16)
    rows = lax.all_gather(attended, "beam", axis=0, tiled=True)
    products = jnp.dot(rows, out_weight, preferred_element_type=f32)
    return lax.psum_scatter(products, "head", scatter_dimension=0, tiled=True).astype(bf16)


def solution(mesh):
    placed = (
        P("beam", "head"),
        P("beam", "head"),
        P("beam", "head"),
        P(None, "beam", "head"),
        P(None, "beam", "head"),
        P("beam", None, "head"),
        P("beam", None, "head"),
        P("beam"),
        P("beam"),
        P("head", "beam"),
    )
    return jax.shard_map(
        per_device, mesh=mesh, in_specs=placed, out_specs=P("head", "beam"), check_vma=False
    )
```

```python
import functools
import math

import jax
import jax.numpy as jnp
from jax import lax
from jax.experimental import pallas as pl
from jax.experimental.pallas import tpu as pltpu
from jax.sharding import PartitionSpec as P

HD = 128
QPK = 8
BEAM_WIDTH = 16
BLOCK_LEN = 128
STATS = 128
SCALE = 1.0 / math.sqrt(HD)
LOG2E = math.log2(math.e)

masked_score = -1e30
f32, bf16 = jnp.float32, jnp.bfloat16


def dot(a, b, ca, cb):
    return lax.dot_general(a, b, (((ca,), (cb,)), ((), ())), preferred_element_type=f32)


def soft(scores):
    top = jnp.max(scores, axis=1, keepdims=True)
    weights = jnp.exp2((scores - top) * (SCALE * LOG2E))
    return weights, top * SCALE, jnp.sum(weights, axis=1, keepdims=True)


def line_order(requests):
    return [requests - 1, 0, *range(1, requests - 1)]


def line_kernel(tail_ref, *refs):
    *pieces, out_ref = refs
    width = pieces[0].shape[1]
    for n, x in enumerate(pieces):
        out_ref[n, :, :width] = x[...]
        out_ref[n, :, width:] = tail_ref[...]


def load_private_kernel(
    q_hbm, par_hbm, cnt_hbm, ck_hbm, cv_hbm,
    q_ref, tail_ref, lim_ref, ck_ref, cv_ref, par_ref, cnt_ref, sems, old_sems,
):
    copies = [
        pltpu.make_async_copy(src, dst, sems.at[n])
        for n, (src, dst) in enumerate(((q_hbm, q_ref), (par_hbm, par_ref), (cnt_hbm, cnt_ref)))
    ] + [
        pltpu.make_async_copy(src.at[o], dst.at[o], old_sems.at[n, o])
        for n, (src, dst) in enumerate(((ck_hbm, ck_ref), (cv_hbm, cv_ref)))
        for o in range(ck_ref.shape[0])
    ]
    for x in copies:
        x.start()
    for x in copies[:3]:
        x.wait()
    row = lax.broadcasted_iota(jnp.int32, tail_ref.shape, 0)
    parent = jnp.zeros(row.shape, jnp.int32)
    for b in range(tail_ref.shape[0]):
        parent = jnp.where(row == b, par_ref[b], parent)
    tail_ref[...] = parent.astype(f32).astype(bf16)
    lane = lax.broadcasted_iota(jnp.int32, lim_ref.shape, 1)
    limit = jnp.zeros(lim_ref.shape, jnp.int32)
    for o in range(ck_ref.shape[0]):
        limit = jnp.where(lane == o, cnt_ref[o] * BLOCK_LEN, limit)
    lim_ref[...] = limit
    for x in copies[3:]:
        x.wait()


def load_prompt_kernel(group, pk_hbm, pv_hbm, pk_ref, pv_ref, sems):
    mine = lax.axis_index("beam") // group
    copies = [
        pltpu.make_async_copy(src.at[mine ^ t], dst.at[at], sems.at[n, at])
        for n, (src, dst) in enumerate(((pk_hbm, pk_ref), (pv_hbm, pv_ref)))
        for at, t in enumerate(line_order(pk_ref.shape[0]))
    ]
    for x in copies:
        x.start()
    for x in copies:
        x.wait()


def attend_kernel(qa_ref, qb_ref, pk_ref, pv_ref, lim_ref, ck_ref, cv_ref, *refs):
    *outs, s_ref, p_ref, cs_ref, cp_ref = refs
    count, half, beams, total = qa_ref.shape
    requests, length, width = pk_ref.shape
    pairs = requests // 2
    heads = width // HD
    olds, span, _ = ck_ref.shape
    block = count * beams
    stride = heads * QPK
    rows = QPK * block
    own_at = line_order(requests).index(0)
    pieces = [
        [qa_ref.at[r, n] for n in range(half)] + [qb_ref.at[r, n] for n in range(half)]
        for r in range(count)
    ]

    def beside(ref, k, places):
        return jnp.concatenate([ref[at, :, k * HD : (k + 1) * HD] for at in places], axis=1)

    me = lax.axis_index("beam")

    parent = jnp.concatenate([x[own_at][:, total - STATS :].astype(f32) for x in pieces], axis=0)
    parent = jnp.concatenate([parent] * QPK, axis=0).astype(jnp.int32) - me * olds
    column = parent[:, :1]
    local = (column >= 0) & (column < olds)
    limit = jnp.zeros((rows, 1), jnp.int32)
    for o in range(olds):
        limit = jnp.where(column == o, lim_ref[0:1, o : o + 1], limit)
    stats = [jnp.zeros((block, STATS), f32) for _ in range(requests)]
    lane = lax.broadcasted_iota(jnp.int32, (block, STATS), 1) % stride
    blank = jnp.zeros((rows, HD), bf16)
    kept = {}

    def scores(k):
        q = [
            jnp.concatenate(
                [
                    x[t][:, (k * QPK + i) * HD : (k * QPK + i + 1) * HD]
                    for i in range(QPK)
                    for x in pieces
                ],
                axis=0,
            )
            for t in range(requests)
        ]
        for u in range(pairs):
            both = jnp.concatenate(
                [
                    jnp.concatenate([q[2 * u], blank], axis=1),
                    jnp.concatenate([blank, q[2 * u + 1]], axis=1),
                ],
                axis=0,
            )
            s_ref[k, 2 * u * rows : 2 * (u + 1) * rows] = dot(
                both, beside(pk_ref, k, (2 * u, 2 * u + 1)), 1, 1
            )
        chosen = jnp.concatenate([jnp.where(parent == o, q[own_at], blank) for o in range(olds)], axis=1)
        cs_ref[k] = dot(chosen, beside(ck_ref, k, range(olds)), 1, 1)

    def weigh(k):
        p, top, den = soft(s_ref[k])
        p_ref[k] = p.astype(bf16)
        place = lax.broadcasted_iota(jnp.int32, (rows, span), 1)
        c, ctop, cden = soft(jnp.where(place < limit, cs_ref[k], masked_score))
        cp_ref[k] = c.astype(bf16)
        kept[k] = (top, den, ctop, cden)

    def values(k):
        tops, dens, ctop, cden = kept.pop(k)
        nums = []
        for u in range(pairs):
            both = dot(
                p_ref[k, 2 * u * rows : 2 * (u + 1) * rows],
                beside(pv_ref, k, (2 * u, 2 * u + 1)),
                1,
                0,
            )
            nums += [both[:rows, :HD], both[rows:, HD:]]
        every = dot(cp_ref[k], beside(cv_ref, k, range(olds)), 1, 0)
        cnum = every[:, :HD]
        for o in range(1, olds):
            cnum = jnp.where(parent == o, every[:, o * HD : (o + 1) * HD], cnum)
        done = []
        for t in range(requests):
            part = slice(t * rows, (t + 1) * rows)
            num, top, den = nums[t], tops[part], dens[part]
            if t == own_at:
                both = jnp.where(local, jnp.maximum(top, ctop), top)
                a = jnp.exp(top - both)
                e = jnp.where(local, jnp.exp(jnp.where(local, ctop, both) - both), 0.0)
                num = a * num + e * cnum
                den = a * den + e * cden
                top = both
            done.append(num * (1.0 / den))
            lse = top + jnp.log(den)
            for i in range(QPK):
                stats[t] = jnp.where(
                    lane == k * QPK + i,
                    jnp.broadcast_to(
                        lse[i * block : (i + 1) * block], (block, STATS)
                    ),
                    stats[t],
                )
        for i in range(QPK):
            cols = slice((k * QPK + i) * HD, (k * QPK + i + 1) * HD)
            for r, out in enumerate(outs):
                first = i * block + r * beams
                out[:, cols] = jnp.concatenate(
                    [x[first : first + beams] for x in done], axis=0
                ).astype(bf16)

    for stage in (scores, weigh, values):
        for k in range(heads):
            stage(k)
    for r, out in enumerate(outs):
        out[:, total - STATS :] = pack_stats(
            jnp.concatenate([x[r * beams : (r + 1) * beams] for x in stats], axis=0), stride
        )


def pack_stats(x, stride):
    hi = x.astype(bf16).astype(f32)
    mid = (x - hi).astype(bf16).astype(f32)
    which = lax.broadcasted_iota(jnp.int32, x.shape, 1) // stride
    return jnp.where(which == 0, hi, jnp.where(which == 1, mid, x - hi - mid)).astype(bf16)


def read_stats(x, stride):
    x = x.astype(f32)
    return x + pltpu.roll(x, STATS - stride, 1) + pltpu.roll(x, STATS - 2 * stride, 1)


def merge(a, b, outs):
    total = a.shape[1]
    count = (total - STATS) // HD
    size = a.shape[0] // len(outs)

    def store(cols, value):
        for n, out in enumerate(outs):
            out[:, cols] = value[n * size : (n + 1) * size]

    la, lb = read_stats(a[:, total - STATS :], count), read_stats(b[:, total - STATS :], count)
    top = jnp.maximum(la, lb)
    wa, wb = jnp.exp(la - top), jnp.exp(lb - top)
    den = wa + wb
    wa = wa * (1.0 / den)
    wb = wb * (1.0 / den)
    for h in range(count):
        cols = slice(h * HD, (h + 1) * HD)
        store(
            cols,
            (
                wa[:, h : h + 1] * a[:, cols].astype(f32)
                + wb[:, h : h + 1] * b[:, cols].astype(f32)
            ).astype(bf16),
        )
    lse = top + jnp.log(den)
    lane = lax.broadcasted_iota(jnp.int32, lse.shape, 1)
    again = jnp.where(
        lane < count,
        lse,
        jnp.where(lane < 2 * count, pltpu.roll(lse, count, 1), pltpu.roll(lse, 2 * count, 1)),
    )
    store(slice(total - STATS, total), pack_stats(again, count))


def core_kernel(kept_ref, came_ref, a_ref, b_ref):
    half = a_ref.shape[0]
    outs = {2 * half - 1 - n: ref.at[n % half] for n, ref in enumerate([a_ref] * half + [b_ref] * half)}
    merge(kept_ref, came_ref, [outs[t] for t in line_order(2 * half)])


def plane_kernel(kept_ref, came_ref, *outs):
    kept, came = (
        jnp.concatenate([x[n] for n in range(len(outs))], axis=0) for x in (kept_ref, came_ref)
    )
    merge(kept, came, outs)


def finish_kernel(q_ref, nk_ref, nv_ref, *refs):
    *parts, out_ref = refs
    beams, total = parts[0].shape
    heads = nv_ref.shape[1] // HD
    stride = heads * QPK
    lane = lax.broadcasted_iota(jnp.int32, (beams, STATS), 1)
    own = jnp.zeros((beams, STATS), f32)
    for h in range(stride):
        key = nk_ref[:, h // QPK * HD : (h // QPK + 1) * HD].astype(f32)
        s = jnp.sum(q_ref[:, h * HD : (h + 1) * HD].astype(f32) * key, axis=1, keepdims=True)
        own = jnp.where(lane == h, s * SCALE, own)
    lses = [read_stats(x[:, total - STATS :], stride) for x in parts]
    top = functools.reduce(jnp.maximum, lses, own)
    ws = [jnp.exp(x - top) for x in lses]
    w_own = jnp.exp(own - top)
    inv = 1.0 / functools.reduce(jnp.add, ws, w_own)
    ws = [w * inv for w in ws]
    w_own = w_own * inv
    for k in range(heads):
        value = nv_ref[:, k * HD : (k + 1) * HD].astype(f32)
        for i in range(QPK):
            h = k * QPK + i
            acc = w_own[:, h : h + 1] * value
            for w, x in zip(ws, parts):
                acc = acc + w[:, h : h + 1] * x[:, h * HD : (h + 1) * HD].astype(f32)
            out_ref[:, h * HD : (h + 1) * HD] = acc.astype(bf16)


def project_kernel(near_a, far_a, near_b, far_b, w_ref, keep_ref, send_ref, rows_ref):
    requests, group = rows_ref.shape[:2]
    me, side = lax.axis_index("beam"), lax.axis_index("head")
    mine, spot = me // group, me % group
    order = [0, requests - 1] + list(range(1, requests - 1))
    for first, refs in ((0, (near_a, far_a)), (requests // 2, (near_b, far_b))):
        for core, ref in enumerate(refs):
            for x in range(2):
                for n in range(requests // 2):
                    rows_ref[mine ^ order[first + n], spot ^ (2 * x + core)] = ref[x, n]
    a = jnp.concatenate(
        [rows_ref[z, j] for z in range(requests) for j in range(group)], axis=0
    )
    out = jnp.dot(a, w_ref[...], preferred_element_type=f32)
    half = requests * BEAM_WIDTH // 2

    @pl.when(side == 0)
    def _():
        keep_ref[...] = out[:half]
        send_ref[...] = out[half:].astype(bf16)

    @pl.when(side != 0)
    def _():
        keep_ref[...] = out[half:]
        send_ref[...] = out[:half].astype(bf16)


def whole_blocks(n, smem=(), far=()):
    places = [pltpu.SMEM if i in smem else pltpu.HBM if i in far else pltpu.VMEM for i in range(n)]
    return [pl.BlockSpec(memory_space=place) for place in places]


def call(kernel, name, out_shape, *args, smem=(), far=(), scratch=(), vmem=8, cost=None):
    many = isinstance(out_shape, tuple)
    return pl.pallas_call(
        kernel,
        out_shape=out_shape,
        in_specs=whole_blocks(len(args), smem, far),
        out_specs=tuple(whole_blocks(len(out_shape))) if many else whole_blocks(1)[0],
        scratch_shapes=list(scratch),
        compiler_params=pltpu.CompilerParams(vmem_limit_bytes=vmem * 1024 * 1024),
        cost_estimate=cost and pl.CostEstimate(flops=cost, bytes_accessed=cost, transcendentals=0),
        name=name,
    )(*(pltpu.with_memory_space_constraint(x, pltpu.HBM) if i in far else x for i, x in enumerate(args)))


def per_device(
    queries,
    new_keys,
    new_values,
    prompt_keys,
    prompt_values,
    private_keys,
    private_values,
    parents,
    block_counts,
    out_weight,
):
    beams, width = queries.shape
    group = BEAM_WIDTH // beams
    assert group == 4
    devices = lax.axis_size("beam")
    requests = prompt_keys.shape[0]
    sides = lax.axis_size("head")
    total = width + STATS

    def swap(x, with_bit):
        return lax.ppermute(x, "beam", [(i, i ^ with_bit) for i in range(devices)])

    rows = requests * beams
    heads = width // (QPK * HD)
    length, span = prompt_keys.shape[1], private_keys.shape[1]
    line = jax.ShapeDtypeStruct((rows, total), bf16)
    order = line_order(requests)
    middle = requests // 2
    came = {t: swap(queries, t * group) for t in [requests - 1, *range(1, requests - 1)]}
    prompt = jax.ShapeDtypeStruct(prompt_keys.shape, bf16)
    private = jax.ShapeDtypeStruct(private_keys.shape, bf16)
    own, parent_tail, *olds = call(
        load_private_kernel,
        "load_private",
        (
            jax.ShapeDtypeStruct((beams, width), bf16),
            jax.ShapeDtypeStruct((beams, STATS), bf16),
            jax.ShapeDtypeStruct((8, STATS), jnp.int32),
            private,
            private,
        ),
        queries,
        parents,
        block_counts,
        private_keys,
        private_values,
        far=(0, 1, 2, 3, 4),
        scratch=[
            pltpu.SMEM((beams,), jnp.int32),
            pltpu.SMEM((beams,), jnp.int32),
            pltpu.SemaphoreType.DMA((3,)),
            pltpu.SemaphoreType.DMA((2, beams)),
        ],
        vmem=10,
        cost=8 * 2**20,
    )
    came[requests - 1], parent_tail = lax.optimization_barrier((came[requests - 1], parent_tail))
    came[0] = own
    asked_a = call(
        line_kernel,
        "line",
        jax.ShapeDtypeStruct((middle, beams, total), bf16),
        parent_tail,
        *(came[t] for t in order[:middle]),
    )
    asked_b = jnp.stack([came[t] for t in order[middle:]])
    prompt_keys, prompt_values, _ = lax.optimization_barrier((prompt_keys, prompt_values, asked_b))
    prompts = call(
        functools.partial(load_prompt_kernel, group),
        "load_prompt",
        (prompt, prompt),
        prompt_keys,
        prompt_values,
        far=(0, 1),
        scratch=[pltpu.SemaphoreType.DMA((2, requests))],
        vmem=10,
        cost=4 * 2**20,
    )
    caches = (*prompts, *olds)

    def attend(asked_a, asked_b, name):
        many = asked_a.shape[0] * beams * QPK
        return call(
            attend_kernel,
            name,
            (line,) * asked_a.shape[0],
            asked_a,
            asked_b,
            *caches,
            scratch=[
                pltpu.VMEM((heads, requests * many, length), f32),
                pltpu.VMEM((heads, requests * many, length), bf16),
                pltpu.VMEM((heads, many, span), f32),
                pltpu.VMEM((heads, many, span), bf16),
            ],
            vmem=24,
        )

    other_a, other_b = swap(asked_a, 2), swap(asked_b, 2)
    (keep0,) = attend(asked_a[None], asked_b[None], "attend_own")
    other_a, other_b, keep0 = lax.optimization_barrier((other_a, other_b, keep0))
    far_a = swap(jnp.stack([asked_a, other_a]), 1)
    far_b = swap(jnp.stack([asked_b, other_b]), 1)
    (keep2,) = attend(other_a[None], other_b[None], "attend_side")
    far_a, far_b, keep2 = lax.optimization_barrier((far_a, far_b, keep2))
    far_own, far_side = attend(far_a, far_b, "attend_far")
    half = jax.ShapeDtypeStruct((requests // 2, beams, total), bf16)
    send_a, send_b = call(core_kernel, "side_merge", (half, half), keep2, swap(far_side, 1))
    keep_a, keep_b = call(core_kernel, "own_merge", (half, half), keep0, swap(far_own, 1))
    piece = jax.ShapeDtypeStruct((beams, total), bf16)
    parts = []
    for keep, send in ((keep_a, send_a), (keep_b, send_b)):
        parts += call(
            plane_kernel, "plane_merge", (piece,) * (requests // 2), keep, swap(send, 2)
        )
    parts = [
        swap(x, t * group) if t else x for t, x in zip(range(requests - 1, -1, -1), parts)
    ]
    attended = call(
        finish_kernel,
        "finish",
        jax.ShapeDtypeStruct((beams, width), bf16),
        own,
        new_keys,
        new_values,
        *parts,
    )
    if sides == 2:
        line = [attended] + [
            swap(attended, t * group) for t in [requests - 1, *range(1, requests - 1)]
        ]
        halves = []
        for pieces in (line[: requests // 2], line[requests // 2 :]):
            near = jnp.stack(pieces)
            near = jnp.stack([near, swap(near, 2)])
            halves += [near, swap(near, 1)]
        shape = (requests * BEAM_WIDTH // 2, out_weight.shape[1])
        keep, send = call(
            project_kernel,
            "project",
            (jax.ShapeDtypeStruct(shape, f32), jax.ShapeDtypeStruct(shape, bf16)),
            *halves,
            out_weight,
            scratch=[pltpu.VMEM((requests, group, beams, width), bf16)],
            vmem=16,
        )
        came = lax.ppermute(send, "head", [(0, 1), (1, 0)])
        return (keep + came.astype(f32)).astype(bf16)
    rows = lax.all_gather(attended, "beam", axis=0, tiled=True)
    products = jnp.dot(rows, out_weight, preferred_element_type=f32)
    return lax.psum_scatter(products, "head", scatter_dimension=0, tiled=True).astype(bf16)


def solution(mesh):
    placed = (
        P("beam", "head"),
        P("beam", "head"),
        P("beam", "head"),
        P(None, "beam", "head"),
        P(None, "beam", "head"),
        P("beam", None, "head"),
        P("beam", None, "head"),
        P("beam"),
        P("beam"),
        P("head", "beam"),
    )
    return jax.shard_map(
        per_device, mesh=mesh, in_specs=placed, out_specs=P("head", "beam"), check_vma=False
    )
```

```python
import functools
import math

import jax
import jax.numpy as jnp
from jax import lax
from jax.experimental import pallas as pl
from jax.experimental.pallas import tpu as pltpu
from jax.sharding import PartitionSpec as P

HD = 128
QPK = 8
BEAM_WIDTH = 16
BLOCK_LEN = 128
STATS = 128
SCALE = 1.0 / math.sqrt(HD)
LOG2E = math.log2(math.e)

masked_score = -1e30
f32, bf16 = jnp.float32, jnp.bfloat16


def dot(a, b, ca, cb):
    return lax.dot_general(a, b, (((ca,), (cb,)), ((), ())), preferred_element_type=f32)


def soft(scores):
    top = jnp.max(scores, axis=1, keepdims=True)
    weights = jnp.exp2((scores - top) * (SCALE * LOG2E))
    return weights, top * SCALE, jnp.sum(weights, axis=1, keepdims=True)


def line_order(requests):
    return list(range(requests))[::-1]


def line_kernel(tail_ref, *refs):
    *pieces, out_ref = refs
    width = pieces[0].shape[1]
    out_ref[:, :width] = jnp.concatenate([x[...] for x in pieces], axis=0)
    out_ref[:, width:] = jnp.concatenate([tail_ref[...]] * len(pieces), axis=0)


def load_private_kernel(
    q_hbm, par_hbm, cnt_hbm, ck_hbm, cv_hbm,
    q_ref, tail_ref, lim_ref, ck_ref, cv_ref, par_ref, cnt_ref, sems, old_sems,
):
    heads = ck_ref.shape[0]
    olds = ck_hbm.shape[0]
    copies = [
        pltpu.make_async_copy(src, dst, sems.at[n])
        for n, (src, dst) in enumerate(((q_hbm, q_ref), (par_hbm, par_ref), (cnt_hbm, cnt_ref)))
    ]
    for k in range(heads):
        for n, (src, dst) in enumerate(((ck_hbm, ck_ref), (cv_hbm, cv_ref))):
            for o in range(olds):
                copies.append(
                    pltpu.make_async_copy(
                        src.at[o, :, pl.ds(k * HD, HD)],
                        dst.at[k, :, pl.ds(o * HD, HD)],
                        old_sems.at[n, k, o],
                    )
                )
    for x in copies:
        x.start()
    for x in copies[:3]:
        x.wait()
    row = lax.broadcasted_iota(jnp.int32, tail_ref.shape, 0)
    parent = jnp.zeros(row.shape, jnp.int32)
    for b in range(tail_ref.shape[0]):
        parent = jnp.where(row == b, par_ref[b], parent)
    tail_ref[...] = parent.astype(f32).astype(bf16)
    lane = lax.broadcasted_iota(jnp.int32, lim_ref.shape, 1)
    limit = jnp.zeros(lim_ref.shape, jnp.int32)
    for o in range(olds):
        limit = jnp.where(lane == o, cnt_ref[o] * BLOCK_LEN, limit)
    lim_ref[...] = limit
    for x in copies[3:]:
        x.wait()


def load_prompt_kernel(group, pk_hbm, pv_hbm, pk_ref, pv_ref, sems):
    heads, pairs, _, _ = pk_ref.shape
    mine = lax.axis_index("beam") // group
    order = line_order(2 * pairs)
    copies = [
        pltpu.make_async_copy(
            src.at[mine ^ t, :, pl.ds(k * HD, HD)],
            dst.at[k, at // 2, :, pl.ds(at % 2 * HD, HD)],
            sems.at[n, k, at],
        )
        for k in range(heads)
        for n, (src, dst) in enumerate(((pk_hbm, pk_ref), (pv_hbm, pv_ref)))
        for at, t in enumerate(order)
    ]
    for x in copies:
        x.start()
    for x in copies:
        x.wait()


def attend_kernel(other, q_ref, pk_ref, pv_ref, lim_ref, ck_ref, cv_ref, *refs):
    *outs, s_ref, p_ref, cs_ref, cp_ref = refs
    count = q_ref.shape[0]
    pieces = [q_ref.at[r] for r in range(count)]
    total = q_ref.shape[2]
    heads = (total - STATS) // (QPK * HD)
    if other:
        requests, length, _ = pk_ref.shape
        olds, span, _ = ck_ref.shape
    else:
        _, pairs, length, _ = pk_ref.shape
        requests = 2 * pairs
        _, span, olds = ck_ref.shape
        olds = olds // HD
    pairs = requests // 2
    beams = q_ref.shape[1] // requests
    block = count * beams
    stride = heads * QPK
    rows = QPK * block
    me = lax.axis_index("beam")
    mine = me // (BEAM_WIDTH // beams)
    order = line_order(requests)

    def prompt(ref, k, u):
        if not other:
            return ref[k, u]
        both = [ref[mine ^ order[2 * u + n], :, k * HD : (k + 1) * HD] for n in range(2)]
        return jnp.concatenate(both, axis=1)

    def private(ref, k):
        if not other:
            return ref[k]
        return jnp.concatenate([ref[o, :, k * HD : (k + 1) * HD] for o in range(olds)], axis=1)

    parent = jnp.concatenate([x[:, total - STATS :].astype(f32)[:beams] for x in pieces], axis=0)
    parent = jnp.concatenate([parent] * QPK, axis=0).astype(jnp.int32) - (me ^ other) * olds
    column = parent[:, :1]
    local = (column >= 0) & (column < olds)
    limit = jnp.zeros((rows, 1), jnp.int32)
    for o in range(olds):
        limit = jnp.where(column == o, lim_ref[0:1, o : o + 1], limit)
    stats = [jnp.zeros((block, STATS), f32) for _ in range(requests)]
    lane = lax.broadcasted_iota(jnp.int32, (block, STATS), 1) % stride
    blank = jnp.zeros((rows, HD), bf16)
    kept = {}

    def scores(k):
        tiles = [
            x[:, (k * QPK + i) * HD : (k * QPK + i + 1) * HD] for i in range(QPK) for x in pieces
        ]
        q = [
            jnp.concatenate([x[t * beams : (t + 1) * beams] for x in tiles], axis=0)
            for t in range(requests)
        ]
        for u in range(pairs):
            both = jnp.concatenate(
                [
                    jnp.concatenate([q[2 * u], blank], axis=1),
                    jnp.concatenate([blank, q[2 * u + 1]], axis=1),
                ],
                axis=0,
            )
            s_ref[k, 2 * u * rows : 2 * (u + 1) * rows] = dot(both, prompt(pk_ref, k, u), 1, 1)
        chosen = jnp.concatenate([jnp.where(parent == o, q[-1], blank) for o in range(olds)], axis=1)
        cs_ref[k] = dot(chosen, private(ck_ref, k), 1, 1)

    def weigh(k):
        p, top, den = soft(s_ref[k])
        p_ref[k] = p.astype(bf16)
        place = lax.broadcasted_iota(jnp.int32, (rows, span), 1)
        c, ctop, cden = soft(jnp.where(place < limit, cs_ref[k], masked_score))
        cp_ref[k] = c.astype(bf16)
        kept[k] = (top, den, ctop, cden)

    def values(k):
        tops, dens, ctop, cden = kept.pop(k)
        nums = []
        for u in range(pairs):
            both = dot(p_ref[k, 2 * u * rows : 2 * (u + 1) * rows], prompt(pv_ref, k, u), 1, 0)
            nums += [both[:rows, :HD], both[rows:, HD:]]
        every = dot(cp_ref[k], private(cv_ref, k), 1, 0)
        cnum = every[:, :HD]
        for o in range(1, olds):
            cnum = jnp.where(parent == o, every[:, o * HD : (o + 1) * HD], cnum)
        done = []
        for t in range(requests):
            part = slice(t * rows, (t + 1) * rows)
            num, top, den = nums[t], tops[part], dens[part]
            if t == requests - 1:
                both = jnp.where(local, jnp.maximum(top, ctop), top)
                a = jnp.exp(top - both)
                e = jnp.where(local, jnp.exp(jnp.where(local, ctop, both) - both), 0.0)
                num = a * num + e * cnum
                den = a * den + e * cden
                top = both
            done.append(num * (1.0 / den))
            lse = top + jnp.log(den)
            for i in range(QPK):
                stats[t] = jnp.where(
                    lane == k * QPK + i,
                    jnp.broadcast_to(
                        lse[i * block : (i + 1) * block], (block, STATS)
                    ),
                    stats[t],
                )
        for i in range(QPK):
            cols = slice((k * QPK + i) * HD, (k * QPK + i + 1) * HD)
            for r, out in enumerate(outs):
                first = i * block + r * beams
                out[:, cols] = jnp.concatenate(
                    [x[first : first + beams] for x in done], axis=0
                ).astype(bf16)

    for stage in (scores, weigh, values):
        for k in range(heads):
            stage(k)
    for r, out in enumerate(outs):
        out[:, total - STATS :] = pack_stats(
            jnp.concatenate([x[r * beams : (r + 1) * beams] for x in stats], axis=0), stride
        )


def pack_stats(x, stride):
    hi = x.astype(bf16).astype(f32)
    mid = (x - hi).astype(bf16).astype(f32)
    which = lax.broadcasted_iota(jnp.int32, x.shape, 1) // stride
    return jnp.where(which == 0, hi, jnp.where(which == 1, mid, x - hi - mid)).astype(bf16)


def read_stats(x, stride):
    x = x.astype(f32)
    return x + pltpu.roll(x, STATS - stride, 1) + pltpu.roll(x, STATS - 2 * stride, 1)


def merge(a, b, outs):
    total = a.shape[1]
    count = (total - STATS) // HD
    size = a.shape[0] // len(outs)

    def store(cols, value):
        for n, out in enumerate(outs):
            out[:, cols] = value[n * size : (n + 1) * size]

    la, lb = read_stats(a[:, total - STATS :], count), read_stats(b[:, total - STATS :], count)
    top = jnp.maximum(la, lb)
    wa, wb = jnp.exp(la - top), jnp.exp(lb - top)
    den = wa + wb
    wa = wa * (1.0 / den)
    wb = wb * (1.0 / den)
    for h in range(count):
        cols = slice(h * HD, (h + 1) * HD)
        store(
            cols,
            (
                wa[:, h : h + 1] * a[:, cols].astype(f32)
                + wb[:, h : h + 1] * b[:, cols].astype(f32)
            ).astype(bf16),
        )
    lse = top + jnp.log(den)
    lane = lax.broadcasted_iota(jnp.int32, lse.shape, 1)
    again = jnp.where(
        lane < count,
        lse,
        jnp.where(lane < 2 * count, pltpu.roll(lse, count, 1), pltpu.roll(lse, 2 * count, 1)),
    )
    store(slice(total - STATS, total), pack_stats(again, count))


def core_kernel(kept_ref, came_ref, *outs):
    merge(kept_ref, came_ref, [out.at[n] for out in outs for n in range(out.shape[0])])


def plane_kernel(kept_ref, came_ref, *outs):
    kept, came = (
        jnp.concatenate([x[n] for n in range(len(outs))], axis=0) for x in (kept_ref, came_ref)
    )
    merge(kept, came, outs)


def finish_kernel(q_ref, nk_ref, nv_ref, *refs):
    *parts, out_ref = refs
    beams, total = parts[0].shape
    heads = nv_ref.shape[1] // HD
    stride = heads * QPK
    lane = lax.broadcasted_iota(jnp.int32, (beams, STATS), 1)
    own = jnp.zeros((beams, STATS), f32)
    for h in range(stride):
        key = nk_ref[:, h // QPK * HD : (h // QPK + 1) * HD].astype(f32)
        s = jnp.sum(q_ref[:, h * HD : (h + 1) * HD].astype(f32) * key, axis=1, keepdims=True)
        own = jnp.where(lane == h, s * SCALE, own)
    lses = [read_stats(x[:, total - STATS :], stride) for x in parts]
    top = functools.reduce(jnp.maximum, lses, own)
    ws = [jnp.exp(x - top) for x in lses]
    w_own = jnp.exp(own - top)
    inv = 1.0 / functools.reduce(jnp.add, ws, w_own)
    ws = [w * inv for w in ws]
    w_own = w_own * inv
    for k in range(heads):
        value = nv_ref[:, k * HD : (k + 1) * HD].astype(f32)
        for i in range(QPK):
            h = k * QPK + i
            acc = w_own[:, h : h + 1] * value
            for w, x in zip(ws, parts):
                acc = acc + w[:, h : h + 1] * x[:, h * HD : (h + 1) * HD].astype(f32)
            out_ref[:, h * HD : (h + 1) * HD] = acc.astype(bf16)


def project_kernel(near_a, far_a, near_b, far_b, w_ref, keep_ref, send_ref, rows_ref):
    requests, group = rows_ref.shape[:2]
    me, side = lax.axis_index("beam"), lax.axis_index("head")
    mine, spot = me // group, me % group
    order = line_order(requests)
    order = order[-1:] + order[:1] + order[-2:0:-1]
    for first, refs in ((0, (near_a, far_a)), (requests // 2, (near_b, far_b))):
        for core, ref in enumerate(refs):
            for x in range(2):
                for n in range(requests // 2):
                    rows_ref[mine ^ order[first + n], spot ^ (2 * x + core)] = ref[x, n]
    a = jnp.concatenate(
        [rows_ref[z, j] for z in range(requests) for j in range(group)], axis=0
    )
    out = jnp.dot(a, w_ref[...], preferred_element_type=f32)
    half = requests * BEAM_WIDTH // 2

    @pl.when(side == 0)
    def _():
        keep_ref[...] = out[:half]
        send_ref[...] = out[half:].astype(bf16)

    @pl.when(side != 0)
    def _():
        keep_ref[...] = out[half:]
        send_ref[...] = out[:half].astype(bf16)


def whole_blocks(n, smem=(), far=()):
    places = [pltpu.SMEM if i in smem else pltpu.HBM if i in far else pltpu.VMEM for i in range(n)]
    return [pl.BlockSpec(memory_space=place) for place in places]


def call(kernel, name, out_shape, *args, smem=(), far=(), scratch=(), vmem=8, cost=None):
    many = isinstance(out_shape, tuple)
    return pl.pallas_call(
        kernel,
        out_shape=out_shape,
        in_specs=whole_blocks(len(args), smem, far),
        out_specs=tuple(whole_blocks(len(out_shape))) if many else whole_blocks(1)[0],
        scratch_shapes=list(scratch),
        compiler_params=pltpu.CompilerParams(vmem_limit_bytes=vmem * 1024 * 1024),
        cost_estimate=cost and pl.CostEstimate(flops=cost, bytes_accessed=cost, transcendentals=0),
        name=name,
    )(*(pltpu.with_memory_space_constraint(x, pltpu.HBM) if i in far else x for i, x in enumerate(args)))


def per_device(
    queries,
    new_keys,
    new_values,
    prompt_keys,
    prompt_values,
    private_keys,
    private_values,
    parents,
    block_counts,
    out_weight,
):
    beams, width = queries.shape
    group = BEAM_WIDTH // beams
    assert group == 4
    devices = lax.axis_size("beam")
    requests = prompt_keys.shape[0]
    sides = lax.axis_size("head")
    total = width + STATS

    def swap(x, with_bit):
        return lax.ppermute(x, "beam", [(i, i ^ with_bit) for i in range(devices)])

    rows = requests * beams
    heads = width // (QPK * HD)
    length, span = prompt_keys.shape[1], private_keys.shape[1]
    line = jax.ShapeDtypeStruct((rows, total), bf16)
    order = line_order(requests)
    others = order[:-1]
    came = [swap(queries, t * group) for t in others]
    prompt = jax.ShapeDtypeStruct((heads, requests // 2, length, 2 * HD), bf16)
    private = jax.ShapeDtypeStruct((heads, span, beams * HD), bf16)
    stored = (swap(private_keys, 1), swap(private_values, 1))
    own, parent_tail, *olds = call(
        load_private_kernel,
        "load_private",
        (
            jax.ShapeDtypeStruct((beams, width), bf16),
            jax.ShapeDtypeStruct((beams, STATS), bf16),
            jax.ShapeDtypeStruct((8, STATS), jnp.int32),
            private,
            private,
        ),
        queries,
        parents,
        block_counts,
        private_keys,
        private_values,
        far=(0, 1, 2, 3, 4),
        scratch=[
            pltpu.SMEM((beams,), jnp.int32),
            pltpu.SMEM((beams,), jnp.int32),
            pltpu.SemaphoreType.DMA((3,)),
            pltpu.SemaphoreType.DMA((2, heads, beams)),
        ],
        vmem=10,
        cost=2**26,
    )
    *came, parent_tail = lax.optimization_barrier((*came, parent_tail))
    asked = call(line_kernel, "line", line, parent_tail, *came, own)
    prompt_keys, prompt_values, _ = lax.optimization_barrier((prompt_keys, prompt_values, asked))
    prompts = call(
        functools.partial(load_prompt_kernel, group),
        "load_prompt",
        (prompt, prompt),
        prompt_keys,
        prompt_values,
        far=(0, 1),
        scratch=[pltpu.SemaphoreType.DMA((2, heads, requests))],
        vmem=10,
        cost=2**26,
    )
    caches = (*prompts, *olds)
    stored = (swap(prompt_keys, 1), swap(prompt_values, 1), swap(olds[0], 1), *stored)

    def attend(asked, name, caches, other=0):
        many = asked.shape[0] * beams * QPK
        return call(
            functools.partial(attend_kernel, other),
            name,
            (line,) * asked.shape[0],
            asked,
            *caches,
            scratch=[
                pltpu.VMEM((heads, requests * many, length), f32),
                pltpu.VMEM((heads, requests * many, length), bf16),
                pltpu.VMEM((heads, many, span), f32),
                pltpu.VMEM((heads, many, span), bf16),
            ],
            vmem=24,
            cost=2**26,
        )

    other = swap(asked, 2)
    (own_here,) = attend(asked[None], "attend_own", caches)
    other, own_here = lax.optimization_barrier((other, own_here))
    (side_here,) = attend(other[None], "attend_side", caches)
    (side_there,) = attend(other[None], "attend_side_other", stored, 1)
    half = jax.ShapeDtypeStruct((requests // 2, beams, total), bf16)
    send_a, send_b = call(core_kernel, "side_merge", (half, half), side_here, side_there)
    asked, _ = lax.optimization_barrier((asked, send_a))
    (own_there,) = attend(asked[None], "attend_own_other", stored, 1)
    keep_a, keep_b = call(core_kernel, "own_merge", (half, half), own_here, own_there)
    piece = jax.ShapeDtypeStruct((beams, total), bf16)
    parts = []
    for keep, send in ((keep_a, send_a), (keep_b, send_b)):
        parts += call(
            plane_kernel, "plane_merge", (piece,) * (requests // 2), keep, swap(send, 2)
        )
    parts = [swap(x, t * group) if t else x for t, x in zip(order, parts)]
    attended = call(
        finish_kernel,
        "finish",
        jax.ShapeDtypeStruct((beams, width), bf16),
        own,
        new_keys,
        new_values,
        *parts,
    )
    if sides == 2:
        line = [attended] + [swap(attended, t * group) for t in others[:1] + others[:0:-1]]
        halves = []
        for pieces in (line[: requests // 2], line[requests // 2 :]):
            near = jnp.stack(pieces)
            near = jnp.stack([near, swap(near, 2)])
            halves += [near, swap(near, 1)]
        shape = (requests * BEAM_WIDTH // 2, out_weight.shape[1])
        keep, send = call(
            project_kernel,
            "project",
            (jax.ShapeDtypeStruct(shape, f32), jax.ShapeDtypeStruct(shape, bf16)),
            *halves,
            out_weight,
            scratch=[pltpu.VMEM((requests, group, beams, width), bf16)],
            vmem=16,
        )
        came = lax.ppermute(send, "head", [(0, 1), (1, 0)])
        return (keep + came.astype(f32)).astype(bf16)
    rows = lax.all_gather(attended, "beam", axis=0, tiled=True)
    products = jnp.dot(rows, out_weight, preferred_element_type=f32)
    return lax.psum_scatter(products, "head", scatter_dimension=0, tiled=True).astype(bf16)


def solution(mesh):
    placed = (
        P("beam", "head"),
        P("beam", "head"),
        P("beam", "head"),
        P(None, "beam", "head"),
        P(None, "beam", "head"),
        P("beam", None, "head"),
        P("beam", None, "head"),
        P("beam"),
        P("beam"),
        P("head", "beam"),
    )
    return jax.shard_map(
        per_device, mesh=mesh, in_specs=placed, out_specs=P("head", "beam"), check_vma=False
    )
```

```python
import functools
import math

import jax
import jax.numpy as jnp
from jax import lax
from jax.experimental import pallas as pl
from jax.experimental.pallas import tpu as pltpu
from jax.sharding import PartitionSpec as P

HD = 128
QPK = 8
BEAM_WIDTH = 16
BLOCK_LEN = 128
STATS = 128
SCALE = 1.0 / math.sqrt(HD)
LOG2E = math.log2(math.e)

masked_score = -1e30
f32, bf16 = jnp.float32, jnp.bfloat16


def dot(a, b, ca, cb):
    return lax.dot_general(a, b, (((ca,), (cb,)), ((), ())), preferred_element_type=f32)


def soft(scores):
    top = jnp.max(scores, axis=1, keepdims=True)
    weights = jnp.exp2((scores - top) * (SCALE * LOG2E))
    return weights, top * SCALE, jnp.sum(weights, axis=1, keepdims=True)


def line_order(requests):
    return list(range(requests))[::-1]


def line_kernel(tail_ref, *refs):
    *pieces, out_ref = refs
    width = pieces[0].shape[1]
    out_ref[:, :width] = jnp.concatenate([x[...] for x in pieces], axis=0)
    out_ref[:, width:] = jnp.concatenate([tail_ref[...]] * len(pieces), axis=0)


def load_private_kernel(
    q_hbm, par_hbm, cnt_hbm, ck_hbm, cv_hbm,
    q_ref, tail_ref, lim_ref, ck_ref, cv_ref, par_ref, cnt_ref, sems, old_sems,
):
    heads = ck_ref.shape[0]
    olds = ck_hbm.shape[0]
    copies = [
        pltpu.make_async_copy(src, dst, sems.at[n])
        for n, (src, dst) in enumerate(((q_hbm, q_ref), (par_hbm, par_ref), (cnt_hbm, cnt_ref)))
    ]
    for k in range(heads):
        for n, (src, dst) in enumerate(((ck_hbm, ck_ref), (cv_hbm, cv_ref))):
            for o in range(olds):
                copies.append(
                    pltpu.make_async_copy(
                        src.at[o, :, pl.ds(k * HD, HD)],
                        dst.at[k, :, pl.ds(o * HD, HD)],
                        old_sems.at[n, k, o],
                    )
                )
    for x in copies:
        x.start()
    for x in copies[:3]:
        x.wait()
    row = lax.broadcasted_iota(jnp.int32, tail_ref.shape, 0)
    parent = jnp.zeros(row.shape, jnp.int32)
    for b in range(tail_ref.shape[0]):
        parent = jnp.where(row == b, par_ref[b], parent)
    tail_ref[...] = parent.astype(f32).astype(bf16)
    lane = lax.broadcasted_iota(jnp.int32, lim_ref.shape, 1)
    limit = jnp.zeros(lim_ref.shape, jnp.int32)
    for o in range(olds):
        limit = jnp.where(lane == o, cnt_ref[o] * BLOCK_LEN, limit)
    lim_ref[...] = limit
    for x in copies[3:]:
        x.wait()


def load_prompt_kernel(group, pk_hbm, pv_hbm, pk_ref, pv_ref, sems):
    heads, pairs, _, _ = pk_ref.shape
    mine = lax.axis_index("beam") // group
    order = line_order(2 * pairs)
    copies = [
        pltpu.make_async_copy(
            src.at[mine ^ t, :, pl.ds(k * HD, HD)],
            dst.at[k, at // 2, :, pl.ds(at % 2 * HD, HD)],
            sems.at[n, k, at],
        )
        for k in range(heads)
        for n, (src, dst) in enumerate(((pk_hbm, pk_ref), (pv_hbm, pv_ref)))
        for at, t in enumerate(order)
    ]
    for x in copies:
        x.start()
    for x in copies:
        x.wait()


def attend_kernel(kinds, q_ref, *refs):
    total = q_ref.shape[1]
    heads = (total - STATS) // (QPK * HD)
    caches = [refs[5 * n : 5 * n + 5] for n in range(len(kinds))]
    *outs, s_ref, p_ref, cs_ref, cp_ref = refs[5 * len(kinds) :]
    requests, span = s_ref.shape[2] // cs_ref.shape[2], cs_ref.shape[3]
    pairs = requests // 2
    beams = q_ref.shape[0] // requests
    stride = heads * QPK
    rows = QPK * beams
    me = lax.axis_index("beam")
    mine = me // (BEAM_WIDTH // beams)
    order = line_order(requests)
    olds = beams

    def prompt(n, ref, k, u):
        if not kinds[n]:
            return ref[k, u]
        both = [ref[mine ^ order[2 * u + m], :, k * HD : (k + 1) * HD] for m in range(2)]
        return jnp.concatenate(both, axis=1)

    def private(n, ref, k):
        if not kinds[n]:
            return ref[k]
        return jnp.concatenate([ref[o, :, k * HD : (k + 1) * HD] for o in range(olds)], axis=1)

    whose = jnp.concatenate([q_ref[:, total - STATS :].astype(f32)[:beams]] * QPK, axis=0)
    parents, limits, locals_ = [], [], []
    for kind, (_, _, lim_ref, _, _) in zip(kinds, caches):
        parent = whose.astype(jnp.int32) - (me ^ kind) * olds
        column = parent[:, :1]
        limit = jnp.zeros((rows, 1), jnp.int32)
        for o in range(olds):
            known = lim_ref[0:1, o : o + 1]
            limit = jnp.where(column == o, known, limit)
        parents.append(parent)
        limits.append(limit)
        locals_.append((column >= 0) & (column < olds))
    stats = [jnp.zeros((beams, STATS), f32) for _ in range(requests)]
    lane = lax.broadcasted_iota(jnp.int32, (beams, STATS), 1) % stride
    blank = jnp.zeros((rows, HD), bf16)
    kept = {}

    def scores(n, k):
        pk_ref, _, _, ck_ref, _ = caches[n]
        tiles = [q_ref[:, (k * QPK + i) * HD : (k * QPK + i + 1) * HD] for i in range(QPK)]
        q = [
            jnp.concatenate([x[t * beams : (t + 1) * beams] for x in tiles], axis=0)
            for t in range(requests)
        ]
        for u in range(pairs):
            both = jnp.concatenate(
                [
                    jnp.concatenate([q[2 * u], blank], axis=1),
                    jnp.concatenate([blank, q[2 * u + 1]], axis=1),
                ],
                axis=0,
            )
            s_ref[n, k, 2 * u * rows : 2 * (u + 1) * rows] = dot(both, prompt(n, pk_ref, k, u), 1, 1)
        chosen = jnp.concatenate(
            [jnp.where(parents[n] == o, q[-1], blank) for o in range(olds)], axis=1
        )
        cs_ref[n, k] = dot(chosen, private(n, ck_ref, k), 1, 1)

    def weigh(n, k):
        p, top, den = soft(s_ref[n, k])
        p_ref[n, k] = p.astype(bf16)
        place = lax.broadcasted_iota(jnp.int32, (rows, span), 1)
        c, ctop, cden = soft(jnp.where(place < limits[n], cs_ref[n, k], masked_score))
        cp_ref[n, k] = c.astype(bf16)
        kept[n, k] = (top, den, ctop, cden)

    def values(n, k):
        _, pv_ref, _, _, cv_ref = caches[n]
        tops, dens, ctop, cden = kept.pop((n, k))
        found = []
        for u in range(pairs):
            both = dot(
                p_ref[n, k, 2 * u * rows : 2 * (u + 1) * rows], prompt(n, pv_ref, k, u), 1, 0
            )
            for m, num in enumerate((both[:rows, :HD], both[rows:, HD:])):
                part = slice((2 * u + m) * rows, (2 * u + m + 1) * rows)
                found.append((num, tops[part], dens[part]))
        every = dot(cp_ref[n, k], private(n, cv_ref, k), 1, 0)
        cnum = every[:, :HD]
        for o in range(1, olds):
            cnum = jnp.where(parents[n] == o, every[:, o * HD : (o + 1) * HD], cnum)
        num, top, den = found[-1]
        both = jnp.where(locals_[n], jnp.maximum(top, ctop), top)
        a = jnp.exp(top - both)
        e = jnp.where(locals_[n], jnp.exp(jnp.where(locals_[n], ctop, both) - both), 0.0)
        found[-1] = (a * num + e * cnum, both, a * den + e * cden)
        return found

    def finish(k):
        found = [values(n, k) for n in range(len(kinds))]
        done = []
        for t in range(requests):
            num, top, den = found[0][t]
            for other in found[1:]:
                num2, top2, den2 = other[t]
                both = jnp.maximum(top, top2)
                a, e = jnp.exp(top - both), jnp.exp(top2 - both)
                num, top, den = a * num + e * num2, both, a * den + e * den2
            done.append(num * (1.0 / den))
            lse = top + jnp.log(den)
            for i in range(QPK):
                stats[t] = jnp.where(
                    lane == k * QPK + i,
                    jnp.broadcast_to(lse[i * beams : (i + 1) * beams], (beams, STATS)),
                    stats[t],
                )
        for i in range(QPK):
            store(
                slice((k * QPK + i) * HD, (k * QPK + i + 1) * HD),
                [x[i * beams : (i + 1) * beams] for x in done],
            )

    def store(cols, pieces):
        if len(outs) == 1:
            outs[0][:, cols] = jnp.concatenate(pieces, axis=0).astype(bf16)
        else:
            for n, piece in enumerate(pieces):
                outs[n // pairs][n % pairs, :, cols] = piece.astype(bf16)

    for stage in (scores, weigh):
        for n in range(len(kinds)):
            for k in range(heads):
                stage(n, k)
    for k in range(heads):
        finish(k)
    store(slice(total - STATS, total), [pack_stats(x, stride) for x in stats])


def pack_stats(x, stride):
    hi = x.astype(bf16).astype(f32)
    mid = (x - hi).astype(bf16).astype(f32)
    which = lax.broadcasted_iota(jnp.int32, x.shape, 1) // stride
    return jnp.where(which == 0, hi, jnp.where(which == 1, mid, x - hi - mid)).astype(bf16)


def read_stats(x, stride):
    x = x.astype(f32)
    return x + pltpu.roll(x, STATS - stride, 1) + pltpu.roll(x, STATS - 2 * stride, 1)


def merge(a, b, outs):
    total = a.shape[1]
    count = (total - STATS) // HD
    size = a.shape[0] // len(outs)

    def store(cols, value):
        for n, out in enumerate(outs):
            out[:, cols] = value[n * size : (n + 1) * size]

    la, lb = read_stats(a[:, total - STATS :], count), read_stats(b[:, total - STATS :], count)
    top = jnp.maximum(la, lb)
    wa, wb = jnp.exp(la - top), jnp.exp(lb - top)
    den = wa + wb
    wa = wa * (1.0 / den)
    wb = wb * (1.0 / den)
    for h in range(count):
        cols = slice(h * HD, (h + 1) * HD)
        store(
            cols,
            (
                wa[:, h : h + 1] * a[:, cols].astype(f32)
                + wb[:, h : h + 1] * b[:, cols].astype(f32)
            ).astype(bf16),
        )
    lse = top + jnp.log(den)
    lane = lax.broadcasted_iota(jnp.int32, lse.shape, 1)
    again = jnp.where(
        lane < count,
        lse,
        jnp.where(lane < 2 * count, pltpu.roll(lse, count, 1), pltpu.roll(lse, 2 * count, 1)),
    )
    store(slice(total - STATS, total), pack_stats(again, count))


def core_kernel(kept_ref, came_ref, *outs):
    merge(kept_ref, came_ref, [out.at[n] for out in outs for n in range(out.shape[0])])


def plane_kernel(kept_ref, came_ref, *outs):
    kept, came = (
        jnp.concatenate([x[n] for n in range(len(outs))], axis=0) for x in (kept_ref, came_ref)
    )
    merge(kept, came, outs)


def finish_kernel(q_ref, nk_ref, nv_ref, *refs):
    *parts, out_ref = refs
    beams, total = parts[0].shape
    heads = nv_ref.shape[1] // HD
    stride = heads * QPK
    lane = lax.broadcasted_iota(jnp.int32, (beams, STATS), 1)
    own = jnp.zeros((beams, STATS), f32)
    for h in range(stride):
        key = nk_ref[:, h // QPK * HD : (h // QPK + 1) * HD].astype(f32)
        s = jnp.sum(q_ref[:, h * HD : (h + 1) * HD].astype(f32) * key, axis=1, keepdims=True)
        own = jnp.where(lane == h, s * SCALE, own)
    lses = [read_stats(x[:, total - STATS :], stride) for x in parts]
    top = functools.reduce(jnp.maximum, lses, own)
    ws = [jnp.exp(x - top) for x in lses]
    w_own = jnp.exp(own - top)
    inv = 1.0 / functools.reduce(jnp.add, ws, w_own)
    ws = [w * inv for w in ws]
    w_own = w_own * inv
    for k in range(heads):
        value = nv_ref[:, k * HD : (k + 1) * HD].astype(f32)
        for i in range(QPK):
            h = k * QPK + i
            acc = w_own[:, h : h + 1] * value
            for w, x in zip(ws, parts):
                acc = acc + w[:, h : h + 1] * x[:, h * HD : (h + 1) * HD].astype(f32)
            out_ref[:, h * HD : (h + 1) * HD] = acc.astype(bf16)


def project_kernel(near_a, far_a, near_b, far_b, w_ref, keep_ref, send_ref, rows_ref):
    requests, group = rows_ref.shape[:2]
    me, side = lax.axis_index("beam"), lax.axis_index("head")
    mine, spot = me // group, me % group
    order = line_order(requests)
    order = order[-1:] + order[:1] + order[-2:0:-1]
    for first, refs in ((0, (near_a, far_a)), (requests // 2, (near_b, far_b))):
        for core, ref in enumerate(refs):
            for x in range(2):
                for n in range(requests // 2):
                    rows_ref[mine ^ order[first + n], spot ^ (2 * x + core)] = ref[x, n]
    a = jnp.concatenate(
        [rows_ref[z, j] for z in range(requests) for j in range(group)], axis=0
    )
    out = jnp.dot(a, w_ref[...], preferred_element_type=f32)
    half = requests * BEAM_WIDTH // 2

    @pl.when(side == 0)
    def _():
        keep_ref[...] = out[:half]
        send_ref[...] = out[half:].astype(bf16)

    @pl.when(side != 0)
    def _():
        keep_ref[...] = out[half:]
        send_ref[...] = out[:half].astype(bf16)


def whole_blocks(n, smem=(), far=()):
    places = [pltpu.SMEM if i in smem else pltpu.HBM if i in far else pltpu.VMEM for i in range(n)]
    return [pl.BlockSpec(memory_space=place) for place in places]


def call(kernel, name, out_shape, *args, smem=(), far=(), scratch=(), vmem=8, cost=None):
    many = isinstance(out_shape, tuple)
    return pl.pallas_call(
        kernel,
        out_shape=out_shape,
        in_specs=whole_blocks(len(args), smem, far),
        out_specs=tuple(whole_blocks(len(out_shape))) if many else whole_blocks(1)[0],
        scratch_shapes=list(scratch),
        compiler_params=pltpu.CompilerParams(vmem_limit_bytes=vmem * 1024 * 1024),
        cost_estimate=cost and pl.CostEstimate(flops=cost, bytes_accessed=cost, transcendentals=0),
        name=name,
    )(*(pltpu.with_memory_space_constraint(x, pltpu.HBM) if i in far else x for i, x in enumerate(args)))


def per_device(
    queries,
    new_keys,
    new_values,
    prompt_keys,
    prompt_values,
    private_keys,
    private_values,
    parents,
    block_counts,
    out_weight,
):
    beams, width = queries.shape
    group = BEAM_WIDTH // beams
    assert group == 4
    devices = lax.axis_size("beam")
    requests = prompt_keys.shape[0]
    sides = lax.axis_size("head")
    total = width + STATS

    def swap(x, with_bit):
        return lax.ppermute(x, "beam", [(i, i ^ with_bit) for i in range(devices)])

    rows = requests * beams
    heads = width // (QPK * HD)
    length, span = prompt_keys.shape[1], private_keys.shape[1]
    line = jax.ShapeDtypeStruct((rows, total), bf16)
    order = line_order(requests)
    others = order[:-1]
    came = [swap(queries, t * group) for t in others]
    prompt = jax.ShapeDtypeStruct((heads, requests // 2, length, 2 * HD), bf16)
    private = jax.ShapeDtypeStruct((heads, span, beams * HD), bf16)
    stored = (swap(private_keys, 1), swap(private_values, 1))
    own, parent_tail, *olds = call(
        load_private_kernel,
        "load_private",
        (
            jax.ShapeDtypeStruct((beams, width), bf16),
            jax.ShapeDtypeStruct((beams, STATS), bf16),
            jax.ShapeDtypeStruct((8, STATS), jnp.int32),
            private,
            private,
        ),
        queries,
        parents,
        block_counts,
        private_keys,
        private_values,
        far=(0, 1, 2, 3, 4),
        scratch=[
            pltpu.SMEM((beams,), jnp.int32),
            pltpu.SMEM((beams,), jnp.int32),
            pltpu.SemaphoreType.DMA((3,)),
            pltpu.SemaphoreType.DMA((2, heads, beams)),
        ],
        vmem=10,
        cost=2**26,
    )
    *came, parent_tail = lax.optimization_barrier((*came, parent_tail))
    asked = call(line_kernel, "line", line, parent_tail, *came, own)
    prompt_keys, prompt_values, _ = lax.optimization_barrier((prompt_keys, prompt_values, asked))
    prompts = call(
        functools.partial(load_prompt_kernel, group),
        "load_prompt",
        (prompt, prompt),
        prompt_keys,
        prompt_values,
        far=(0, 1),
        scratch=[pltpu.SemaphoreType.DMA((2, heads, requests))],
        vmem=10,
        cost=2**26,
    )
    caches = (*prompts, *olds)
    limits, late_keys, late_values = lax.optimization_barrier(
        (swap(olds[0], 1), prompt_keys, prompt_values)
    )
    stored = (swap(late_keys, 1), swap(late_values, 1), limits, *stored)

    many = beams * QPK

    def attend(asked, name, out_shape, kinds, *caches):
        return call(
            functools.partial(attend_kernel, kinds),
            name,
            out_shape,
            asked,
            *caches,
            scratch=[
                pltpu.VMEM((len(kinds), heads, requests * many, length), f32),
                pltpu.VMEM((len(kinds), heads, requests * many, length), bf16),
                pltpu.VMEM((len(kinds), heads, many, span), f32),
                pltpu.VMEM((len(kinds), heads, many, span), bf16),
            ],
            vmem=24,
            cost=2**26,
        )

    other = swap(asked, 2)
    own_here = attend(asked, "attend_own", line, (0,), *caches)
    other, own_here = lax.optimization_barrier((other, own_here))
    half = jax.ShapeDtypeStruct((requests // 2, beams, total), bf16)
    send_a, send_b = attend(other, "attend_side", (half, half), (0, 1), *caches, *stored)
    asked, _ = lax.optimization_barrier((asked, send_a))
    own_there = attend(asked, "attend_own_other", line, (1,), *stored)
    keep_a, keep_b = call(core_kernel, "own_merge", (half, half), own_here, own_there)
    piece = jax.ShapeDtypeStruct((beams, total), bf16)
    parts = []
    for keep, send in ((keep_a, send_a), (keep_b, send_b)):
        parts += call(
            plane_kernel, "plane_merge", (piece,) * (requests // 2), keep, swap(send, 2)
        )
    parts = [swap(x, t * group) if t else x for t, x in zip(order, parts)]
    attended = call(
        finish_kernel,
        "finish",
        jax.ShapeDtypeStruct((beams, width), bf16),
        own,
        new_keys,
        new_values,
        *parts,
    )
    if sides == 2:
        line = [attended] + [swap(attended, t * group) for t in others[:1] + others[:0:-1]]
        halves = []
        for pieces in (line[: requests // 2], line[requests // 2 :]):
            near = jnp.stack(pieces)
            near = jnp.stack([near, swap(near, 2)])
            halves += [near, swap(near, 1)]
        shape = (requests * BEAM_WIDTH // 2, out_weight.shape[1])
        keep, send = call(
            project_kernel,
            "project",
            (jax.ShapeDtypeStruct(shape, f32), jax.ShapeDtypeStruct(shape, bf16)),
            *halves,
            out_weight,
            scratch=[pltpu.VMEM((requests, group, beams, width), bf16)],
            vmem=16,
        )
        came = lax.ppermute(send, "head", [(0, 1), (1, 0)])
        return (keep + came.astype(f32)).astype(bf16)
    rows = lax.all_gather(attended, "beam", axis=0, tiled=True)
    products = jnp.dot(rows, out_weight, preferred_element_type=f32)
    return lax.psum_scatter(products, "head", scatter_dimension=0, tiled=True).astype(bf16)


def solution(mesh):
    placed = (
        P("beam", "head"),
        P("beam", "head"),
        P("beam", "head"),
        P(None, "beam", "head"),
        P(None, "beam", "head"),
        P("beam", None, "head"),
        P("beam", None, "head"),
        P("beam"),
        P("beam"),
        P("head", "beam"),
    )
    return jax.shard_map(
        per_device, mesh=mesh, in_specs=placed, out_specs=P("head", "beam"), check_vma=False
    )
```

```python
import functools
import math

import jax
import jax.numpy as jnp
from jax import lax
from jax.experimental import pallas as pl
from jax.experimental.pallas import tpu as pltpu
from jax.sharding import PartitionSpec as P

HD = 128
QPK = 8
BEAM_WIDTH = 16
BLOCK_LEN = 128
STATS = 128
SCALE = 1.0 / math.sqrt(HD)
LOG2E = math.log2(math.e)

masked_score = -1e30
f32, bf16 = jnp.float32, jnp.bfloat16


def dot(a, b, ca, cb):
    return lax.dot_general(a, b, (((ca,), (cb,)), ((), ())), preferred_element_type=f32)


def soft(scores):
    top = jnp.max(scores, axis=1, keepdims=True)
    weights = jnp.exp2((scores - top) * (SCALE * LOG2E))
    return weights, top * SCALE, jnp.sum(weights, axis=1, keepdims=True)


def line_order(requests):
    return list(range(requests))[::-1]


def line_kernel(tail_ref, *refs):
    *pieces, out_ref = refs
    width = pieces[0].shape[1]
    out_ref[:, :width] = jnp.concatenate([x[...] for x in pieces], axis=0)
    out_ref[:, width:] = jnp.concatenate([tail_ref[...]] * len(pieces), axis=0)


def load_private_kernel(
    q_hbm, par_hbm, cnt_hbm, ck_hbm, cv_hbm,
    q_ref, tail_ref, lim_ref, ck_ref, cv_ref, par_ref, cnt_ref, sems, old_sems,
):
    olds = ck_hbm.shape[0]
    copies = [
        pltpu.make_async_copy(src, dst, sems.at[n])
        for n, (src, dst) in enumerate(((q_hbm, q_ref), (par_hbm, par_ref), (cnt_hbm, cnt_ref)))
    ] + [
        pltpu.make_async_copy(src.at[o], dst.at[o], old_sems.at[n, o])
        for n, (src, dst) in enumerate(((ck_hbm, ck_ref), (cv_hbm, cv_ref)))
        for o in range(olds)
    ]
    for x in copies:
        x.start()
    for x in copies[:3]:
        x.wait()
    row = lax.broadcasted_iota(jnp.int32, tail_ref.shape, 0)
    parent = jnp.zeros(row.shape, jnp.int32)
    for b in range(tail_ref.shape[0]):
        parent = jnp.where(row == b, par_ref[b], parent)
    tail_ref[...] = parent.astype(f32).astype(bf16)
    lane = lax.broadcasted_iota(jnp.int32, lim_ref.shape, 1)
    limit = jnp.zeros(lim_ref.shape, jnp.int32)
    for o in range(olds):
        limit = jnp.where(lane == o, cnt_ref[o] * BLOCK_LEN, limit)
    lim_ref[...] = limit
    for x in copies[3:]:
        x.wait()


def load_prompt_kernel(pk_hbm, pv_hbm, pk_ref, pv_ref, sems):
    copies = [
        pltpu.make_async_copy(src.at[r], dst.at[r], sems.at[n, r])
        for n, (src, dst) in enumerate(((pk_hbm, pk_ref), (pv_hbm, pv_ref)))
        for r in range(pk_ref.shape[0])
    ]
    for x in copies:
        x.start()
    for x in copies:
        x.wait()


def attend_kernel(kinds, q_ref, *refs):
    total = q_ref.shape[1]
    heads = (total - STATS) // (QPK * HD)
    caches = [refs[5 * n : 5 * n + 5] for n in range(len(kinds))]
    *outs, s_ref, p_ref, cs_ref, cp_ref = refs[5 * len(kinds) :]
    requests, span = s_ref.shape[2] // cs_ref.shape[2], cs_ref.shape[3]
    pairs = requests // 2
    beams = q_ref.shape[0] // requests
    stride = heads * QPK
    rows = QPK * beams
    me = lax.axis_index("beam")
    mine = me // (BEAM_WIDTH // beams)
    order = line_order(requests)
    olds = beams

    def prompt(ref, k, u):
        both = [ref[mine ^ order[2 * u + m], :, k * HD : (k + 1) * HD] for m in range(2)]
        return jnp.concatenate(both, axis=1)

    def private(ref, k):
        return jnp.concatenate([ref[o, :, k * HD : (k + 1) * HD] for o in range(olds)], axis=1)

    whose = jnp.concatenate([q_ref[:, total - STATS :].astype(f32)[:beams]] * QPK, axis=0)
    parents, limits, locals_ = [], [], []
    for kind, (_, _, lim_ref, _, _) in zip(kinds, caches):
        parent = whose.astype(jnp.int32) - (me ^ kind) * olds
        column = parent[:, :1]
        limit = jnp.zeros((rows, 1), jnp.int32)
        for o in range(olds):
            known = lim_ref[0:1, o : o + 1]
            limit = jnp.where(column == o, known, limit)
        parents.append(parent)
        limits.append(limit)
        locals_.append((column >= 0) & (column < olds))
    stats = [jnp.zeros((beams, STATS), f32) for _ in range(requests)]
    lane = lax.broadcasted_iota(jnp.int32, (beams, STATS), 1) % stride
    blank = jnp.zeros((rows, HD), bf16)
    kept = {}

    def scores(n, k):
        pk_ref, _, _, ck_ref, _ = caches[n]
        tiles = [q_ref[:, (k * QPK + i) * HD : (k * QPK + i + 1) * HD] for i in range(QPK)]
        q = [
            jnp.concatenate([x[t * beams : (t + 1) * beams] for x in tiles], axis=0)
            for t in range(requests)
        ]
        for u in range(pairs):
            both = jnp.concatenate(
                [
                    jnp.concatenate([q[2 * u], blank], axis=1),
                    jnp.concatenate([blank, q[2 * u + 1]], axis=1),
                ],
                axis=0,
            )
            s_ref[n, k, 2 * u * rows : 2 * (u + 1) * rows] = dot(both, prompt(pk_ref, k, u), 1, 1)
        chosen = jnp.concatenate(
            [jnp.where(parents[n] == o, q[-1], blank) for o in range(olds)], axis=1
        )
        cs_ref[n, k] = dot(chosen, private(ck_ref, k), 1, 1)

    def weigh(n, k):
        p, top, den = soft(s_ref[n, k])
        p_ref[n, k] = p.astype(bf16)
        place = lax.broadcasted_iota(jnp.int32, (rows, span), 1)
        c, ctop, cden = soft(jnp.where(place < limits[n], cs_ref[n, k], masked_score))
        cp_ref[n, k] = c.astype(bf16)
        kept[n, k] = (top, den, ctop, cden)

    def values(n, k):
        _, pv_ref, _, _, cv_ref = caches[n]
        tops, dens, ctop, cden = kept.pop((n, k))
        found = []
        for u in range(pairs):
            both = dot(
                p_ref[n, k, 2 * u * rows : 2 * (u + 1) * rows], prompt(pv_ref, k, u), 1, 0
            )
            for m, num in enumerate((both[:rows, :HD], both[rows:, HD:])):
                part = slice((2 * u + m) * rows, (2 * u + m + 1) * rows)
                found.append((num, tops[part], dens[part]))
        every = dot(cp_ref[n, k], private(cv_ref, k), 1, 0)
        cnum = every[:, :HD]
        for o in range(1, olds):
            cnum = jnp.where(parents[n] == o, every[:, o * HD : (o + 1) * HD], cnum)
        num, top, den = found[-1]
        both = jnp.where(locals_[n], jnp.maximum(top, ctop), top)
        a = jnp.exp(top - both)
        e = jnp.where(locals_[n], jnp.exp(jnp.where(locals_[n], ctop, both) - both), 0.0)
        found[-1] = (a * num + e * cnum, both, a * den + e * cden)
        return found

    def finish(k):
        found = [values(n, k) for n in range(len(kinds))]
        done = []
        for t in range(requests):
            num, top, den = found[0][t]
            for other in found[1:]:
                num2, top2, den2 = other[t]
                both = jnp.maximum(top, top2)
                a, e = jnp.exp(top - both), jnp.exp(top2 - both)
                num, top, den = a * num + e * num2, both, a * den + e * den2
            done.append(num * (1.0 / den))
            lse = top + jnp.log(den)
            for i in range(QPK):
                stats[t] = jnp.where(
                    lane == k * QPK + i,
                    jnp.broadcast_to(lse[i * beams : (i + 1) * beams], (beams, STATS)),
                    stats[t],
                )
        for i in range(QPK):
            store(
                slice((k * QPK + i) * HD, (k * QPK + i + 1) * HD),
                [x[i * beams : (i + 1) * beams] for x in done],
            )

    def store(cols, pieces):
        if len(outs) == 1:
            outs[0][:, cols] = jnp.concatenate(pieces, axis=0).astype(bf16)
        else:
            for n, piece in enumerate(pieces):
                outs[n // pairs][n % pairs, :, cols] = piece.astype(bf16)

    for stage in (scores, weigh):
        for n in range(len(kinds)):
            for k in range(heads):
                stage(n, k)
    for k in range(heads):
        finish(k)
    store(slice(total - STATS, total), [pack_stats(x, stride) for x in stats])


def pack_stats(x, stride):
    hi = x.astype(bf16).astype(f32)
    mid = (x - hi).astype(bf16).astype(f32)
    which = lax.broadcasted_iota(jnp.int32, x.shape, 1) // stride
    return jnp.where(which == 0, hi, jnp.where(which == 1, mid, x - hi - mid)).astype(bf16)


def read_stats(x, stride):
    x = x.astype(f32)
    return x + pltpu.roll(x, STATS - stride, 1) + pltpu.roll(x, STATS - 2 * stride, 1)


def merge(a, b, outs):
    total = a.shape[1]
    count = (total - STATS) // HD
    size = a.shape[0] // len(outs)

    def store(cols, value):
        for n, out in enumerate(outs):
            out[:, cols] = value[n * size : (n + 1) * size]

    la, lb = read_stats(a[:, total - STATS :], count), read_stats(b[:, total - STATS :], count)
    top = jnp.maximum(la, lb)
    wa, wb = jnp.exp(la - top), jnp.exp(lb - top)
    den = wa + wb
    wa = wa * (1.0 / den)
    wb = wb * (1.0 / den)
    for h in range(count):
        cols = slice(h * HD, (h + 1) * HD)
        store(
            cols,
            (
                wa[:, h : h + 1] * a[:, cols].astype(f32)
                + wb[:, h : h + 1] * b[:, cols].astype(f32)
            ).astype(bf16),
        )
    lse = top + jnp.log(den)
    lane = lax.broadcasted_iota(jnp.int32, lse.shape, 1)
    again = jnp.where(
        lane < count,
        lse,
        jnp.where(lane < 2 * count, pltpu.roll(lse, count, 1), pltpu.roll(lse, 2 * count, 1)),
    )
    store(slice(total - STATS, total), pack_stats(again, count))


def core_kernel(kept_ref, came_ref, *outs):
    merge(kept_ref, came_ref, [out.at[n] for out in outs for n in range(out.shape[0])])


def plane_kernel(kept_ref, came_ref, *outs):
    kept, came = (
        jnp.concatenate([x[n] for n in range(len(outs))], axis=0) for x in (kept_ref, came_ref)
    )
    merge(kept, came, outs)


def finish_kernel(q_ref, nk_ref, nv_ref, *refs):
    *parts, out_ref = refs
    beams, total = parts[0].shape
    heads = nv_ref.shape[1] // HD
    stride = heads * QPK
    lane = lax.broadcasted_iota(jnp.int32, (beams, STATS), 1)
    own = jnp.zeros((beams, STATS), f32)
    for h in range(stride):
        key = nk_ref[:, h // QPK * HD : (h // QPK + 1) * HD].astype(f32)
        s = jnp.sum(q_ref[:, h * HD : (h + 1) * HD].astype(f32) * key, axis=1, keepdims=True)
        own = jnp.where(lane == h, s * SCALE, own)
    lses = [read_stats(x[:, total - STATS :], stride) for x in parts]
    top = functools.reduce(jnp.maximum, lses, own)
    ws = [jnp.exp(x - top) for x in lses]
    w_own = jnp.exp(own - top)
    inv = 1.0 / functools.reduce(jnp.add, ws, w_own)
    ws = [w * inv for w in ws]
    w_own = w_own * inv
    for k in range(heads):
        value = nv_ref[:, k * HD : (k + 1) * HD].astype(f32)
        for i in range(QPK):
            h = k * QPK + i
            acc = w_own[:, h : h + 1] * value
            for w, x in zip(ws, parts):
                acc = acc + w[:, h : h + 1] * x[:, h * HD : (h + 1) * HD].astype(f32)
            out_ref[:, h * HD : (h + 1) * HD] = acc.astype(bf16)


def project_kernel(near_a, far_a, near_b, far_b, w_ref, keep_ref, send_ref, rows_ref):
    requests, group = rows_ref.shape[:2]
    me, side = lax.axis_index("beam"), lax.axis_index("head")
    mine, spot = me // group, me % group
    order = line_order(requests)
    order = order[-1:] + order[:1] + order[-2:0:-1]
    for first, refs in ((0, (near_a, far_a)), (requests // 2, (near_b, far_b))):
        for core, ref in enumerate(refs):
            for x in range(2):
                for n in range(requests // 2):
                    rows_ref[mine ^ order[first + n], spot ^ (2 * x + core)] = ref[x, n]
    a = jnp.concatenate(
        [rows_ref[z, j] for z in range(requests) for j in range(group)], axis=0
    )
    out = jnp.dot(a, w_ref[...], preferred_element_type=f32)
    half = requests * BEAM_WIDTH // 2

    @pl.when(side == 0)
    def _():
        keep_ref[...] = out[:half]
        send_ref[...] = out[half:].astype(bf16)

    @pl.when(side != 0)
    def _():
        keep_ref[...] = out[half:]
        send_ref[...] = out[:half].astype(bf16)


def whole_blocks(n, smem=(), far=()):
    places = [pltpu.SMEM if i in smem else pltpu.HBM if i in far else pltpu.VMEM for i in range(n)]
    return [pl.BlockSpec(memory_space=place) for place in places]


def call(kernel, name, out_shape, *args, smem=(), far=(), scratch=(), vmem=8, cost=None):
    many = isinstance(out_shape, tuple)
    return pl.pallas_call(
        kernel,
        out_shape=out_shape,
        in_specs=whole_blocks(len(args), smem, far),
        out_specs=tuple(whole_blocks(len(out_shape))) if many else whole_blocks(1)[0],
        scratch_shapes=list(scratch),
        compiler_params=pltpu.CompilerParams(vmem_limit_bytes=vmem * 1024 * 1024),
        cost_estimate=cost and pl.CostEstimate(flops=cost, bytes_accessed=cost, transcendentals=0),
        name=name,
    )(*(pltpu.with_memory_space_constraint(x, pltpu.HBM) if i in far else x for i, x in enumerate(args)))


def per_device(
    queries,
    new_keys,
    new_values,
    prompt_keys,
    prompt_values,
    private_keys,
    private_values,
    parents,
    block_counts,
    out_weight,
):
    beams, width = queries.shape
    group = BEAM_WIDTH // beams
    assert group == 4
    devices = lax.axis_size("beam")
    requests = prompt_keys.shape[0]
    sides = lax.axis_size("head")
    total = width + STATS

    def swap(x, with_bit):
        return lax.ppermute(x, "beam", [(i, i ^ with_bit) for i in range(devices)])

    rows = requests * beams
    heads = width // (QPK * HD)
    length, span = prompt_keys.shape[1], private_keys.shape[1]
    line = jax.ShapeDtypeStruct((rows, total), bf16)
    order = line_order(requests)
    others = order[:-1]
    came = [swap(queries, t * group) for t in others]
    prompt = jax.ShapeDtypeStruct(prompt_keys.shape, bf16)
    private = jax.ShapeDtypeStruct(private_keys.shape, bf16)
    stored = (swap(private_keys, 1), swap(private_values, 1))
    own, parent_tail, *olds = call(
        load_private_kernel,
        "load_private",
        (
            jax.ShapeDtypeStruct((beams, width), bf16),
            jax.ShapeDtypeStruct((beams, STATS), bf16),
            jax.ShapeDtypeStruct((8, STATS), jnp.int32),
            private,
            private,
        ),
        queries,
        parents,
        block_counts,
        private_keys,
        private_values,
        far=(0, 1, 2, 3, 4),
        scratch=[
            pltpu.SMEM((beams,), jnp.int32),
            pltpu.SMEM((beams,), jnp.int32),
            pltpu.SemaphoreType.DMA((3,)),
            pltpu.SemaphoreType.DMA((2, beams)),
        ],
        vmem=10,
        cost=2**26,
    )
    *came, parent_tail = lax.optimization_barrier((*came, parent_tail))
    asked = call(line_kernel, "line", line, parent_tail, *came, own)
    prompt_keys, prompt_values, _ = lax.optimization_barrier((prompt_keys, prompt_values, asked))
    prompts = call(
        load_prompt_kernel,
        "load_prompt",
        (prompt, prompt),
        prompt_keys,
        prompt_values,
        far=(0, 1),
        scratch=[pltpu.SemaphoreType.DMA((2, requests))],
        vmem=10,
        cost=2**26,
    )
    caches = (*prompts, *olds)
    limits, late_keys, late_values = lax.optimization_barrier(
        (swap(olds[0], 1), prompt_keys, prompt_values)
    )
    stored = (swap(late_keys, 1), swap(late_values, 1), limits, *stored)

    many = beams * QPK

    def attend(asked, name, out_shape, kinds, *caches):
        return call(
            functools.partial(attend_kernel, kinds),
            name,
            out_shape,
            asked,
            *caches,
            scratch=[
                pltpu.VMEM((len(kinds), heads, requests * many, length), f32),
                pltpu.VMEM((len(kinds), heads, requests * many, length), bf16),
                pltpu.VMEM((len(kinds), heads, many, span), f32),
                pltpu.VMEM((len(kinds), heads, many, span), bf16),
            ],
            vmem=24,
            cost=2**26,
        )

    other = swap(asked, 2)
    own_here = attend(asked, "attend_own", line, (0,), *caches)
    other, own_here = lax.optimization_barrier((other, own_here))
    half = jax.ShapeDtypeStruct((requests // 2, beams, total), bf16)
    send_a, send_b = attend(other, "attend_side", (half, half), (0, 1), *caches, *stored)
    asked, _ = lax.optimization_barrier((asked, send_a))
    own_there = attend(asked, "attend_own_other", line, (1,), *stored)
    keep_a, keep_b = call(core_kernel, "own_merge", (half, half), own_here, own_there)
    piece = jax.ShapeDtypeStruct((beams, total), bf16)
    parts = []
    for keep, send in ((keep_a, send_a), (keep_b, send_b)):
        parts += call(
            plane_kernel, "plane_merge", (piece,) * (requests // 2), keep, swap(send, 2)
        )
    parts = [swap(x, t * group) if t else x for t, x in zip(order, parts)]
    attended = call(
        finish_kernel,
        "finish",
        jax.ShapeDtypeStruct((beams, width), bf16),
        own,
        new_keys,
        new_values,
        *parts,
    )
    if sides == 2:
        line = [attended] + [swap(attended, t * group) for t in others[:1] + others[:0:-1]]
        halves = []
        for pieces in (line[: requests // 2], line[requests // 2 :]):
            near = jnp.stack(pieces)
            near = jnp.stack([near, swap(near, 2)])
            halves += [near, swap(near, 1)]
        shape = (requests * BEAM_WIDTH // 2, out_weight.shape[1])
        keep, send = call(
            project_kernel,
            "project",
            (jax.ShapeDtypeStruct(shape, f32), jax.ShapeDtypeStruct(shape, bf16)),
            *halves,
            out_weight,
            scratch=[pltpu.VMEM((requests, group, beams, width), bf16)],
            vmem=16,
        )
        came = lax.ppermute(send, "head", [(0, 1), (1, 0)])
        return (keep + came.astype(f32)).astype(bf16)
    rows = lax.all_gather(attended, "beam", axis=0, tiled=True)
    products = jnp.dot(rows, out_weight, preferred_element_type=f32)
    return lax.psum_scatter(products, "head", scatter_dimension=0, tiled=True).astype(bf16)


def solution(mesh):
    placed = (
        P("beam", "head"),
        P("beam", "head"),
        P("beam", "head"),
        P(None, "beam", "head"),
        P(None, "beam", "head"),
        P("beam", None, "head"),
        P("beam", None, "head"),
        P("beam"),
        P("beam"),
        P("head", "beam"),
    )
    return jax.shard_map(
        per_device, mesh=mesh, in_specs=placed, out_specs=P("head", "beam"), check_vma=False
    )
```

```python
import functools
import math

import jax
import jax.numpy as jnp
from jax import lax
from jax.experimental import pallas as pl
from jax.experimental.pallas import tpu as pltpu
from jax.sharding import PartitionSpec as P

HD = 128
QPK = 8
BEAM_WIDTH = 16
BLOCK_LEN = 128
STATS = 128
SCALE = 1.0 / math.sqrt(HD)
LOG2E = math.log2(math.e)

masked_score = -1e30
f32, bf16 = jnp.float32, jnp.bfloat16


def dot(a, b, ca, cb):
    return lax.dot_general(a, b, (((ca,), (cb,)), ((), ())), preferred_element_type=f32)


def soft(scores):
    top = jnp.max(scores, axis=1, keepdims=True)
    weights = jnp.exp2((scores - top) * (SCALE * LOG2E))
    return weights, top * SCALE, jnp.sum(weights, axis=1, keepdims=True)


def line_order(requests):
    return list(range(requests))[::-1]


def line_kernel(tail_ref, *refs):
    *pieces, out_ref = refs
    width = pieces[0].shape[1]
    out_ref[:, :width] = jnp.concatenate([x[...] for x in pieces], axis=0)
    out_ref[:, width:] = jnp.concatenate([tail_ref[...]] * len(pieces), axis=0)


def load_private_kernel(
    q_hbm, par_hbm, cnt_hbm, ck_hbm, cv_hbm,
    q_ref, tail_ref, lim_ref, ck_ref, cv_ref, par_ref, cnt_ref, sems, old_sems,
):
    olds = ck_hbm.shape[0]
    copies = [
        pltpu.make_async_copy(src, dst, sems.at[n])
        for n, (src, dst) in enumerate(((q_hbm, q_ref), (par_hbm, par_ref), (cnt_hbm, cnt_ref)))
    ] + [
        pltpu.make_async_copy(src.at[o], dst.at[o], old_sems.at[n, o])
        for n, (src, dst) in enumerate(((ck_hbm, ck_ref), (cv_hbm, cv_ref)))
        for o in range(olds)
    ]
    for x in copies:
        x.start()
    for x in copies[:3]:
        x.wait()
    row = lax.broadcasted_iota(jnp.int32, tail_ref.shape, 0)
    parent = jnp.zeros(row.shape, jnp.int32)
    for b in range(tail_ref.shape[0]):
        parent = jnp.where(row == b, par_ref[b], parent)
    tail_ref[...] = parent.astype(f32).astype(bf16)
    lane = lax.broadcasted_iota(jnp.int32, lim_ref.shape, 1)
    limit = jnp.zeros(lim_ref.shape, jnp.int32)
    for o in range(olds):
        limit = jnp.where(lane == o, cnt_ref[o] * BLOCK_LEN, limit)
    lim_ref[...] = limit
    for x in copies[3:]:
        x.wait()


def load_prompt_kernel(pk_hbm, pv_hbm, pk_ref, pv_ref, sems):
    copies = [
        pltpu.make_async_copy(src.at[r], dst.at[r], sems.at[n, r])
        for n, (src, dst) in enumerate(((pk_hbm, pk_ref), (pv_hbm, pv_ref)))
        for r in range(pk_ref.shape[0])
    ]
    for x in copies:
        x.start()
    for x in copies:
        x.wait()


def attend_kernel(kinds, q_ref, *refs):
    total = q_ref.shape[1]
    heads = (total - STATS) // (QPK * HD)
    caches = [refs[5 * n : 5 * n + 5] for n in range(len(kinds))]
    *outs, s_ref, p_ref, cs_ref, cp_ref = refs[5 * len(kinds) :]
    requests, span = s_ref.shape[2] // cs_ref.shape[2], cs_ref.shape[3]
    pairs = requests // 2
    beams = q_ref.shape[0] // requests
    stride = heads * QPK
    rows = QPK * beams
    me = lax.axis_index("beam")
    mine = me // (BEAM_WIDTH // beams)
    order = line_order(requests)
    olds = beams

    def prompt(ref, k, u):
        both = [ref[mine ^ order[2 * u + m], :, k * HD : (k + 1) * HD] for m in range(2)]
        return jnp.concatenate(both, axis=1)

    def private(ref, k):
        return jnp.concatenate([ref[o, :, k * HD : (k + 1) * HD] for o in range(olds)], axis=1)

    whose = jnp.concatenate([q_ref[:, total - STATS :].astype(f32)[:beams]] * QPK, axis=0)
    parents, limits, locals_ = [], [], []
    for kind, (_, _, lim_ref, _, _) in zip(kinds, caches):
        parent = whose.astype(jnp.int32) - (me ^ kind) * olds
        column = parent[:, :1]
        limit = jnp.zeros((rows, 1), jnp.int32)
        for o in range(olds):
            known = lim_ref[0:1, o : o + 1]
            limit = jnp.where(column == o, known, limit)
        parents.append(parent)
        limits.append(limit)
        locals_.append((column >= 0) & (column < olds))
    stats = [jnp.zeros((beams, STATS), f32) for _ in range(requests)]
    lane = lax.broadcasted_iota(jnp.int32, (beams, STATS), 1) % stride
    blank = jnp.zeros((rows, HD), bf16)
    kept = {}

    def scores(n, k):
        pk_ref, _, _, ck_ref, _ = caches[n]
        tiles = [q_ref[:, (k * QPK + i) * HD : (k * QPK + i + 1) * HD] for i in range(QPK)]
        q = [
            jnp.concatenate([x[t * beams : (t + 1) * beams] for x in tiles], axis=0)
            for t in range(requests)
        ]
        for u in range(pairs):
            both = jnp.concatenate(
                [
                    jnp.concatenate([q[2 * u], blank], axis=1),
                    jnp.concatenate([blank, q[2 * u + 1]], axis=1),
                ],
                axis=0,
            )
            s_ref[n, k, 2 * u * rows : 2 * (u + 1) * rows] = dot(both, prompt(pk_ref, k, u), 1, 1)
        chosen = jnp.concatenate(
            [jnp.where(parents[n] == o, q[-1], blank) for o in range(olds)], axis=1
        )
        cs_ref[n, k] = dot(chosen, private(ck_ref, k), 1, 1)

    def weigh(n, k):
        p, top, den = soft(s_ref[n, k])
        p_ref[n, k] = p.astype(bf16)
        place = lax.broadcasted_iota(jnp.int32, (rows, span), 1)
        c, ctop, cden = soft(jnp.where(place < limits[n], cs_ref[n, k], masked_score))
        cp_ref[n, k] = c.astype(bf16)
        kept[n, k] = (top, den, ctop, cden)

    def values(n, k):
        _, pv_ref, _, _, cv_ref = caches[n]
        tops, dens, ctop, cden = kept.pop((n, k))
        found = []
        for u in range(pairs):
            both = dot(
                p_ref[n, k, 2 * u * rows : 2 * (u + 1) * rows], prompt(pv_ref, k, u), 1, 0
            )
            for m, num in enumerate((both[:rows, :HD], both[rows:, HD:])):
                part = slice((2 * u + m) * rows, (2 * u + m + 1) * rows)
                found.append((num, tops[part], dens[part]))
        every = dot(cp_ref[n, k], private(cv_ref, k), 1, 0)
        cnum = every[:, :HD]
        for o in range(1, olds):
            cnum = jnp.where(parents[n] == o, every[:, o * HD : (o + 1) * HD], cnum)
        num, top, den = found[-1]
        both = jnp.where(locals_[n], jnp.maximum(top, ctop), top)
        a = jnp.exp(top - both)
        e = jnp.where(locals_[n], jnp.exp(jnp.where(locals_[n], ctop, both) - both), 0.0)
        found[-1] = (a * num + e * cnum, both, a * den + e * cden)
        return found

    def finish(k):
        found = [values(n, k) for n in range(len(kinds))]
        done = []
        for t in range(requests):
            num, top, den = found[0][t]
            for other in found[1:]:
                num2, top2, den2 = other[t]
                both = jnp.maximum(top, top2)
                a, e = jnp.exp(top - both), jnp.exp(top2 - both)
                num, top, den = a * num + e * num2, both, a * den + e * den2
            done.append(num * (1.0 / den))
            lse = top + jnp.log(den)
            for i in range(QPK):
                stats[t] = jnp.where(
                    lane == k * QPK + i,
                    jnp.broadcast_to(lse[i * beams : (i + 1) * beams], (beams, STATS)),
                    stats[t],
                )
        for i in range(QPK):
            store(
                slice((k * QPK + i) * HD, (k * QPK + i + 1) * HD),
                [x[i * beams : (i + 1) * beams] for x in done],
            )

    def store(cols, pieces):
        if len(outs) == 1:
            outs[0][:, cols] = jnp.concatenate(pieces, axis=0).astype(bf16)
        else:
            for n, piece in enumerate(pieces):
                outs[n // pairs][n % pairs, :, cols] = piece.astype(bf16)

    for stage in (scores, weigh):
        for n in range(len(kinds)):
            for k in range(heads):
                stage(n, k)
    for k in range(heads):
        finish(k)
    store(slice(total - STATS, total), [pack_stats(x, stride) for x in stats])


def side_kernel(q_ref, own_ref, *refs):
    caches, (a_ref, b_ref, early_ref), scratch = refs[:10], refs[10:13], refs[13:]
    attend_kernel((0, 1), q_ref, *caches, a_ref, b_ref, *scratch)

    @pl.when(lax.axis_index("beam") % 2 == 1)
    def _():
        attend_kernel((1,), own_ref, *caches[5:], early_ref, *scratch)


def late_kernel(q_ref, early_ref, *refs):
    out_ref = refs[5]
    core = lax.axis_index("beam") % 2

    @pl.when(core == 0)
    def _():
        attend_kernel((1,), q_ref, *refs)

    @pl.when(core == 1)
    def _():
        out_ref[...] = early_ref[...]


def pack_stats(x, stride):
    hi = x.astype(bf16).astype(f32)
    mid = (x - hi).astype(bf16).astype(f32)
    which = lax.broadcasted_iota(jnp.int32, x.shape, 1) // stride
    return jnp.where(which == 0, hi, jnp.where(which == 1, mid, x - hi - mid)).astype(bf16)


def read_stats(x, stride):
    x = x.astype(f32)
    return x + pltpu.roll(x, STATS - stride, 1) + pltpu.roll(x, STATS - 2 * stride, 1)


def merge(a, b, outs):
    total = a.shape[1]
    count = (total - STATS) // HD
    size = a.shape[0] // len(outs)

    def store(cols, value):
        for n, out in enumerate(outs):
            out[:, cols] = value[n * size : (n + 1) * size]

    la, lb = read_stats(a[:, total - STATS :], count), read_stats(b[:, total - STATS :], count)
    top = jnp.maximum(la, lb)
    wa, wb = jnp.exp(la - top), jnp.exp(lb - top)
    den = wa + wb
    wa = wa * (1.0 / den)
    wb = wb * (1.0 / den)
    for h in range(count):
        cols = slice(h * HD, (h + 1) * HD)
        store(
            cols,
            (
                wa[:, h : h + 1] * a[:, cols].astype(f32)
                + wb[:, h : h + 1] * b[:, cols].astype(f32)
            ).astype(bf16),
        )
    lse = top + jnp.log(den)
    lane = lax.broadcasted_iota(jnp.int32, lse.shape, 1)
    again = jnp.where(
        lane < count,
        lse,
        jnp.where(lane < 2 * count, pltpu.roll(lse, count, 1), pltpu.roll(lse, 2 * count, 1)),
    )
    store(slice(total - STATS, total), pack_stats(again, count))


def core_kernel(kept_ref, came_ref, *outs):
    merge(kept_ref, came_ref, [out.at[n] for out in outs for n in range(out.shape[0])])


def plane_kernel(kept_ref, came_ref, *outs):
    kept, came = (
        jnp.concatenate([x[n] for n in range(len(outs))], axis=0) for x in (kept_ref, came_ref)
    )
    merge(kept, came, outs)


def finish_kernel(q_ref, nk_ref, nv_ref, *refs):
    *parts, out_ref = refs
    beams, total = parts[0].shape
    heads = nv_ref.shape[1] // HD
    stride = heads * QPK
    lane = lax.broadcasted_iota(jnp.int32, (beams, STATS), 1)
    own = jnp.zeros((beams, STATS), f32)
    for h in range(stride):
        key = nk_ref[:, h // QPK * HD : (h // QPK + 1) * HD].astype(f32)
        s = jnp.sum(q_ref[:, h * HD : (h + 1) * HD].astype(f32) * key, axis=1, keepdims=True)
        own = jnp.where(lane == h, s * SCALE, own)
    lses = [read_stats(x[:, total - STATS :], stride) for x in parts]
    top = functools.reduce(jnp.maximum, lses, own)
    ws = [jnp.exp(x - top) for x in lses]
    w_own = jnp.exp(own - top)
    inv = 1.0 / functools.reduce(jnp.add, ws, w_own)
    ws = [w * inv for w in ws]
    w_own = w_own * inv
    for k in range(heads):
        value = nv_ref[:, k * HD : (k + 1) * HD].astype(f32)
        for i in range(QPK):
            h = k * QPK + i
            acc = w_own[:, h : h + 1] * value
            for w, x in zip(ws, parts):
                acc = acc + w[:, h : h + 1] * x[:, h * HD : (h + 1) * HD].astype(f32)
            out_ref[:, h * HD : (h + 1) * HD] = acc.astype(bf16)


def project_kernel(near_a, far_a, near_b, far_b, w_ref, keep_ref, send_ref, rows_ref):
    requests, group = rows_ref.shape[:2]
    me, side = lax.axis_index("beam"), lax.axis_index("head")
    mine, spot = me // group, me % group
    order = line_order(requests)
    order = order[-1:] + order[:1] + order[-2:0:-1]
    for first, refs in ((0, (near_a, far_a)), (requests // 2, (near_b, far_b))):
        for core, ref in enumerate(refs):
            for x in range(2):
                for n in range(requests // 2):
                    rows_ref[mine ^ order[first + n], spot ^ (2 * x + core)] = ref[x, n]
    a = jnp.concatenate(
        [rows_ref[z, j] for z in range(requests) for j in range(group)], axis=0
    )
    out = jnp.dot(a, w_ref[...], preferred_element_type=f32)
    half = requests * BEAM_WIDTH // 2

    @pl.when(side == 0)
    def _():
        keep_ref[...] = out[:half]
        send_ref[...] = out[half:].astype(bf16)

    @pl.when(side != 0)
    def _():
        keep_ref[...] = out[half:]
        send_ref[...] = out[:half].astype(bf16)


def whole_blocks(n, smem=(), far=()):
    places = [pltpu.SMEM if i in smem else pltpu.HBM if i in far else pltpu.VMEM for i in range(n)]
    return [pl.BlockSpec(memory_space=place) for place in places]


def call(kernel, name, out_shape, *args, smem=(), far=(), scratch=(), vmem=8, cost=None):
    many = isinstance(out_shape, tuple)
    return pl.pallas_call(
        kernel,
        out_shape=out_shape,
        in_specs=whole_blocks(len(args), smem, far),
        out_specs=tuple(whole_blocks(len(out_shape))) if many else whole_blocks(1)[0],
        scratch_shapes=list(scratch),
        compiler_params=pltpu.CompilerParams(vmem_limit_bytes=vmem * 1024 * 1024),
        cost_estimate=cost and pl.CostEstimate(flops=cost, bytes_accessed=cost, transcendentals=0),
        name=name,
    )(*(pltpu.with_memory_space_constraint(x, pltpu.HBM) if i in far else x for i, x in enumerate(args)))


def per_device(
    queries,
    new_keys,
    new_values,
    prompt_keys,
    prompt_values,
    private_keys,
    private_values,
    parents,
    block_counts,
    out_weight,
):
    beams, width = queries.shape
    group = BEAM_WIDTH // beams
    assert group == 4
    devices = lax.axis_size("beam")
    requests = prompt_keys.shape[0]
    sides = lax.axis_size("head")
    total = width + STATS

    def swap(x, with_bit):
        return lax.ppermute(x, "beam", [(i, i ^ with_bit) for i in range(devices)])

    rows = requests * beams
    heads = width // (QPK * HD)
    length, span = prompt_keys.shape[1], private_keys.shape[1]
    line = jax.ShapeDtypeStruct((rows, total), bf16)
    order = line_order(requests)
    others = order[:-1]
    came = [swap(queries, t * group) for t in others]
    prompt = jax.ShapeDtypeStruct(prompt_keys.shape, bf16)
    private = jax.ShapeDtypeStruct(private_keys.shape, bf16)
    stored = (swap(private_keys, 1), swap(private_values, 1))
    own, parent_tail, *olds = call(
        load_private_kernel,
        "load_private",
        (
            jax.ShapeDtypeStruct((beams, width), bf16),
            jax.ShapeDtypeStruct((beams, STATS), bf16),
            jax.ShapeDtypeStruct((8, STATS), jnp.int32),
            private,
            private,
        ),
        queries,
        parents,
        block_counts,
        private_keys,
        private_values,
        far=(0, 1, 2, 3, 4),
        scratch=[
            pltpu.SMEM((beams,), jnp.int32),
            pltpu.SMEM((beams,), jnp.int32),
            pltpu.SemaphoreType.DMA((3,)),
            pltpu.SemaphoreType.DMA((2, beams)),
        ],
        vmem=10,
        cost=2**26,
    )
    *came, parent_tail = lax.optimization_barrier((*came, parent_tail))
    asked = call(line_kernel, "line", line, parent_tail, *came, own)
    prompt_keys, prompt_values, _ = lax.optimization_barrier((prompt_keys, prompt_values, asked))
    prompts = call(
        load_prompt_kernel,
        "load_prompt",
        (prompt, prompt),
        prompt_keys,
        prompt_values,
        far=(0, 1),
        scratch=[pltpu.SemaphoreType.DMA((2, requests))],
        vmem=10,
        cost=2**26,
    )
    caches = (*prompts, *olds)
    limits, late_keys, late_values = lax.optimization_barrier(
        (swap(olds[0], 1), prompt_keys, prompt_values)
    )
    stored = (swap(late_keys, 1), swap(late_values, 1), limits, *stored)

    many = beams * QPK

    def attend(kernel, name, out_shape, kinds, *args):
        return call(
            kernel,
            name,
            out_shape,
            *args,
            scratch=[
                pltpu.VMEM((kinds, heads, requests * many, length), f32),
                pltpu.VMEM((kinds, heads, requests * many, length), bf16),
                pltpu.VMEM((kinds, heads, many, span), f32),
                pltpu.VMEM((kinds, heads, many, span), bf16),
            ],
            vmem=24,
            cost=2**26,
        )

    other = swap(asked, 2)
    own_kernel = functools.partial(attend_kernel, (0,))
    own_here = attend(own_kernel, "attend_own", line, 1, asked, *caches)
    other, own_here = lax.optimization_barrier((other, own_here))
    half = jax.ShapeDtypeStruct((requests // 2, beams, total), bf16)
    send_a, send_b, early = attend(
        side_kernel, "attend_side", (half, half, line), 2, other, asked, *caches, *stored
    )
    asked, _ = lax.optimization_barrier((asked, send_a))
    own_there = attend(late_kernel, "attend_late", line, 1, asked, early, *stored)
    keep_a, keep_b = call(core_kernel, "own_merge", (half, half), own_here, own_there)
    piece = jax.ShapeDtypeStruct((beams, total), bf16)
    parts = []
    for keep, send in ((keep_a, send_a), (keep_b, send_b)):
        parts += call(
            plane_kernel, "plane_merge", (piece,) * (requests // 2), keep, swap(send, 2)
        )
    parts = [swap(x, t * group) if t else x for t, x in zip(order, parts)]
    attended = call(
        finish_kernel,
        "finish",
        jax.ShapeDtypeStruct((beams, width), bf16),
        own,
        new_keys,
        new_values,
        *parts,
    )
    if sides == 2:
        line = [attended] + [swap(attended, t * group) for t in others[:1] + others[:0:-1]]
        halves = []
        for pieces in (line[: requests // 2], line[requests // 2 :]):
            near = jnp.stack(pieces)
            near = jnp.stack([near, swap(near, 2)])
            halves += [near, swap(near, 1)]
        shape = (requests * BEAM_WIDTH // 2, out_weight.shape[1])
        keep, send = call(
            project_kernel,
            "project",
            (jax.ShapeDtypeStruct(shape, f32), jax.ShapeDtypeStruct(shape, bf16)),
            *halves,
            out_weight,
            scratch=[pltpu.VMEM((requests, group, beams, width), bf16)],
            vmem=16,
        )
        came = lax.ppermute(send, "head", [(0, 1), (1, 0)])
        return (keep + came.astype(f32)).astype(bf16)
    rows = lax.all_gather(attended, "beam", axis=0, tiled=True)
    products = jnp.dot(rows, out_weight, preferred_element_type=f32)
    return lax.psum_scatter(products, "head", scatter_dimension=0, tiled=True).astype(bf16)


def solution(mesh):
    placed = (
        P("beam", "head"),
        P("beam", "head"),
        P("beam", "head"),
        P(None, "beam", "head"),
        P(None, "beam", "head"),
        P("beam", None, "head"),
        P("beam", None, "head"),
        P("beam"),
        P("beam"),
        P("head", "beam"),
    )
    return jax.shard_map(
        per_device, mesh=mesh, in_specs=placed, out_specs=P("head", "beam"), check_vma=False
    )
```

```python
import functools
import math

import jax
import jax.numpy as jnp
from jax import lax
from jax.experimental import pallas as pl
from jax.experimental.pallas import tpu as pltpu
from jax.sharding import PartitionSpec as P

HD = 128
QPK = 8
BEAM_WIDTH = 16
BLOCK_LEN = 128
STATS = 128
SCALE = 1.0 / math.sqrt(HD)
LOG2E = math.log2(math.e)

masked_score = -1e30
f32, bf16 = jnp.float32, jnp.bfloat16


def dot(a, b, ca, cb):
    return lax.dot_general(a, b, (((ca,), (cb,)), ((), ())), preferred_element_type=f32)


def soft(scores):
    top = jnp.max(scores, axis=1, keepdims=True)
    weights = jnp.exp2((scores - top) * (SCALE * LOG2E))
    return weights, top * SCALE, jnp.sum(weights, axis=1, keepdims=True)


def line_order(requests):
    return list(range(requests))[::-1]


def line_kernel(tail_ref, *refs):
    *pieces, out_ref = refs
    width = pieces[0].shape[1]
    pieces = pieces[:1] + pieces[-2:0:-1] + pieces[-1:]
    out_ref[:, :width] = jnp.concatenate([x[...] for x in pieces], axis=0)
    out_ref[:, width:] = jnp.concatenate([tail_ref[...]] * len(pieces), axis=0)


def load_private_kernel(
    q_hbm, par_hbm, cnt_hbm, ck_hbm, cv_hbm,
    q_ref, tail_ref, lim_ref, ck_ref, cv_ref, par_ref, cnt_ref, sems, old_sems,
):
    olds = ck_hbm.shape[0]
    copies = [
        pltpu.make_async_copy(src, dst, sems.at[n])
        for n, (src, dst) in enumerate(((q_hbm, q_ref), (par_hbm, par_ref), (cnt_hbm, cnt_ref)))
    ] + [
        pltpu.make_async_copy(src.at[o], dst.at[o], old_sems.at[n, o])
        for n, (src, dst) in enumerate(((ck_hbm, ck_ref), (cv_hbm, cv_ref)))
        for o in range(olds)
    ]
    for x in copies:
        x.start()
    for x in copies[:3]:
        x.wait()
    row = lax.broadcasted_iota(jnp.int32, tail_ref.shape, 0)
    parent = jnp.zeros(row.shape, jnp.int32)
    for b in range(tail_ref.shape[0]):
        parent = jnp.where(row == b, par_ref[b], parent)
    tail_ref[...] = parent.astype(f32).astype(bf16)
    lane = lax.broadcasted_iota(jnp.int32, lim_ref.shape, 1)
    limit = jnp.zeros(lim_ref.shape, jnp.int32)
    for o in range(olds):
        limit = jnp.where(lane == o, cnt_ref[o] * BLOCK_LEN, limit)
    lim_ref[...] = limit
    for x in copies[3:]:
        x.wait()


def load_prompt_kernel(pk_hbm, pv_hbm, pk_ref, pv_ref, sems):
    copies = [
        pltpu.make_async_copy(src.at[r], dst.at[r], sems.at[n, r])
        for n, (src, dst) in enumerate(((pk_hbm, pk_ref), (pv_hbm, pv_ref)))
        for r in range(pk_ref.shape[0])
    ]
    for x in copies:
        x.start()
    for x in copies:
        x.wait()


def attend_kernel(kinds, prompts, privates, q_ref, *refs):
    total = q_ref.shape[1]
    heads = (total - STATS) // (QPK * HD)
    caches = [refs[5 * n : 5 * n + 5] for n in range(len(kinds))]
    *outs, s_ref, p_ref, cs_ref, cp_ref = refs[5 * len(kinds) :]
    if not prompts:
        base_ref, *outs = outs
    requests, span = s_ref.shape[2] // cs_ref.shape[2], cs_ref.shape[3]
    pairs = requests // 2
    beams = q_ref.shape[0] // requests
    stride = heads * QPK
    rows = QPK * beams
    me = lax.axis_index("beam")
    mine = me // (BEAM_WIDTH // beams)
    order = line_order(requests)
    olds = beams

    def prompt(ref, k, u):
        both = [ref[mine ^ order[2 * u + m], :, k * HD : (k + 1) * HD] for m in range(2)]
        return jnp.concatenate(both, axis=1)

    def private(ref, k):
        return jnp.concatenate([ref[o, :, k * HD : (k + 1) * HD] for o in range(olds)], axis=1)

    whose = jnp.concatenate([q_ref[:, total - STATS :].astype(f32)[:beams]] * QPK, axis=0)
    parents, limits, locals_ = [], [], []
    for kind, (_, _, lim_ref, _, _) in zip(kinds, caches):
        parent = whose.astype(jnp.int32) - (me ^ kind) * olds
        column = parent[:, :1]
        limit = jnp.zeros((rows, 1), jnp.int32)
        for o in range(olds):
            known = lim_ref[0:1, o : o + 1]
            limit = jnp.where(column == o, known, limit)
        parents.append(parent)
        limits.append(limit)
        locals_.append((column >= 0) & (column < olds))
    stats = [jnp.zeros((beams, STATS), f32) for _ in range(requests)]
    lane = lax.broadcasted_iota(jnp.int32, (beams, STATS), 1) % stride
    blank = jnp.zeros((rows, HD), bf16)
    kept = {}

    def scores(n, k):
        pk_ref, _, _, ck_ref, _ = caches[n]
        tiles = [q_ref[:, (k * QPK + i) * HD : (k * QPK + i + 1) * HD] for i in range(QPK)]
        q = [
            jnp.concatenate([x[t * beams : (t + 1) * beams] for x in tiles], axis=0)
            for t in range(requests)
        ]
        for u in range(pairs if prompts else 0):
            both = jnp.concatenate(
                [
                    jnp.concatenate([q[2 * u], blank], axis=1),
                    jnp.concatenate([blank, q[2 * u + 1]], axis=1),
                ],
                axis=0,
            )
            s_ref[n, k, 2 * u * rows : 2 * (u + 1) * rows] = dot(both, prompt(pk_ref, k, u), 1, 1)
        if not privates:
            return
        chosen = jnp.concatenate(
            [jnp.where(parents[n] == o, q[-1], blank) for o in range(olds)], axis=1
        )
        cs_ref[n, k] = dot(chosen, private(ck_ref, k), 1, 1)

    def weigh(n, k):
        top = den = ctop = cden = None
        if prompts:
            p, top, den = soft(s_ref[n, k])
            p_ref[n, k] = p.astype(bf16)
        if not privates:
            kept[n, k] = (top, den, ctop, cden)
            return
        place = lax.broadcasted_iota(jnp.int32, (rows, span), 1)
        c, ctop, cden = soft(jnp.where(place < limits[n], cs_ref[n, k], masked_score))
        cp_ref[n, k] = c.astype(bf16)
        kept[n, k] = (top, den, ctop, cden)

    def values(n, k):
        _, pv_ref, _, _, cv_ref = caches[n]
        tops, dens, ctop, cden = kept.pop((n, k))
        found = []
        for u in range(pairs if prompts else 0):
            both = dot(
                p_ref[n, k, 2 * u * rows : 2 * (u + 1) * rows], prompt(pv_ref, k, u), 1, 0
            )
            for m, num in enumerate((both[:rows, :HD], both[rows:, HD:])):
                part = slice((2 * u + m) * rows, (2 * u + m + 1) * rows)
                found.append((num, tops[part], dens[part]))
        if not privates:
            return found
        every = dot(cp_ref[n, k], private(cv_ref, k), 1, 0)
        cnum = every[:, :HD]
        for o in range(1, olds):
            cnum = jnp.where(parents[n] == o, every[:, o * HD : (o + 1) * HD], cnum)
        if not prompts:
            cden = jnp.where(locals_[n], cden, 0.0)
            return [(jnp.where(locals_[n], cnum, 0.0), jnp.where(locals_[n], ctop, masked_score), cden)]
        num, top, den = found[-1]
        both = jnp.where(locals_[n], jnp.maximum(top, ctop), top)
        a = jnp.exp(top - both)
        e = jnp.where(locals_[n], jnp.exp(jnp.where(locals_[n], ctop, both) - both), 0.0)
        found[-1] = (a * num + e * cnum, both, a * den + e * cden)
        return found

    def finish(k):
        found = [values(n, k) for n in range(len(kinds))]
        done = []
        for t in range(requests):
            if not prompts and t < requests - 1:
                continue
            at = t if prompts else 0
            if prompts:
                num, top, den = found[0][t]
                others = found[1:]
            else:
                cols = [
                    slice((k * QPK + i) * HD, (k * QPK + i + 1) * HD) for i in range(QPK)
                ]
                num = jnp.concatenate([base_ref[pairs - 1, :, c] for c in cols], axis=0).astype(f32)
                top = jnp.concatenate(
                    [base_lse[:, k * QPK + i : k * QPK + i + 1] for i in range(QPK)], axis=0
                )
                den = jnp.ones_like(top)
                others = found
            for other in others:
                num2, top2, den2 = other[at]
                both = jnp.maximum(top, top2)
                a, e = jnp.exp(top - both), jnp.exp(top2 - both)
                num, top, den = a * num + e * num2, both, a * den + e * den2
            done.append(num * (1.0 / den))
            lse = top + jnp.log(den)
            for i in range(QPK):
                stats[t] = jnp.where(
                    lane == k * QPK + i,
                    jnp.broadcast_to(lse[i * beams : (i + 1) * beams], (beams, STATS)),
                    stats[t],
                )
        for i in range(QPK):
            cols = slice((k * QPK + i) * HD, (k * QPK + i + 1) * HD)
            if prompts:
                store(cols, [x[i * beams : (i + 1) * beams] for x in done])
            else:
                outs[0][pairs - 1, :, cols] = done[0][i * beams : (i + 1) * beams].astype(bf16)

    def store(cols, pieces):
        for n, piece in enumerate(pieces):
            outs[n // pairs][n % pairs, :, cols] = piece.astype(bf16)

    if not prompts:
        base_lse = read_stats(base_ref[pairs - 1, :, total - STATS :], stride)
        for n in range(pairs - 1):
            outs[0][n] = base_ref[n]
    for stage in (scores, weigh):
        for n in range(len(kinds)):
            for k in range(heads):
                stage(n, k)
    for k in range(heads):
        finish(k)
    if prompts:
        store(slice(total - STATS, total), [pack_stats(x, stride) for x in stats])
    else:
        outs[0][pairs - 1, :, total - STATS :] = pack_stats(stats[-1], stride)


def pack_stats(x, stride):
    hi = x.astype(bf16).astype(f32)
    mid = (x - hi).astype(bf16).astype(f32)
    which = lax.broadcasted_iota(jnp.int32, x.shape, 1) // stride
    return jnp.where(which == 0, hi, jnp.where(which == 1, mid, x - hi - mid)).astype(bf16)


def read_stats(x, stride):
    x = x.astype(f32)
    return x + pltpu.roll(x, STATS - stride, 1) + pltpu.roll(x, STATS - 2 * stride, 1)


def plane_kernel(*refs):
    count, beams, total = refs[0].shape
    parts, outs = refs[:-count], refs[-count:]
    parts = [jnp.concatenate([x[n] for n in range(count)], axis=0) for x in parts]
    heads = (total - STATS) // HD

    def store(cols, value):
        for n, out in enumerate(outs):
            out[:, cols] = value[n * beams : (n + 1) * beams]

    lses = [read_stats(x[:, total - STATS :], heads) for x in parts]
    top = functools.reduce(jnp.maximum, lses)
    ws = [jnp.exp(x - top) for x in lses]
    den = functools.reduce(jnp.add, ws)
    inv = 1.0 / den
    ws = [w * inv for w in ws]
    for h in range(heads):
        cols = slice(h * HD, (h + 1) * HD)
        acc = None
        for w, x in zip(ws, parts):
            one = w[:, h : h + 1] * x[:, cols].astype(f32)
            acc = one if acc is None else acc + one
        store(cols, acc.astype(bf16))
    lse = top + jnp.log(den)
    lane = lax.broadcasted_iota(jnp.int32, lse.shape, 1)
    again = jnp.where(
        lane < heads,
        lse,
        jnp.where(lane < 2 * heads, pltpu.roll(lse, heads, 1), pltpu.roll(lse, 2 * heads, 1)),
    )
    store(slice(total - STATS, total), pack_stats(again, heads))


def finish_kernel(q_ref, nk_ref, nv_ref, *refs):
    *parts, out_ref = refs
    beams, total = parts[0].shape
    heads = nv_ref.shape[1] // HD
    stride = heads * QPK
    lane = lax.broadcasted_iota(jnp.int32, (beams, STATS), 1)
    own = jnp.zeros((beams, STATS), f32)
    for h in range(stride):
        key = nk_ref[:, h // QPK * HD : (h // QPK + 1) * HD].astype(f32)
        s = jnp.sum(q_ref[:, h * HD : (h + 1) * HD].astype(f32) * key, axis=1, keepdims=True)
        own = jnp.where(lane == h, s * SCALE, own)
    lses = [read_stats(x[:, total - STATS :], stride) for x in parts]
    top = functools.reduce(jnp.maximum, lses, own)
    ws = [jnp.exp(x - top) for x in lses]
    w_own = jnp.exp(own - top)
    inv = 1.0 / functools.reduce(jnp.add, ws, w_own)
    ws = [w * inv for w in ws]
    w_own = w_own * inv
    for k in range(heads):
        value = nv_ref[:, k * HD : (k + 1) * HD].astype(f32)
        for i in range(QPK):
            h = k * QPK + i
            acc = w_own[:, h : h + 1] * value
            for w, x in zip(ws, parts):
                acc = acc + w[:, h : h + 1] * x[:, h * HD : (h + 1) * HD].astype(f32)
            out_ref[:, h * HD : (h + 1) * HD] = acc.astype(bf16)


def project_kernel(near_a, far_a, near_b, far_b, w_ref, keep_ref, send_ref, rows_ref):
    requests, group = rows_ref.shape[:2]
    me, side = lax.axis_index("beam"), lax.axis_index("head")
    mine, spot = me // group, me % group
    order = line_order(requests)
    order = order[-1:] + order[:1] + order[-2:0:-1]
    for first, refs in ((0, (near_a, far_a)), (requests // 2, (near_b, far_b))):
        for core, ref in enumerate(refs):
            for x in range(2):
                for n in range(requests // 2):
                    rows_ref[mine ^ order[first + n], spot ^ (2 * x + core)] = ref[x, n]
    a = jnp.concatenate(
        [rows_ref[z, j] for z in range(requests) for j in range(group)], axis=0
    )
    out = jnp.dot(a, w_ref[...], preferred_element_type=f32)
    half = requests * BEAM_WIDTH // 2

    @pl.when(side == 0)
    def _():
        keep_ref[...] = out[:half]
        send_ref[...] = out[half:].astype(bf16)

    @pl.when(side != 0)
    def _():
        keep_ref[...] = out[half:]
        send_ref[...] = out[:half].astype(bf16)


def whole_blocks(n, smem=(), far=()):
    places = [pltpu.SMEM if i in smem else pltpu.HBM if i in far else pltpu.VMEM for i in range(n)]
    return [pl.BlockSpec(memory_space=place) for place in places]


def call(kernel, name, out_shape, *args, smem=(), far=(), scratch=(), vmem=8, cost=None):
    many = isinstance(out_shape, tuple)
    return pl.pallas_call(
        kernel,
        out_shape=out_shape,
        in_specs=whole_blocks(len(args), smem, far),
        out_specs=tuple(whole_blocks(len(out_shape))) if many else whole_blocks(1)[0],
        scratch_shapes=list(scratch),
        compiler_params=pltpu.CompilerParams(vmem_limit_bytes=vmem * 1024 * 1024),
        cost_estimate=cost and pl.CostEstimate(flops=cost, bytes_accessed=cost, transcendentals=0),
        name=name,
    )(*(pltpu.with_memory_space_constraint(x, pltpu.HBM) if i in far else x for i, x in enumerate(args)))


def per_device(
    queries,
    new_keys,
    new_values,
    prompt_keys,
    prompt_values,
    private_keys,
    private_values,
    parents,
    block_counts,
    out_weight,
):
    beams, width = queries.shape
    group = BEAM_WIDTH // beams
    assert group == 4
    devices = lax.axis_size("beam")
    requests = prompt_keys.shape[0]
    sides = lax.axis_size("head")
    total = width + STATS

    def swap(x, with_bit):
        return lax.ppermute(x, "beam", [(i, i ^ with_bit) for i in range(devices)])

    rows = requests * beams
    heads = width // (QPK * HD)
    length, span = prompt_keys.shape[1], private_keys.shape[1]
    line = jax.ShapeDtypeStruct((rows, total), bf16)
    order = line_order(requests)
    others = order[:-1]
    came = [swap(queries, t * group) for t in others[:1] + others[:0:-1]]
    prompt = jax.ShapeDtypeStruct(prompt_keys.shape, bf16)
    private = jax.ShapeDtypeStruct(private_keys.shape, bf16)
    stored = (swap(private_keys, 1), swap(private_values, 1))
    own, parent_tail, *olds = call(
        load_private_kernel,
        "load_private",
        (
            jax.ShapeDtypeStruct((beams, width), bf16),
            jax.ShapeDtypeStruct((beams, STATS), bf16),
            jax.ShapeDtypeStruct((8, STATS), jnp.int32),
            private,
            private,
        ),
        queries,
        parents,
        block_counts,
        private_keys,
        private_values,
        far=(0, 1, 2, 3, 4),
        scratch=[
            pltpu.SMEM((beams,), jnp.int32),
            pltpu.SMEM((beams,), jnp.int32),
            pltpu.SemaphoreType.DMA((3,)),
            pltpu.SemaphoreType.DMA((2, beams)),
        ],
        vmem=10,
        cost=2**26,
    )
    *came, parent_tail = lax.optimization_barrier((*came, parent_tail))
    asked = call(line_kernel, "line", line, parent_tail, *came, own)
    prompt_keys, prompt_values, _ = lax.optimization_barrier((prompt_keys, prompt_values, asked))
    prompts = call(
        load_prompt_kernel,
        "load_prompt",
        (prompt, prompt),
        prompt_keys,
        prompt_values,
        far=(0, 1),
        scratch=[pltpu.SemaphoreType.DMA((2, requests))],
        vmem=10,
        cost=2**26,
    )
    caches = (*prompts, *olds)
    limits, late_keys, late_values = lax.optimization_barrier(
        (swap(olds[0], 1), prompt_keys, prompt_values)
    )
    stored = (swap(late_keys, 1), swap(late_values, 1), limits, *stored)

    many = beams * QPK

    def attend(name, kinds, prompts, privates, asked, *caches):
        both = (half, half) if prompts else half
        return call(
            functools.partial(attend_kernel, kinds, prompts, privates),
            name,
            both,
            asked,
            *caches,
            scratch=[
                pltpu.VMEM((len(kinds), heads, requests * many, length), f32),
                pltpu.VMEM((len(kinds), heads, requests * many, length), bf16),
                pltpu.VMEM((len(kinds), heads, many, span), f32),
                pltpu.VMEM((len(kinds), heads, many, span), bf16),
            ],
            vmem=24,
            cost=2**26,
        )

    half = jax.ShapeDtypeStruct((requests // 2, beams, total), bf16)
    other = swap(asked, 2)
    here_a, here_b = attend("attend_own", (0,), True, True, asked, *caches)
    other, here_a, here_b = lax.optimization_barrier((other, here_a, here_b))
    send_a, send_b = attend("side_prompt", (0, 1), True, False, other, *caches, *stored)
    asked, send_a = lax.optimization_barrier((asked, send_a))
    there_a, there_b = attend("own_prompt", (1,), True, False, asked, *stored)
    send_b, there_a = lax.optimization_barrier((send_b, there_a))
    send_b = attend("side_private", (0, 1), False, True, other, *caches, *stored, send_b)
    piece = jax.ShapeDtypeStruct((beams, total), bf16)
    few = (piece,) * (requests // 2)
    came_a, came_b = swap(send_a, 2), swap(send_b, 2)
    parts = call(plane_kernel, "plane_merge", few, here_a, there_a, came_a)
    there_b, *parts = lax.optimization_barrier((there_b, *parts))
    there_b = attend("own_private", (1,), False, True, asked, *stored, there_b)
    parts = [*parts, *call(plane_kernel, "plane_merge", few, here_b, there_b, came_b)]
    parts = [swap(x, t * group) if t else x for t, x in zip(order, parts)]
    attended = call(
        finish_kernel,
        "finish",
        jax.ShapeDtypeStruct((beams, width), bf16),
        own,
        new_keys,
        new_values,
        *parts,
    )
    if sides == 2:
        line = [attended] + [swap(attended, t * group) for t in others[:1] + others[:0:-1]]
        halves = []
        for pieces in (line[: requests // 2], line[requests // 2 :]):
            near = jnp.stack(pieces)
            near = jnp.stack([near, swap(near, 2)])
            halves += [near, swap(near, 1)]
        shape = (requests * BEAM_WIDTH // 2, out_weight.shape[1])
        keep, send = call(
            project_kernel,
            "project",
            (jax.ShapeDtypeStruct(shape, f32), jax.ShapeDtypeStruct(shape, bf16)),
            *halves,
            out_weight,
            scratch=[pltpu.VMEM((requests, group, beams, width), bf16)],
            vmem=16,
        )
        came = lax.ppermute(send, "head", [(0, 1), (1, 0)])
        return (keep + came.astype(f32)).astype(bf16)
    rows = lax.all_gather(attended, "beam", axis=0, tiled=True)
    products = jnp.dot(rows, out_weight, preferred_element_type=f32)
    return lax.psum_scatter(products, "head", scatter_dimension=0, tiled=True).astype(bf16)


def solution(mesh):
    placed = (
        P("beam", "head"),
        P("beam", "head"),
        P("beam", "head"),
        P(None, "beam", "head"),
        P(None, "beam", "head"),
        P("beam", None, "head"),
        P("beam", None, "head"),
        P("beam"),
        P("beam"),
        P("head", "beam"),
    )
    return jax.shard_map(
        per_device, mesh=mesh, in_specs=placed, out_specs=P("head", "beam"), check_vma=False
    )
```

```python
import functools
import math

import jax
import jax.numpy as jnp
from jax import lax
from jax.experimental import pallas as pl
from jax.experimental.pallas import tpu as pltpu
from jax.sharding import PartitionSpec as P

HD = 128
QPK = 8
BEAM_WIDTH = 16
BLOCK_LEN = 128
STATS = 128
SCALE = 1.0 / math.sqrt(HD)
LOG2E = math.log2(math.e)

masked_score = -1e30
f32, bf16 = jnp.float32, jnp.bfloat16


def dot(a, b, ca, cb):
    return lax.dot_general(a, b, (((ca,), (cb,)), ((), ())), preferred_element_type=f32)


def soft(scores):
    top = jnp.max(scores, axis=1, keepdims=True)
    weights = jnp.exp2((scores - top) * (SCALE * LOG2E))
    return weights, top * SCALE, jnp.sum(weights, axis=1, keepdims=True)


def line_order(requests):
    return list(range(requests))[::-1]


def line_kernel(tail_ref, *refs):
    *pieces, out_ref = refs
    width = pieces[0].shape[1]
    pieces = pieces[:1] + pieces[-2:0:-1] + pieces[-1:]
    out_ref[:, :width] = jnp.concatenate([x[...] for x in pieces], axis=0)
    out_ref[:, width:] = jnp.concatenate([tail_ref[...]] * len(pieces), axis=0)


def load_private_kernel(
    q_hbm, par_hbm, cnt_hbm, ck_hbm, cv_hbm,
    q_ref, tail_ref, lim_ref, ck_ref, cv_ref, par_ref, cnt_ref, sems, old_sems,
):
    olds = ck_hbm.shape[0]
    copies = [
        pltpu.make_async_copy(src, dst, sems.at[n])
        for n, (src, dst) in enumerate(((q_hbm, q_ref), (par_hbm, par_ref), (cnt_hbm, cnt_ref)))
    ] + [
        pltpu.make_async_copy(src.at[o], dst.at[o], old_sems.at[n, o])
        for n, (src, dst) in enumerate(((ck_hbm, ck_ref), (cv_hbm, cv_ref)))
        for o in range(olds)
    ]
    for x in copies:
        x.start()
    for x in copies[:3]:
        x.wait()
    row = lax.broadcasted_iota(jnp.int32, tail_ref.shape, 0)
    parent = jnp.zeros(row.shape, jnp.int32)
    for b in range(tail_ref.shape[0]):
        parent = jnp.where(row == b, par_ref[b], parent)
    tail_ref[...] = parent.astype(f32).astype(bf16)
    lane = lax.broadcasted_iota(jnp.int32, lim_ref.shape, 1)
    limit = jnp.zeros(lim_ref.shape, jnp.int32)
    for o in range(olds):
        limit = jnp.where(lane == o, cnt_ref[o] * BLOCK_LEN, limit)
    lim_ref[...] = limit
    for x in copies[3:]:
        x.wait()


def load_prompt_kernel(pk_hbm, pv_hbm, pk_ref, pv_ref, sems):
    copies = [
        pltpu.make_async_copy(src.at[r], dst.at[r], sems.at[n, r])
        for n, (src, dst) in enumerate(((pk_hbm, pk_ref), (pv_hbm, pv_ref)))
        for r in range(pk_ref.shape[0])
    ]
    for x in copies:
        x.start()
    for x in copies:
        x.wait()


def attend_kernel(kinds, prompts, privates, q_ref, *refs):
    total = q_ref.shape[1]
    heads = (total - STATS) // (QPK * HD)
    caches = [refs[5 * n : 5 * n + 5] for n in range(len(kinds))]
    *outs, s_ref, p_ref, cs_ref, cp_ref = refs[5 * len(kinds) :]
    if not prompts:
        base_ref, *outs = outs
    requests, span = s_ref.shape[2] // cs_ref.shape[2], cs_ref.shape[3]
    pairs = requests // 2
    beams = q_ref.shape[0] // requests
    stride = heads * QPK
    rows = QPK * beams
    me = lax.axis_index("beam")
    mine = me // (BEAM_WIDTH // beams)
    order = line_order(requests)
    olds = beams

    def prompt(ref, k, u):
        both = [ref[mine ^ order[2 * u + m], :, k * HD : (k + 1) * HD] for m in range(2)]
        return jnp.concatenate(both, axis=1)

    def private(ref, k):
        return jnp.concatenate([ref[o, :, k * HD : (k + 1) * HD] for o in range(olds)], axis=1)

    whose = jnp.concatenate([q_ref[:, total - STATS :].astype(f32)[:beams]] * QPK, axis=0)
    parents, limits, locals_ = [], [], []
    for kind, (_, _, lim_ref, _, _) in zip(kinds, caches):
        parent = whose.astype(jnp.int32) - (me ^ kind) * olds
        column = parent[:, :1]
        limit = jnp.zeros((rows, 1), jnp.int32)
        for o in range(olds):
            known = lim_ref[0:1, o : o + 1]
            limit = jnp.where(column == o, known, limit)
        parents.append(parent)
        limits.append(limit)
        locals_.append((column >= 0) & (column < olds))
    stats = [jnp.zeros((beams, STATS), f32) for _ in range(requests)]
    lane = lax.broadcasted_iota(jnp.int32, (beams, STATS), 1) % stride
    blank = jnp.zeros((rows, HD), bf16)
    kept = {}

    def scores(n, k):
        pk_ref, _, _, ck_ref, _ = caches[n]
        tiles = [q_ref[:, (k * QPK + i) * HD : (k * QPK + i + 1) * HD] for i in range(QPK)]
        q = [
            jnp.concatenate([x[t * beams : (t + 1) * beams] for x in tiles], axis=0)
            for t in range(requests)
        ]
        for u in range(pairs if prompts else 0):
            both = jnp.concatenate(
                [
                    jnp.concatenate([q[2 * u], blank], axis=1),
                    jnp.concatenate([blank, q[2 * u + 1]], axis=1),
                ],
                axis=0,
            )
            s_ref[n, k, 2 * u * rows : 2 * (u + 1) * rows] = dot(both, prompt(pk_ref, k, u), 1, 1)
        if not privates:
            return
        chosen = jnp.concatenate(
            [jnp.where(parents[n] == o, q[-1], blank) for o in range(olds)], axis=1
        )
        cs_ref[n, k] = dot(chosen, private(ck_ref, k), 1, 1)

    def weigh(n, k):
        top = den = ctop = cden = None
        if prompts:
            p, top, den = soft(s_ref[n, k])
            p_ref[n, k] = p.astype(bf16)
        if not privates:
            kept[n, k] = (top, den, ctop, cden)
            return
        place = lax.broadcasted_iota(jnp.int32, (rows, span), 1)
        c, ctop, cden = soft(jnp.where(place < limits[n], cs_ref[n, k], masked_score))
        cp_ref[n, k] = c.astype(bf16)
        kept[n, k] = (top, den, ctop, cden)

    def values(n, k):
        _, pv_ref, _, _, cv_ref = caches[n]
        tops, dens, ctop, cden = kept.pop((n, k))
        found = []
        for u in range(pairs if prompts else 0):
            both = dot(
                p_ref[n, k, 2 * u * rows : 2 * (u + 1) * rows], prompt(pv_ref, k, u), 1, 0
            )
            for m, num in enumerate((both[:rows, :HD], both[rows:, HD:])):
                part = slice((2 * u + m) * rows, (2 * u + m + 1) * rows)
                found.append((num, tops[part], dens[part]))
        if not privates:
            return found
        every = dot(cp_ref[n, k], private(cv_ref, k), 1, 0)
        cnum = every[:, :HD]
        for o in range(1, olds):
            cnum = jnp.where(parents[n] == o, every[:, o * HD : (o + 1) * HD], cnum)
        if not prompts:
            cden = jnp.where(locals_[n], cden, 0.0)
            return [(jnp.where(locals_[n], cnum, 0.0), jnp.where(locals_[n], ctop, masked_score), cden)]
        num, top, den = found[-1]
        both = jnp.where(locals_[n], jnp.maximum(top, ctop), top)
        a = jnp.exp(top - both)
        e = jnp.where(locals_[n], jnp.exp(jnp.where(locals_[n], ctop, both) - both), 0.0)
        found[-1] = (a * num + e * cnum, both, a * den + e * cden)
        return found

    def finish(k):
        found = [values(n, k) for n in range(len(kinds))]
        done = []
        for t in range(requests):
            if not prompts and t < requests - 1:
                continue
            at = t if prompts else 0
            if prompts:
                num, top, den = found[0][t]
                others = found[1:]
            else:
                cols = [
                    slice((k * QPK + i) * HD, (k * QPK + i + 1) * HD) for i in range(QPK)
                ]
                num = jnp.concatenate([base_ref[pairs - 1, :, c] for c in cols], axis=0).astype(f32)
                top = jnp.concatenate(
                    [base_lse[:, k * QPK + i : k * QPK + i + 1] for i in range(QPK)], axis=0
                )
                den = jnp.ones_like(top)
                others = found
            for other in others:
                num2, top2, den2 = other[at]
                both = jnp.maximum(top, top2)
                a, e = jnp.exp(top - both), jnp.exp(top2 - both)
                num, top, den = a * num + e * num2, both, a * den + e * den2
            done.append(num * (1.0 / den))
            lse = top + jnp.log(den)
            for i in range(QPK):
                stats[t] = jnp.where(
                    lane == k * QPK + i,
                    jnp.broadcast_to(lse[i * beams : (i + 1) * beams], (beams, STATS)),
                    stats[t],
                )
        for i in range(QPK):
            cols = slice((k * QPK + i) * HD, (k * QPK + i + 1) * HD)
            if prompts:
                store(cols, [x[i * beams : (i + 1) * beams] for x in done])
            else:
                outs[0][pairs - 1, :, cols] = done[0][i * beams : (i + 1) * beams].astype(bf16)

    def store(cols, pieces):
        for n, piece in enumerate(pieces):
            outs[n // pairs][n % pairs, :, cols] = piece.astype(bf16)

    if not prompts:
        base_lse = read_stats(base_ref[pairs - 1, :, total - STATS :], stride)
        for n in range(pairs - 1):
            outs[0][n] = base_ref[n]
    for stage in (scores, weigh):
        for n in range(len(kinds)):
            for k in range(heads):
                stage(n, k)
    for k in range(heads):
        finish(k)
    if prompts:
        store(slice(total - STATS, total), [pack_stats(x, stride) for x in stats])
    else:
        outs[0][pairs - 1, :, total - STATS :] = pack_stats(stats[-1], stride)


def pack_stats(x, stride):
    hi = x.astype(bf16).astype(f32)
    mid = (x - hi).astype(bf16).astype(f32)
    which = lax.broadcasted_iota(jnp.int32, x.shape, 1) // stride
    return jnp.where(which == 0, hi, jnp.where(which == 1, mid, x - hi - mid)).astype(bf16)


def read_stats(x, stride):
    x = x.astype(f32)
    return x + pltpu.roll(x, STATS - stride, 1) + pltpu.roll(x, STATS - 2 * stride, 1)


def plane_kernel(*refs):
    count, beams, total = refs[0].shape
    parts, outs = refs[:-count], refs[-count:]
    parts = [jnp.concatenate([x[n] for n in range(count)], axis=0) for x in parts]
    heads = (total - STATS) // HD

    def store(cols, value):
        for n, out in enumerate(outs):
            out[:, cols] = value[n * beams : (n + 1) * beams]

    lses = [read_stats(x[:, total - STATS :], heads) for x in parts]
    top = functools.reduce(jnp.maximum, lses)
    ws = [jnp.exp(x - top) for x in lses]
    den = functools.reduce(jnp.add, ws)
    inv = 1.0 / den
    ws = [w * inv for w in ws]
    for h in range(heads):
        cols = slice(h * HD, (h + 1) * HD)
        acc = None
        for w, x in zip(ws, parts):
            one = w[:, h : h + 1] * x[:, cols].astype(f32)
            acc = one if acc is None else acc + one
        store(cols, acc.astype(bf16))
    lse = top + jnp.log(den)
    lane = lax.broadcasted_iota(jnp.int32, lse.shape, 1)
    again = jnp.where(
        lane < heads,
        lse,
        jnp.where(lane < 2 * heads, pltpu.roll(lse, heads, 1), pltpu.roll(lse, 2 * heads, 1)),
    )
    store(slice(total - STATS, total), pack_stats(again, heads))


def finish_kernel(q_ref, nk_ref, nv_ref, *refs):
    *parts, out_ref = refs
    beams, total = parts[0].shape
    heads = nv_ref.shape[1] // HD
    stride = heads * QPK
    lane = lax.broadcasted_iota(jnp.int32, (beams, STATS), 1)
    own = jnp.zeros((beams, STATS), f32)
    for h in range(stride):
        key = nk_ref[:, h // QPK * HD : (h // QPK + 1) * HD].astype(f32)
        s = jnp.sum(q_ref[:, h * HD : (h + 1) * HD].astype(f32) * key, axis=1, keepdims=True)
        own = jnp.where(lane == h, s * SCALE, own)
    lses = [read_stats(x[:, total - STATS :], stride) for x in parts]
    top = functools.reduce(jnp.maximum, lses, own)
    ws = [jnp.exp(x - top) for x in lses]
    w_own = jnp.exp(own - top)
    inv = 1.0 / functools.reduce(jnp.add, ws, w_own)
    ws = [w * inv for w in ws]
    w_own = w_own * inv
    for k in range(heads):
        value = nv_ref[:, k * HD : (k + 1) * HD].astype(f32)
        for i in range(QPK):
            h = k * QPK + i
            acc = w_own[:, h : h + 1] * value
            for w, x in zip(ws, parts):
                acc = acc + w[:, h : h + 1] * x[:, h * HD : (h + 1) * HD].astype(f32)
            out_ref[:, h * HD : (h + 1) * HD] = acc.astype(bf16)


def project_kernel(near_a, far_a, near_b, far_b, w_ref, keep_ref, send_ref, rows_ref):
    requests, group = rows_ref.shape[:2]
    me, side = lax.axis_index("beam"), lax.axis_index("head")
    mine, spot = me // group, me % group
    order = line_order(requests)
    order = order[-1:] + order[:1] + order[-2:0:-1]
    for first, refs in ((0, (near_a, far_a)), (requests // 2, (near_b, far_b))):
        for core, ref in enumerate(refs):
            for x in range(2):
                for n in range(requests // 2):
                    rows_ref[mine ^ order[first + n], spot ^ (2 * x + core)] = ref[x, n]
    a = jnp.concatenate(
        [rows_ref[z, j] for z in range(requests) for j in range(group)], axis=0
    )
    out = jnp.dot(a, w_ref[...], preferred_element_type=f32)
    half = requests * BEAM_WIDTH // 2

    @pl.when(side == 0)
    def _():
        keep_ref[...] = out[:half]
        send_ref[...] = out[half:].astype(bf16)

    @pl.when(side != 0)
    def _():
        keep_ref[...] = out[half:]
        send_ref[...] = out[:half].astype(bf16)


def whole_blocks(n, smem=(), far=()):
    places = [pltpu.SMEM if i in smem else pltpu.HBM if i in far else pltpu.VMEM for i in range(n)]
    return [pl.BlockSpec(memory_space=place) for place in places]


def call(kernel, name, out_shape, *args, smem=(), far=(), scratch=(), vmem=8, cost=None):
    many = isinstance(out_shape, tuple)
    return pl.pallas_call(
        kernel,
        out_shape=out_shape,
        in_specs=whole_blocks(len(args), smem, far),
        out_specs=tuple(whole_blocks(len(out_shape))) if many else whole_blocks(1)[0],
        scratch_shapes=list(scratch),
        compiler_params=pltpu.CompilerParams(vmem_limit_bytes=vmem * 1024 * 1024),
        cost_estimate=cost and pl.CostEstimate(flops=cost, bytes_accessed=cost, transcendentals=0),
        name=name,
    )(*(pltpu.with_memory_space_constraint(x, pltpu.HBM) if i in far else x for i, x in enumerate(args)))


def per_device(
    queries,
    new_keys,
    new_values,
    prompt_keys,
    prompt_values,
    private_keys,
    private_values,
    parents,
    block_counts,
    out_weight,
):
    beams, width = queries.shape
    group = BEAM_WIDTH // beams
    assert group == 4
    devices = lax.axis_size("beam")
    requests = prompt_keys.shape[0]
    sides = lax.axis_size("head")
    total = width + STATS

    def swap(x, with_bit):
        return lax.ppermute(x, "beam", [(i, i ^ with_bit) for i in range(devices)])

    rows = requests * beams
    heads = width // (QPK * HD)
    length, span = prompt_keys.shape[1], private_keys.shape[1]
    line = jax.ShapeDtypeStruct((rows, total), bf16)
    order = line_order(requests)
    others = order[:-1]
    came = [swap(queries, t * group) for t in others[:1] + others[:0:-1]]
    prompt = jax.ShapeDtypeStruct(prompt_keys.shape, bf16)
    private = jax.ShapeDtypeStruct(private_keys.shape, bf16)
    stored = (swap(private_keys, 1), swap(private_values, 1))
    own, parent_tail, *olds = call(
        load_private_kernel,
        "load_private",
        (
            jax.ShapeDtypeStruct((beams, width), bf16),
            jax.ShapeDtypeStruct((beams, STATS), bf16),
            jax.ShapeDtypeStruct((8, STATS), jnp.int32),
            private,
            private,
        ),
        queries,
        parents,
        block_counts,
        private_keys,
        private_values,
        far=(0, 1, 2, 3, 4),
        scratch=[
            pltpu.SMEM((beams,), jnp.int32),
            pltpu.SMEM((beams,), jnp.int32),
            pltpu.SemaphoreType.DMA((3,)),
            pltpu.SemaphoreType.DMA((2, beams)),
        ],
        vmem=10,
        cost=2**26,
    )
    *came, parent_tail = lax.optimization_barrier((*came, parent_tail))
    asked = call(line_kernel, "line", line, parent_tail, *came, own)
    prompt_keys, prompt_values, _ = lax.optimization_barrier((prompt_keys, prompt_values, asked))
    prompts = call(
        load_prompt_kernel,
        "load_prompt",
        (prompt, prompt),
        prompt_keys,
        prompt_values,
        far=(0, 1),
        scratch=[pltpu.SemaphoreType.DMA((2, requests))],
        vmem=10,
        cost=2**26,
    )
    caches = (*prompts, *olds)
    limits, late_keys, late_values = lax.optimization_barrier(
        (swap(olds[0], 1), prompt_keys, prompt_values)
    )
    stored = (swap(late_keys, 1), swap(late_values, 1), limits, *stored)

    many = beams * QPK

    def attend(name, kinds, prompts, privates, asked, *caches):
        both = (half, half) if prompts else half
        return call(
            functools.partial(attend_kernel, kinds, prompts, privates),
            name,
            both,
            asked,
            *caches,
            scratch=[
                pltpu.VMEM((len(kinds), heads, requests * many, length), f32),
                pltpu.VMEM((len(kinds), heads, requests * many, length), bf16),
                pltpu.VMEM((len(kinds), heads, many, span), f32),
                pltpu.VMEM((len(kinds), heads, many, span), bf16),
            ],
            vmem=24,
            cost=2**26,
        )

    half = jax.ShapeDtypeStruct((requests // 2, beams, total), bf16)
    other = swap(asked, 2)
    here_a, here_b = attend("attend_own", (0,), True, True, asked, *caches)
    here_b = attend("own_private", (1,), False, True, asked, *stored, here_b)
    other, here_a, here_b = lax.optimization_barrier((other, here_a, here_b))
    send_a, send_b = attend("side_prompt", (0, 1), True, False, other, *caches, *stored)
    asked, send_a = lax.optimization_barrier((asked, send_a))
    there_a, there_b = attend("own_prompt", (1,), True, False, asked, *stored)
    send_b, there_a = lax.optimization_barrier((send_b, there_a))
    send_b = attend("side_private", (0, 1), False, True, other, *caches, *stored, send_b)
    piece = jax.ShapeDtypeStruct((beams, total), bf16)
    few = (piece,) * (requests // 2)
    came_a, came_b = swap(send_a, 2), swap(send_b, 2)
    parts = call(plane_kernel, "plane_merge", few, here_a, there_a, came_a)
    here_b, *parts = lax.optimization_barrier((here_b, *parts))
    parts = [*parts, *call(plane_kernel, "plane_merge", few, here_b, there_b, came_b)]
    parts = [swap(x, t * group) if t else x for t, x in zip(order, parts)]
    attended = call(
        finish_kernel,
        "finish",
        jax.ShapeDtypeStruct((beams, width), bf16),
        own,
        new_keys,
        new_values,
        *parts,
    )
    if sides == 2:
        line = [attended] + [swap(attended, t * group) for t in others[:1] + others[:0:-1]]
        halves = []
        for pieces in (line[: requests // 2], line[requests // 2 :]):
            near = jnp.stack(pieces)
            near = jnp.stack([near, swap(near, 2)])
            halves += [near, swap(near, 1)]
        shape = (requests * BEAM_WIDTH // 2, out_weight.shape[1])
        keep, send = call(
            project_kernel,
            "project",
            (jax.ShapeDtypeStruct(shape, f32), jax.ShapeDtypeStruct(shape, bf16)),
            *halves,
            out_weight,
            scratch=[pltpu.VMEM((requests, group, beams, width), bf16)],
            vmem=16,
        )
        came = lax.ppermute(send, "head", [(0, 1), (1, 0)])
        return (keep + came.astype(f32)).astype(bf16)
    rows = lax.all_gather(attended, "beam", axis=0, tiled=True)
    products = jnp.dot(rows, out_weight, preferred_element_type=f32)
    return lax.psum_scatter(products, "head", scatter_dimension=0, tiled=True).astype(bf16)


def solution(mesh):
    placed = (
        P("beam", "head"),
        P("beam", "head"),
        P("beam", "head"),
        P(None, "beam", "head"),
        P(None, "beam", "head"),
        P("beam", None, "head"),
        P("beam", None, "head"),
        P("beam"),
        P("beam"),
        P("head", "beam"),
    )
    return jax.shard_map(
        per_device, mesh=mesh, in_specs=placed, out_specs=P("head", "beam"), check_vma=False
    )
```

```python
import functools
import math

import jax
import jax.numpy as jnp
from jax import lax
from jax.experimental import pallas as pl
from jax.experimental.pallas import tpu as pltpu
from jax.sharding import PartitionSpec as P

HD = 128
QPK = 8
BEAM_WIDTH = 16
BLOCK_LEN = 128
STATS = 128
SCALE = 1.0 / math.sqrt(HD)
LOG2E = math.log2(math.e)

masked_score = -1e30
f32, bf16 = jnp.float32, jnp.bfloat16


def dot(a, b, ca, cb):
    return lax.dot_general(a, b, (((ca,), (cb,)), ((), ())), preferred_element_type=f32)


def soft(scores):
    top = jnp.max(scores, axis=1, keepdims=True)
    weights = jnp.exp2((scores - top) * (SCALE * LOG2E))
    return weights, top * SCALE, jnp.sum(weights, axis=1, keepdims=True)


def line_order(requests):
    return list(range(requests))[::-1]


def line_kernel(tail_ref, *refs):
    *pieces, out_ref = refs
    width = pieces[0].shape[1]
    pieces = pieces[:1] + pieces[-2:0:-1] + pieces[-1:]
    out_ref[:, :width] = jnp.concatenate([x[...] for x in pieces], axis=0)
    out_ref[:, width:] = jnp.concatenate([tail_ref[...]] * len(pieces), axis=0)


def load_private_kernel(
    q_hbm, par_hbm, cnt_hbm, ck_hbm, cv_hbm,
    q_ref, tail_ref, lim_ref, ck_ref, cv_ref, par_ref, cnt_ref, sems, old_sems,
):
    olds = ck_hbm.shape[0]
    copies = [
        pltpu.make_async_copy(src, dst, sems.at[n])
        for n, (src, dst) in enumerate(((q_hbm, q_ref), (par_hbm, par_ref), (cnt_hbm, cnt_ref)))
    ] + [
        pltpu.make_async_copy(src.at[o], dst.at[o], old_sems.at[n, o])
        for n, (src, dst) in enumerate(((ck_hbm, ck_ref), (cv_hbm, cv_ref)))
        for o in range(olds)
    ]
    for x in copies:
        x.start()
    for x in copies[:3]:
        x.wait()
    row = lax.broadcasted_iota(jnp.int32, tail_ref.shape, 0)
    parent = jnp.zeros(row.shape, jnp.int32)
    for b in range(tail_ref.shape[0]):
        parent = jnp.where(row == b, par_ref[b], parent)
    tail_ref[...] = parent.astype(f32).astype(bf16)
    lane = lax.broadcasted_iota(jnp.int32, lim_ref.shape, 1)
    limit = jnp.zeros(lim_ref.shape, jnp.int32)
    for o in range(olds):
        limit = jnp.where(lane == o, cnt_ref[o] * BLOCK_LEN, limit)
    lim_ref[...] = limit
    for x in copies[3:]:
        x.wait()


def load_prompt_kernel(pk_hbm, pv_hbm, pk_ref, pv_ref, sems):
    copies = [
        pltpu.make_async_copy(src.at[r], dst.at[r], sems.at[n, r])
        for n, (src, dst) in enumerate(((pk_hbm, pk_ref), (pv_hbm, pv_ref)))
        for r in range(pk_ref.shape[0])
    ]
    for x in copies:
        x.start()
    for x in copies:
        x.wait()


def attend_kernel(kinds, prompts, privates, q_ref, *refs):
    total = q_ref.shape[1]
    heads = (total - STATS) // (QPK * HD)
    caches = [refs[5 * n : 5 * n + 5] for n in range(len(kinds))]
    *outs, s_ref, p_ref, cs_ref, cp_ref = refs[5 * len(kinds) :]
    if not prompts:
        base_ref, *outs = outs
    requests, span = s_ref.shape[2] // cs_ref.shape[2], cs_ref.shape[3]
    pairs = requests // 2
    beams = q_ref.shape[0] // requests
    stride = heads * QPK
    rows = QPK * beams
    me = lax.axis_index("beam")
    mine = me // (BEAM_WIDTH // beams)
    order = line_order(requests)
    olds = beams

    def prompt(ref, k, u):
        both = [ref[mine ^ order[2 * u + m], :, k * HD : (k + 1) * HD] for m in range(2)]
        return jnp.concatenate(both, axis=1)

    def private(ref, k):
        return jnp.concatenate([ref[o, :, k * HD : (k + 1) * HD] for o in range(olds)], axis=1)

    whose = jnp.concatenate([q_ref[:, total - STATS :].astype(f32)[:beams]] * QPK, axis=0)
    parents, limits, locals_ = [], [], []
    for kind, (_, _, lim_ref, _, _) in zip(kinds, caches):
        parent = whose.astype(jnp.int32) - (me ^ kind) * olds
        column = parent[:, :1]
        limit = jnp.zeros((rows, 1), jnp.int32)
        for o in range(olds):
            known = lim_ref[0:1, o : o + 1]
            limit = jnp.where(column == o, known, limit)
        parents.append(parent)
        limits.append(limit)
        locals_.append((column >= 0) & (column < olds))
    stats = [jnp.zeros((beams, STATS), f32) for _ in range(requests)]
    lane = lax.broadcasted_iota(jnp.int32, (beams, STATS), 1) % stride
    blank = jnp.zeros((rows, HD), bf16)
    kept = {}

    def scores(n, k):
        pk_ref, _, _, ck_ref, _ = caches[n]
        tiles = [q_ref[:, (k * QPK + i) * HD : (k * QPK + i + 1) * HD] for i in range(QPK)]
        q = [
            jnp.concatenate([x[t * beams : (t + 1) * beams] for x in tiles], axis=0)
            for t in range(requests)
        ]
        for u in range(pairs if prompts else 0):
            both = jnp.concatenate(
                [
                    jnp.concatenate([q[2 * u], blank], axis=1),
                    jnp.concatenate([blank, q[2 * u + 1]], axis=1),
                ],
                axis=0,
            )
            s_ref[n, k, 2 * u * rows : 2 * (u + 1) * rows] = dot(both, prompt(pk_ref, k, u), 1, 1)
        if not privates:
            return
        chosen = jnp.concatenate(
            [jnp.where(parents[n] == o, q[-1], blank) for o in range(olds)], axis=1
        )
        cs_ref[n, k] = dot(chosen, private(ck_ref, k), 1, 1)

    def weigh(n, k):
        top = den = ctop = cden = None
        if prompts:
            p, top, den = soft(s_ref[n, k])
            p_ref[n, k] = p.astype(bf16)
        if not privates:
            kept[n, k] = (top, den, ctop, cden)
            return
        place = lax.broadcasted_iota(jnp.int32, (rows, span), 1)
        c, ctop, cden = soft(jnp.where(place < limits[n], cs_ref[n, k], masked_score))
        cp_ref[n, k] = c.astype(bf16)
        kept[n, k] = (top, den, ctop, cden)

    def values(n, k):
        _, pv_ref, _, _, cv_ref = caches[n]
        tops, dens, ctop, cden = kept.pop((n, k))
        found = []
        for u in range(pairs if prompts else 0):
            both = dot(
                p_ref[n, k, 2 * u * rows : 2 * (u + 1) * rows], prompt(pv_ref, k, u), 1, 0
            )
            for m, num in enumerate((both[:rows, :HD], both[rows:, HD:])):
                part = slice((2 * u + m) * rows, (2 * u + m + 1) * rows)
                found.append((num, tops[part], dens[part]))
        if not privates:
            return found
        every = dot(cp_ref[n, k], private(cv_ref, k), 1, 0)
        cnum = every[:, :HD]
        for o in range(1, olds):
            cnum = jnp.where(parents[n] == o, every[:, o * HD : (o + 1) * HD], cnum)
        if not prompts:
            cden = jnp.where(locals_[n], cden, 0.0)
            return [(jnp.where(locals_[n], cnum, 0.0), jnp.where(locals_[n], ctop, masked_score), cden)]
        num, top, den = found[-1]
        both = jnp.where(locals_[n], jnp.maximum(top, ctop), top)
        a = jnp.exp(top - both)
        e = jnp.where(locals_[n], jnp.exp(jnp.where(locals_[n], ctop, both) - both), 0.0)
        found[-1] = (a * num + e * cnum, both, a * den + e * cden)
        return found

    def finish(k):
        found = [values(n, k) for n in range(len(kinds))]
        done = []
        for t in range(requests):
            if not prompts and t < requests - 1:
                continue
            at = t if prompts else 0
            if prompts:
                num, top, den = found[0][t]
                others = found[1:]
            else:
                cols = [
                    slice((k * QPK + i) * HD, (k * QPK + i + 1) * HD) for i in range(QPK)
                ]
                num = jnp.concatenate([base_ref[pairs - 1, :, c] for c in cols], axis=0).astype(f32)
                top = jnp.concatenate(
                    [base_lse[:, k * QPK + i : k * QPK + i + 1] for i in range(QPK)], axis=0
                )
                den = jnp.ones_like(top)
                others = found
            for other in others:
                num2, top2, den2 = other[at]
                both = jnp.maximum(top, top2)
                a, e = jnp.exp(top - both), jnp.exp(top2 - both)
                num, top, den = a * num + e * num2, both, a * den + e * den2
            done.append(num * (1.0 / den))
            lse = top + jnp.log(den)
            for i in range(QPK):
                stats[t] = jnp.where(
                    lane == k * QPK + i,
                    jnp.broadcast_to(lse[i * beams : (i + 1) * beams], (beams, STATS)),
                    stats[t],
                )
        for i in range(QPK):
            cols = slice((k * QPK + i) * HD, (k * QPK + i + 1) * HD)
            if prompts:
                store(cols, [x[i * beams : (i + 1) * beams] for x in done])
            else:
                outs[0][pairs - 1, :, cols] = done[0][i * beams : (i + 1) * beams].astype(bf16)

    def store(cols, pieces):
        for n, piece in enumerate(pieces):
            outs[n // pairs][n % pairs, :, cols] = piece.astype(bf16)

    if not prompts:
        base_lse = read_stats(base_ref[pairs - 1, :, total - STATS :], stride)
        for n in range(pairs - 1):
            outs[0][n] = base_ref[n]
    for stage in (scores, weigh):
        for n in range(len(kinds)):
            for k in range(heads):
                stage(n, k)
    for k in range(heads):
        finish(k)
    if prompts:
        store(slice(total - STATS, total), [pack_stats(x, stride) for x in stats])
    else:
        outs[0][pairs - 1, :, total - STATS :] = pack_stats(stats[-1], stride)


def pack_stats(x, stride):
    hi = x.astype(bf16).astype(f32)
    mid = (x - hi).astype(bf16).astype(f32)
    which = lax.broadcasted_iota(jnp.int32, x.shape, 1) // stride
    return jnp.where(which == 0, hi, jnp.where(which == 1, mid, x - hi - mid)).astype(bf16)


def read_stats(x, stride):
    x = x.astype(f32)
    return x + pltpu.roll(x, STATS - stride, 1) + pltpu.roll(x, STATS - 2 * stride, 1)


def plane_kernel(*refs):
    count, beams, total = refs[0].shape
    parts, outs = refs[:-count], refs[-count:]
    parts = [jnp.concatenate([x[n] for n in range(count)], axis=0) for x in parts]
    heads = (total - STATS) // HD

    def store(cols, value):
        for n, out in enumerate(outs):
            out[:, cols] = value[n * beams : (n + 1) * beams]

    lses = [read_stats(x[:, total - STATS :], heads) for x in parts]
    top = functools.reduce(jnp.maximum, lses)
    ws = [jnp.exp(x - top) for x in lses]
    den = functools.reduce(jnp.add, ws)
    inv = 1.0 / den
    ws = [w * inv for w in ws]
    for h in range(heads):
        cols = slice(h * HD, (h + 1) * HD)
        acc = None
        for w, x in zip(ws, parts):
            one = w[:, h : h + 1] * x[:, cols].astype(f32)
            acc = one if acc is None else acc + one
        store(cols, acc.astype(bf16))
    lse = top + jnp.log(den)
    lane = lax.broadcasted_iota(jnp.int32, lse.shape, 1)
    again = jnp.where(
        lane < heads,
        lse,
        jnp.where(lane < 2 * heads, pltpu.roll(lse, heads, 1), pltpu.roll(lse, 2 * heads, 1)),
    )
    store(slice(total - STATS, total), pack_stats(again, heads))


def finish_kernel(q_ref, nk_ref, nv_ref, *refs):
    *parts, out_ref = refs
    beams, total = parts[0].shape
    heads = nv_ref.shape[1] // HD
    stride = heads * QPK
    lane = lax.broadcasted_iota(jnp.int32, (beams, STATS), 1)
    own = jnp.zeros((beams, STATS), f32)
    for h in range(stride):
        key = nk_ref[:, h // QPK * HD : (h // QPK + 1) * HD].astype(f32)
        s = jnp.sum(q_ref[:, h * HD : (h + 1) * HD].astype(f32) * key, axis=1, keepdims=True)
        own = jnp.where(lane == h, s * SCALE, own)
    lses = [read_stats(x[:, total - STATS :], stride) for x in parts]
    top = functools.reduce(jnp.maximum, lses, own)
    ws = [jnp.exp(x - top) for x in lses]
    w_own = jnp.exp(own - top)
    inv = 1.0 / functools.reduce(jnp.add, ws, w_own)
    ws = [w * inv for w in ws]
    w_own = w_own * inv
    for k in range(heads):
        value = nv_ref[:, k * HD : (k + 1) * HD].astype(f32)
        for i in range(QPK):
            h = k * QPK + i
            acc = w_own[:, h : h + 1] * value
            for w, x in zip(ws, parts):
                acc = acc + w[:, h : h + 1] * x[:, h * HD : (h + 1) * HD].astype(f32)
            out_ref[:, h * HD : (h + 1) * HD] = acc.astype(bf16)


def project_kernel(near_a, far_a, near_b, far_b, w_ref, keep_ref, send_ref, rows_ref):
    requests, group = rows_ref.shape[:2]
    me, side = lax.axis_index("beam"), lax.axis_index("head")
    mine, spot = me // group, me % group
    order = line_order(requests)
    order = order[-1:] + order[:1] + order[-2:0:-1]
    for first, refs in ((0, (near_a, far_a)), (requests // 2, (near_b, far_b))):
        for core, ref in enumerate(refs):
            for x in range(2):
                for n in range(requests // 2):
                    rows_ref[mine ^ order[first + n], spot ^ (2 * x + core)] = ref[x, n]
    a = jnp.concatenate(
        [rows_ref[z, j] for z in range(requests) for j in range(group)], axis=0
    )
    out = jnp.dot(a, w_ref[...], preferred_element_type=f32)
    half = requests * BEAM_WIDTH // 2

    @pl.when(side == 0)
    def _():
        keep_ref[...] = out[:half]
        send_ref[...] = out[half:].astype(bf16)

    @pl.when(side != 0)
    def _():
        keep_ref[...] = out[half:]
        send_ref[...] = out[:half].astype(bf16)


def whole_blocks(n, smem=(), far=()):
    places = [pltpu.SMEM if i in smem else pltpu.HBM if i in far else pltpu.VMEM for i in range(n)]
    return [pl.BlockSpec(memory_space=place) for place in places]


def call(kernel, name, out_shape, *args, smem=(), far=(), scratch=(), vmem=8, cost=None):
    many = isinstance(out_shape, tuple)
    return pl.pallas_call(
        kernel,
        out_shape=out_shape,
        in_specs=whole_blocks(len(args), smem, far),
        out_specs=tuple(whole_blocks(len(out_shape))) if many else whole_blocks(1)[0],
        scratch_shapes=list(scratch),
        compiler_params=pltpu.CompilerParams(vmem_limit_bytes=vmem * 1024 * 1024),
        cost_estimate=cost and pl.CostEstimate(flops=cost, bytes_accessed=cost, transcendentals=0),
        name=name,
    )(*(pltpu.with_memory_space_constraint(x, pltpu.HBM) if i in far else x for i, x in enumerate(args)))


def per_device(
    queries,
    new_keys,
    new_values,
    prompt_keys,
    prompt_values,
    private_keys,
    private_values,
    parents,
    block_counts,
    out_weight,
):
    beams, width = queries.shape
    group = BEAM_WIDTH // beams
    assert group == 4
    devices = lax.axis_size("beam")
    requests = prompt_keys.shape[0]
    sides = lax.axis_size("head")
    total = width + STATS

    def swap(x, with_bit):
        return lax.ppermute(x, "beam", [(i, i ^ with_bit) for i in range(devices)])

    rows = requests * beams
    heads = width // (QPK * HD)
    length, span = prompt_keys.shape[1], private_keys.shape[1]
    line = jax.ShapeDtypeStruct((rows, total), bf16)
    order = line_order(requests)
    others = order[:-1]
    came = [swap(queries, t * group) for t in others[:1] + others[:0:-1]]
    prompt = jax.ShapeDtypeStruct(prompt_keys.shape, bf16)
    private = jax.ShapeDtypeStruct(private_keys.shape, bf16)
    stored = (swap(private_keys, 1), swap(private_values, 1))
    own, parent_tail, *olds = call(
        load_private_kernel,
        "load_private",
        (
            jax.ShapeDtypeStruct((beams, width), bf16),
            jax.ShapeDtypeStruct((beams, STATS), bf16),
            jax.ShapeDtypeStruct((8, STATS), jnp.int32),
            private,
            private,
        ),
        queries,
        parents,
        block_counts,
        private_keys,
        private_values,
        far=(0, 1, 2, 3, 4),
        scratch=[
            pltpu.SMEM((beams,), jnp.int32),
            pltpu.SMEM((beams,), jnp.int32),
            pltpu.SemaphoreType.DMA((3,)),
            pltpu.SemaphoreType.DMA((2, beams)),
        ],
        vmem=10,
        cost=2**26,
    )
    *came, parent_tail = lax.optimization_barrier((*came, parent_tail))
    asked = call(line_kernel, "line", line, parent_tail, *came, own)
    prompt_keys, prompt_values, _ = lax.optimization_barrier((prompt_keys, prompt_values, asked))
    prompts = call(
        load_prompt_kernel,
        "load_prompt",
        (prompt, prompt),
        prompt_keys,
        prompt_values,
        far=(0, 1),
        scratch=[pltpu.SemaphoreType.DMA((2, requests))],
        vmem=10,
        cost=2**26,
    )
    caches = (*prompts, *olds)
    limits, late_keys, late_values = lax.optimization_barrier(
        (swap(olds[0], 1), prompt_keys, prompt_values)
    )
    stored = (swap(late_keys, 1), swap(late_values, 1), limits, *stored)

    many = beams * QPK

    def attend(name, kinds, prompts, privates, asked, *caches):
        both = (half, half) if prompts else half
        return call(
            functools.partial(attend_kernel, kinds, prompts, privates),
            name,
            both,
            asked,
            *caches,
            scratch=[
                pltpu.VMEM((len(kinds), heads, requests * many, length), f32),
                pltpu.VMEM((len(kinds), heads, requests * many, length), bf16),
                pltpu.VMEM((len(kinds), heads, many, span), f32),
                pltpu.VMEM((len(kinds), heads, many, span), bf16),
            ],
            vmem=24,
            cost=2**26,
        )

    half = jax.ShapeDtypeStruct((requests // 2, beams, total), bf16)
    other = swap(asked, 2)
    here_a, here_b = attend("attend_own", (0,), True, True, asked, *caches)
    there_a, there_b = attend("own_prompt", (1,), True, False, asked, *stored)
    other, here_a, there_a = lax.optimization_barrier((other, here_a, there_a))
    send_a, send_b = attend("side_prompt", (0, 1), True, False, other, *caches, *stored)
    send_b = attend("side_private", (0, 1), False, True, other, *caches, *stored, send_b)
    piece = jax.ShapeDtypeStruct((beams, total), bf16)
    few = (piece,) * (requests // 2)
    came_a, came_b = swap(send_a, 2), swap(send_b, 2)
    parts = call(plane_kernel, "plane_merge", few, here_a, there_a, came_a)
    there_b, *parts = lax.optimization_barrier((there_b, *parts))
    there_b = attend("own_private", (1,), False, True, asked, *stored, there_b)
    parts = [*parts, *call(plane_kernel, "plane_merge", few, here_b, there_b, came_b)]
    parts = [swap(x, t * group) if t else x for t, x in zip(order, parts)]
    attended = call(
        finish_kernel,
        "finish",
        jax.ShapeDtypeStruct((beams, width), bf16),
        own,
        new_keys,
        new_values,
        *parts,
    )
    if sides == 2:
        line = [attended] + [swap(attended, t * group) for t in others[:1] + others[:0:-1]]
        halves = []
        for pieces in (line[: requests // 2], line[requests // 2 :]):
            near = jnp.stack(pieces)
            near = jnp.stack([near, swap(near, 2)])
            halves += [near, swap(near, 1)]
        shape = (requests * BEAM_WIDTH // 2, out_weight.shape[1])
        keep, send = call(
            project_kernel,
            "project",
            (jax.ShapeDtypeStruct(shape, f32), jax.ShapeDtypeStruct(shape, bf16)),
            *halves,
            out_weight,
            scratch=[pltpu.VMEM((requests, group, beams, width), bf16)],
            vmem=16,
        )
        came = lax.ppermute(send, "head", [(0, 1), (1, 0)])
        return (keep + came.astype(f32)).astype(bf16)
    rows = lax.all_gather(attended, "beam", axis=0, tiled=True)
    products = jnp.dot(rows, out_weight, preferred_element_type=f32)
    return lax.psum_scatter(products, "head", scatter_dimension=0, tiled=True).astype(bf16)


def solution(mesh):
    placed = (
        P("beam", "head"),
        P("beam", "head"),
        P("beam", "head"),
        P(None, "beam", "head"),
        P(None, "beam", "head"),
        P("beam", None, "head"),
        P("beam", None, "head"),
        P("beam"),
        P("beam"),
        P("head", "beam"),
    )
    return jax.shard_map(
        per_device, mesh=mesh, in_specs=placed, out_specs=P("head", "beam"), check_vma=False
    )
```

```python
import functools
import math

import jax
import jax.numpy as jnp
from jax import lax
from jax.experimental import pallas as pl
from jax.experimental.pallas import tpu as pltpu
from jax.sharding import PartitionSpec as P

HD = 128
QPK = 8
BEAM_WIDTH = 16
BLOCK_LEN = 128
STATS = 128
SCALE = 1.0 / math.sqrt(HD)
LOG2E = math.log2(math.e)

masked_score = -1e30
f32, bf16 = jnp.float32, jnp.bfloat16


def dot(a, b, ca, cb):
    return lax.dot_general(a, b, (((ca,), (cb,)), ((), ())), preferred_element_type=f32)


def soft(scores):
    top = jnp.max(scores, axis=1, keepdims=True)
    weights = jnp.exp2((scores - top) * (SCALE * LOG2E))
    return weights, top * SCALE, jnp.sum(weights, axis=1, keepdims=True)


def line_order(requests):
    return list(range(requests))[::-1]


def line_kernel(tail_ref, *refs):
    *pieces, out_ref = refs
    width = pieces[0].shape[1]
    pieces = pieces[:1] + pieces[-2:0:-1] + pieces[-1:]
    out_ref[:, :width] = jnp.concatenate([x[...] for x in pieces], axis=0)
    out_ref[:, width:] = jnp.concatenate([tail_ref[...]] * len(pieces), axis=0)


def load_private_kernel(
    q_hbm, par_hbm, cnt_hbm, ck_hbm, cv_hbm,
    q_ref, tail_ref, lim_ref, ck_ref, cv_ref, par_ref, cnt_ref, sems, old_sems,
):
    olds = ck_hbm.shape[0]
    copies = [
        pltpu.make_async_copy(src, dst, sems.at[n])
        for n, (src, dst) in enumerate(((q_hbm, q_ref), (par_hbm, par_ref), (cnt_hbm, cnt_ref)))
    ] + [
        pltpu.make_async_copy(src.at[o], dst.at[o], old_sems.at[n, o])
        for n, (src, dst) in enumerate(((ck_hbm, ck_ref), (cv_hbm, cv_ref)))
        for o in range(olds)
    ]
    for x in copies:
        x.start()
    for x in copies[:3]:
        x.wait()
    row = lax.broadcasted_iota(jnp.int32, tail_ref.shape, 0)
    parent = jnp.zeros(row.shape, jnp.int32)
    for b in range(tail_ref.shape[0]):
        parent = jnp.where(row == b, par_ref[b], parent)
    tail_ref[...] = parent.astype(f32).astype(bf16)
    lane = lax.broadcasted_iota(jnp.int32, lim_ref.shape, 1)
    limit = jnp.zeros(lim_ref.shape, jnp.int32)
    for o in range(olds):
        limit = jnp.where(lane == o, cnt_ref[o] * BLOCK_LEN, limit)
    lim_ref[...] = limit
    for x in copies[3:]:
        x.wait()


def load_prompt_kernel(pk_hbm, pv_hbm, pk_ref, pv_ref, sems):
    copies = [
        pltpu.make_async_copy(src.at[r], dst.at[r], sems.at[n, r])
        for n, (src, dst) in enumerate(((pk_hbm, pk_ref), (pv_hbm, pv_ref)))
        for r in range(pk_ref.shape[0])
    ]
    for x in copies:
        x.start()
    for x in copies:
        x.wait()


def attend_kernel(kinds, prompts, privates, q_ref, *refs):
    total = q_ref.shape[1]
    heads = (total - STATS) // (QPK * HD)
    caches = [refs[5 * n : 5 * n + 5] for n in range(len(kinds))]
    *outs, s_ref, p_ref, cs_ref, cp_ref = refs[5 * len(kinds) :]
    if not prompts:
        base_ref, *outs = outs
    requests, span = s_ref.shape[2] // cs_ref.shape[2], cs_ref.shape[3]
    pairs = requests // 2
    beams = q_ref.shape[0] // requests
    stride = heads * QPK
    rows = QPK * beams
    me = lax.axis_index("beam")
    mine = me // (BEAM_WIDTH // beams)
    order = line_order(requests)
    olds = beams

    def prompt(ref, k, u):
        both = [ref[mine ^ order[2 * u + m], :, k * HD : (k + 1) * HD] for m in range(2)]
        return jnp.concatenate(both, axis=1)

    def private(ref, k):
        return jnp.concatenate([ref[o, :, k * HD : (k + 1) * HD] for o in range(olds)], axis=1)

    whose = jnp.concatenate([q_ref[:, total - STATS :].astype(f32)[:beams]] * QPK, axis=0)
    parents, limits, locals_ = [], [], []
    for kind, (_, _, lim_ref, _, _) in zip(kinds, caches):
        parent = whose.astype(jnp.int32) - (me ^ kind) * olds
        column = parent[:, :1]
        limit = jnp.zeros((rows, 1), jnp.int32)
        for o in range(olds):
            known = lim_ref[0:1, o : o + 1]
            limit = jnp.where(column == o, known, limit)
        parents.append(parent)
        limits.append(limit)
        locals_.append((column >= 0) & (column < olds))
    stats = [jnp.zeros((beams, STATS), f32) for _ in range(requests)]
    lane = lax.broadcasted_iota(jnp.int32, (beams, STATS), 1) % stride
    blank = jnp.zeros((rows, HD), bf16)
    kept = {}

    def scores(n, k):
        pk_ref, _, _, ck_ref, _ = caches[n]
        tiles = [q_ref[:, (k * QPK + i) * HD : (k * QPK + i + 1) * HD] for i in range(QPK)]
        q = [
            jnp.concatenate([x[t * beams : (t + 1) * beams] for x in tiles], axis=0)
            for t in range(requests)
        ]
        for u in range(pairs if prompts else 0):
            both = jnp.concatenate(
                [
                    jnp.concatenate([q[2 * u], blank], axis=1),
                    jnp.concatenate([blank, q[2 * u + 1]], axis=1),
                ],
                axis=0,
            )
            s_ref[n, k, 2 * u * rows : 2 * (u + 1) * rows] = dot(both, prompt(pk_ref, k, u), 1, 1)
        if not privates:
            return
        chosen = jnp.concatenate(
            [jnp.where(parents[n] == o, q[-1], blank) for o in range(olds)], axis=1
        )
        cs_ref[n, k] = dot(chosen, private(ck_ref, k), 1, 1)

    def weigh(n, k):
        top = den = ctop = cden = None
        if prompts:
            p, top, den = soft(s_ref[n, k])
            p_ref[n, k] = p.astype(bf16)
        if not privates:
            kept[n, k] = (top, den, ctop, cden)
            return
        place = lax.broadcasted_iota(jnp.int32, (rows, span), 1)
        c, ctop, cden = soft(jnp.where(place < limits[n], cs_ref[n, k], masked_score))
        cp_ref[n, k] = c.astype(bf16)
        kept[n, k] = (top, den, ctop, cden)

    def values(n, k):
        _, pv_ref, _, _, cv_ref = caches[n]
        tops, dens, ctop, cden = kept.pop((n, k))
        found = []
        for u in range(pairs if prompts else 0):
            both = dot(
                p_ref[n, k, 2 * u * rows : 2 * (u + 1) * rows], prompt(pv_ref, k, u), 1, 0
            )
            for m, num in enumerate((both[:rows, :HD], both[rows:, HD:])):
                part = slice((2 * u + m) * rows, (2 * u + m + 1) * rows)
                found.append((num, tops[part], dens[part]))
        if not privates:
            return found
        every = dot(cp_ref[n, k], private(cv_ref, k), 1, 0)
        cnum = every[:, :HD]
        for o in range(1, olds):
            cnum = jnp.where(parents[n] == o, every[:, o * HD : (o + 1) * HD], cnum)
        if not prompts:
            cden = jnp.where(locals_[n], cden, 0.0)
            return [(jnp.where(locals_[n], cnum, 0.0), jnp.where(locals_[n], ctop, masked_score), cden)]
        num, top, den = found[-1]
        both = jnp.where(locals_[n], jnp.maximum(top, ctop), top)
        a = jnp.exp(top - both)
        e = jnp.where(locals_[n], jnp.exp(jnp.where(locals_[n], ctop, both) - both), 0.0)
        found[-1] = (a * num + e * cnum, both, a * den + e * cden)
        return found

    def finish(k):
        found = [values(n, k) for n in range(len(kinds))]
        done = []
        for t in range(requests):
            if not prompts and t < requests - 1:
                continue
            at = t if prompts else 0
            if prompts:
                num, top, den = found[0][t]
                others = found[1:]
            else:
                cols = [
                    slice((k * QPK + i) * HD, (k * QPK + i + 1) * HD) for i in range(QPK)
                ]
                num = jnp.concatenate([base_ref[pairs - 1, :, c] for c in cols], axis=0).astype(f32)
                top = jnp.concatenate(
                    [base_lse[:, k * QPK + i : k * QPK + i + 1] for i in range(QPK)], axis=0
                )
                den = jnp.ones_like(top)
                others = found
            for other in others:
                num2, top2, den2 = other[at]
                both = jnp.maximum(top, top2)
                a, e = jnp.exp(top - both), jnp.exp(top2 - both)
                num, top, den = a * num + e * num2, both, a * den + e * den2
            done.append(num * (1.0 / den))
            lse = top + jnp.log(den)
            for i in range(QPK):
                stats[t] = jnp.where(
                    lane == k * QPK + i,
                    jnp.broadcast_to(lse[i * beams : (i + 1) * beams], (beams, STATS)),
                    stats[t],
                )
        for i in range(QPK):
            cols = slice((k * QPK + i) * HD, (k * QPK + i + 1) * HD)
            if prompts:
                store(cols, [x[i * beams : (i + 1) * beams] for x in done])
            else:
                outs[0][pairs - 1, :, cols] = done[0][i * beams : (i + 1) * beams].astype(bf16)

    def store(cols, pieces):
        for n, piece in enumerate(pieces):
            outs[n // pairs][n % pairs, :, cols] = piece.astype(bf16)

    if not prompts:
        base_lse = read_stats(base_ref[pairs - 1, :, total - STATS :], stride)
        for n in range(pairs - 1):
            outs[0][n] = base_ref[n]
    for stage in (scores, weigh):
        for n in range(len(kinds)):
            for k in range(heads):
                stage(n, k)
    for k in range(heads):
        finish(k)
    if prompts:
        store(slice(total - STATS, total), [pack_stats(x, stride) for x in stats])
    else:
        outs[0][pairs - 1, :, total - STATS :] = pack_stats(stats[-1], stride)


def pack_stats(x, stride):
    hi = x.astype(bf16).astype(f32)
    mid = (x - hi).astype(bf16).astype(f32)
    which = lax.broadcasted_iota(jnp.int32, x.shape, 1) // stride
    return jnp.where(which == 0, hi, jnp.where(which == 1, mid, x - hi - mid)).astype(bf16)


def read_stats(x, stride):
    x = x.astype(f32)
    return x + pltpu.roll(x, STATS - stride, 1) + pltpu.roll(x, STATS - 2 * stride, 1)


def plane_kernel(first, last, *refs):
    _, beams, total = refs[0].shape
    count = last - first
    parts, outs = refs[:-count], refs[-count:]
    parts = [jnp.concatenate([x[n] for n in range(first, last)], axis=0) for x in parts]
    heads = (total - STATS) // HD

    def store(cols, value):
        for n, out in enumerate(outs):
            out[:, cols] = value[n * beams : (n + 1) * beams]

    lses = [read_stats(x[:, total - STATS :], heads) for x in parts]
    top = functools.reduce(jnp.maximum, lses)
    ws = [jnp.exp(x - top) for x in lses]
    den = functools.reduce(jnp.add, ws)
    inv = 1.0 / den
    ws = [w * inv for w in ws]
    for h in range(heads):
        cols = slice(h * HD, (h + 1) * HD)
        acc = None
        for w, x in zip(ws, parts):
            one = w[:, h : h + 1] * x[:, cols].astype(f32)
            acc = one if acc is None else acc + one
        store(cols, acc.astype(bf16))
    lse = top + jnp.log(den)
    lane = lax.broadcasted_iota(jnp.int32, lse.shape, 1)
    again = jnp.where(
        lane < heads,
        lse,
        jnp.where(lane < 2 * heads, pltpu.roll(lse, heads, 1), pltpu.roll(lse, 2 * heads, 1)),
    )
    store(slice(total - STATS, total), pack_stats(again, heads))


def finish_kernel(q_ref, nk_ref, nv_ref, *refs):
    *parts, out_ref = refs
    beams, total = parts[0].shape
    heads = nv_ref.shape[1] // HD
    stride = heads * QPK
    lane = lax.broadcasted_iota(jnp.int32, (beams, STATS), 1)
    own = jnp.zeros((beams, STATS), f32)
    for h in range(stride):
        key = nk_ref[:, h // QPK * HD : (h // QPK + 1) * HD].astype(f32)
        s = jnp.sum(q_ref[:, h * HD : (h + 1) * HD].astype(f32) * key, axis=1, keepdims=True)
        own = jnp.where(lane == h, s * SCALE, own)
    lses = [read_stats(x[:, total - STATS :], stride) for x in parts]
    top = functools.reduce(jnp.maximum, lses, own)
    ws = [jnp.exp(x - top) for x in lses]
    w_own = jnp.exp(own - top)
    inv = 1.0 / functools.reduce(jnp.add, ws, w_own)
    ws = [w * inv for w in ws]
    w_own = w_own * inv
    for k in range(heads):
        value = nv_ref[:, k * HD : (k + 1) * HD].astype(f32)
        for i in range(QPK):
            h = k * QPK + i
            acc = w_own[:, h : h + 1] * value
            for w, x in zip(ws, parts):
                acc = acc + w[:, h : h + 1] * x[:, h * HD : (h + 1) * HD].astype(f32)
            out_ref[:, h * HD : (h + 1) * HD] = acc.astype(bf16)


def project_kernel(near_a, far_a, near_b, far_b, w_ref, keep_ref, send_ref, rows_ref):
    requests, group = rows_ref.shape[:2]
    me, side = lax.axis_index("beam"), lax.axis_index("head")
    mine, spot = me // group, me % group
    order = line_order(requests)
    order = order[-1:] + order[:1] + order[-2:0:-1]
    for first, refs in ((0, (near_a, far_a)), (requests // 2, (near_b, far_b))):
        for core, ref in enumerate(refs):
            for x in range(2):
                for n in range(requests // 2):
                    rows_ref[mine ^ order[first + n], spot ^ (2 * x + core)] = ref[x, n]
    a = jnp.concatenate(
        [rows_ref[z, j] for z in range(requests) for j in range(group)], axis=0
    )
    out = jnp.dot(a, w_ref[...], preferred_element_type=f32)
    half = requests * BEAM_WIDTH // 2

    @pl.when(side == 0)
    def _():
        keep_ref[...] = out[:half]
        send_ref[...] = out[half:].astype(bf16)

    @pl.when(side != 0)
    def _():
        keep_ref[...] = out[half:]
        send_ref[...] = out[:half].astype(bf16)


def whole_blocks(n, smem=(), far=()):
    places = [pltpu.SMEM if i in smem else pltpu.HBM if i in far else pltpu.VMEM for i in range(n)]
    return [pl.BlockSpec(memory_space=place) for place in places]


def call(kernel, name, out_shape, *args, smem=(), far=(), scratch=(), vmem=8, cost=None):
    many = isinstance(out_shape, tuple)
    return pl.pallas_call(
        kernel,
        out_shape=out_shape,
        in_specs=whole_blocks(len(args), smem, far),
        out_specs=tuple(whole_blocks(len(out_shape))) if many else whole_blocks(1)[0],
        scratch_shapes=list(scratch),
        compiler_params=pltpu.CompilerParams(vmem_limit_bytes=vmem * 1024 * 1024),
        cost_estimate=cost and pl.CostEstimate(flops=cost, bytes_accessed=cost, transcendentals=0),
        name=name,
    )(*(pltpu.with_memory_space_constraint(x, pltpu.HBM) if i in far else x for i, x in enumerate(args)))


def per_device(
    queries,
    new_keys,
    new_values,
    prompt_keys,
    prompt_values,
    private_keys,
    private_values,
    parents,
    block_counts,
    out_weight,
):
    beams, width = queries.shape
    group = BEAM_WIDTH // beams
    assert group == 4
    devices = lax.axis_size("beam")
    requests = prompt_keys.shape[0]
    sides = lax.axis_size("head")
    total = width + STATS

    def swap(x, with_bit):
        return lax.ppermute(x, "beam", [(i, i ^ with_bit) for i in range(devices)])

    rows = requests * beams
    heads = width // (QPK * HD)
    length, span = prompt_keys.shape[1], private_keys.shape[1]
    line = jax.ShapeDtypeStruct((rows, total), bf16)
    order = line_order(requests)
    others = order[:-1]
    came = [swap(queries, t * group) for t in others[:1] + others[:0:-1]]
    prompt = jax.ShapeDtypeStruct(prompt_keys.shape, bf16)
    private = jax.ShapeDtypeStruct(private_keys.shape, bf16)
    stored = (swap(private_keys, 1), swap(private_values, 1))
    own, parent_tail, *olds = call(
        load_private_kernel,
        "load_private",
        (
            jax.ShapeDtypeStruct((beams, width), bf16),
            jax.ShapeDtypeStruct((beams, STATS), bf16),
            jax.ShapeDtypeStruct((8, STATS), jnp.int32),
            private,
            private,
        ),
        queries,
        parents,
        block_counts,
        private_keys,
        private_values,
        far=(0, 1, 2, 3, 4),
        scratch=[
            pltpu.SMEM((beams,), jnp.int32),
            pltpu.SMEM((beams,), jnp.int32),
            pltpu.SemaphoreType.DMA((3,)),
            pltpu.SemaphoreType.DMA((2, beams)),
        ],
        vmem=10,
        cost=2**26,
    )
    *came, parent_tail = lax.optimization_barrier((*came, parent_tail))
    asked = call(line_kernel, "line", line, parent_tail, *came, own)
    prompt_keys, prompt_values, _ = lax.optimization_barrier((prompt_keys, prompt_values, asked))
    prompts = call(
        load_prompt_kernel,
        "load_prompt",
        (prompt, prompt),
        prompt_keys,
        prompt_values,
        far=(0, 1),
        scratch=[pltpu.SemaphoreType.DMA((2, requests))],
        vmem=10,
        cost=2**26,
    )
    caches = (*prompts, *olds)
    limits, late_keys, late_values = lax.optimization_barrier(
        (swap(olds[0], 1), prompt_keys, prompt_values)
    )
    stored = (swap(late_keys, 1), swap(late_values, 1), limits, *stored)

    many = beams * QPK

    def attend(name, kinds, prompts, privates, asked, *caches):
        both = (half, half) if prompts else half
        return call(
            functools.partial(attend_kernel, kinds, prompts, privates),
            name,
            both,
            asked,
            *caches,
            scratch=[
                pltpu.VMEM((len(kinds), heads, requests * many, length), f32),
                pltpu.VMEM((len(kinds), heads, requests * many, length), bf16),
                pltpu.VMEM((len(kinds), heads, many, span), f32),
                pltpu.VMEM((len(kinds), heads, many, span), bf16),
            ],
            vmem=24,
            cost=2**26,
        )

    half = jax.ShapeDtypeStruct((requests // 2, beams, total), bf16)
    other = swap(asked, 2)
    here_a, here_b = attend("attend_own", (0,), True, True, asked, *caches)
    there_a, there_b = attend("own_prompt", (1,), True, False, asked, *stored)
    other, here_a, there_a = lax.optimization_barrier((other, here_a, there_a))
    send_a, send_b = attend("side_prompt", (0, 1), True, False, other, *caches, *stored)
    send_b = attend("side_private", (0, 1), False, True, other, *caches, *stored, send_b)
    piece = jax.ShapeDtypeStruct((beams, total), bf16)
    half_count = requests // 2

    def plane_merge(first, last, *partials):
        kernel = functools.partial(plane_kernel, first, last)
        return call(kernel, "plane_merge", (piece,) * (last - first), *partials)

    came_a, came_b = swap(send_a, 2), swap(send_b, 2)
    far_parts = plane_merge(0, half_count, here_a, there_a, came_a)
    here_b, *far_parts = lax.optimization_barrier((here_b, *far_parts))
    near_parts = plane_merge(0, half_count - 1, here_b, there_b, came_b)
    there_b, *near_parts = lax.optimization_barrier((there_b, *near_parts))
    there_b = attend("own_private", (1,), False, True, asked, *stored, there_b)
    own_parts = plane_merge(half_count - 1, half_count, here_b, there_b, came_b)
    parts = [*far_parts, *near_parts, *own_parts]
    parts = [swap(x, t * group) if t else x for t, x in zip(order, parts)]
    attended = call(
        finish_kernel,
        "finish",
        jax.ShapeDtypeStruct((beams, width), bf16),
        own,
        new_keys,
        new_values,
        *parts,
    )
    if sides == 2:
        line = [attended] + [swap(attended, t * group) for t in others[:1] + others[:0:-1]]
        halves = []
        for pieces in (line[: requests // 2], line[requests // 2 :]):
            near = jnp.stack(pieces)
            near = jnp.stack([near, swap(near, 2)])
            halves += [near, swap(near, 1)]
        shape = (requests * BEAM_WIDTH // 2, out_weight.shape[1])
        keep, send = call(
            project_kernel,
            "project",
            (jax.ShapeDtypeStruct(shape, f32), jax.ShapeDtypeStruct(shape, bf16)),
            *halves,
            out_weight,
            scratch=[pltpu.VMEM((requests, group, beams, width), bf16)],
            vmem=16,
        )
        came = lax.ppermute(send, "head", [(0, 1), (1, 0)])
        return (keep + came.astype(f32)).astype(bf16)
    rows = lax.all_gather(attended, "beam", axis=0, tiled=True)
    products = jnp.dot(rows, out_weight, preferred_element_type=f32)
    return lax.psum_scatter(products, "head", scatter_dimension=0, tiled=True).astype(bf16)


def solution(mesh):
    placed = (
        P("beam", "head"),
        P("beam", "head"),
        P("beam", "head"),
        P(None, "beam", "head"),
        P(None, "beam", "head"),
        P("beam", None, "head"),
        P("beam", None, "head"),
        P("beam"),
        P("beam"),
        P("head", "beam"),
    )
    return jax.shard_map(
        per_device, mesh=mesh, in_specs=placed, out_specs=P("head", "beam"), check_vma=False
    )
```
